128 devices in a mesh: dp: 8 (over y, z_hi), fsdp: 16 (over z_lo, x, core).
Axes of the slice: x: 4, y: 4, z: 4 (z_hi: 2, z_lo: 2; z = z_hi * 2 + z_lo), core: 2. Of those that a mesh axis runs over, the one named last changes fastest.
Arguments:
- cap_hidden: bfloat16 [4096, 4096], P('dp'), may hold values from -6 to 6
- t5_norm_gain: bfloat16 [4096], replicated, may hold values from 0.5 to 1.5
- t5_wi0: bfloat16 [4096, 6144], P(None, 'fsdp'), may hold values from -0.09375 to 0.09375
- t5_wi1: bfloat16 [4096, 6144], P(None, 'fsdp'), may hold values from -0.09375 to 0.09375
- t5_wo: bfloat16 [6144, 4096], P('fsdp'), may hold values from -0.15625 to 0.15625
- t5_final_gain: bfloat16 [4096], replicated, may hold values from 0.5 to 1.5
- cap_lengths: int32 [16], P('dp'), may hold values from 1 to 256, 3072 in all
- latents: bfloat16 [16384, 4096], P(('dp', 'fsdp')), may hold values from -6 to 6
- w_query: bfloat16 [4096, 2048], P('fsdp'), may hold values from -0.109375 to 0.109375
- w_key: bfloat16 [4096, 2048], P(None, 'fsdp'), may hold values from -0.109375 to 0.109375
- w_value: bfloat16 [4096, 2048], P(None, 'fsdp'), may hold values from -0.09375 to 0.09375
- caption_of_image: int32 [16], P('dp'), may hold values from 0 to 1
- grad_out: bfloat16 [16384, 2048], P(('dp', 'fsdp')), may hold values from -6 to 6
Outputs:
- attn_out: float32 [16384, 2048], P(('dp', 'fsdp'))
- latent_token_gradient: float32 [16384, 4096], P(('dp', 'fsdp'))
- grad_query: float32 [4096, 2048], P('fsdp')
- grad_key: float32 [4096, 2048], P(None, 'fsdp')
- grad_value: float32 [4096, 2048], P(None, 'fsdp')
The draws below stay inside these ranges and needn't reach their ends.
Inputs may be any that keep to these rules, and one draw needn't show every extreme that they name: `cap_lengths`: a caption's keys at positions at or past its length are masked; some caption has all 256 positions live. `caption_of_image`: an index among the 2 captions of the image's own dp index.
All inputs are finite; a program needn't handle non-finite values. No bound on the sum of `cap_lengths` on one device may be relied on, other than what follows from the above.
Results may differ from the reference program's by a relative error of at most 0.03.
Values may be sent and summed in bfloat16 or wider, within the bound.
A program may use at most 192 MiB of HBM per device.

```python
import math
import jax
import jax.numpy as jnp
import numpy as np
from jax import lax

D = 4096
DT = 4096
FFT = 6144
HD = 128
LCAP = 256
IMG_TOK = 1024
CAPS = 2
TOK_DEV = 128
QW = 2048
CAPTIONS = 16
TOKENS = 16384
IMAGES = 16
N_DP = 8
N_FSDP = 16


def shared_signs(key, salt, count):
    flips = jax.random.randint(jax.random.fold_in(key, salt), (count,), 0, 2)
    return (2 * flips - 1).astype(jnp.float32)


def draw_latents(key, part):
    pattern = shared_signs(key, 101, D)
    key = jax.random.fold_in(key, 1)
    pick_key, level_key, noise_key = jax.random.split(key, 3)
    planted = jax.random.randint(pick_key, (TOKENS, 1), 0, 32) == 0
    noise = jnp.clip(jax.random.normal(noise_key, (TOKENS, D), jnp.float32), -6.0, 6.0)
    level = jax.random.uniform(level_key, (TOKENS, 1), jnp.float32, 0.75, 4.0)
    values = jnp.where(planted, level * pattern[None, :] + noise, noise)
    return jnp.clip(values, -6.0, 6.0).astype(jnp.bfloat16)


def draw_cap_hidden(key, part):
    pattern = shared_signs(key, 103, DT)
    key = jax.random.fold_in(key, 2)
    pick_key, level_key, noise_key = jax.random.split(key, 3)
    rows = CAPTIONS * LCAP
    planted = jax.random.randint(pick_key, (rows, 1), 0, 32) == 0
    noise = jnp.clip(jax.random.normal(noise_key, (rows, DT), jnp.float32), -6.0, 6.0)
    level = jax.random.uniform(level_key, (rows, 1), jnp.float32, 1.5, 4.0)
    values = jnp.where(planted, level * pattern[None, :] + noise, noise)
    return jnp.clip(values, -6.0, 6.0).astype(jnp.bfloat16)


def draw_w_query(key, part):
    pattern = shared_signs(key, 101, D)
    tangent_vector = shared_signs(key, 102, QW)
    key = jax.random.fold_in(key, 3)
    noise = jnp.clip(jax.random.normal(key, (D, QW), jnp.float32), -6.0, 6.0) * D ** (-0.5)
    values = noise + 5.0 / D * pattern[:, None] * tangent_vector[None, :]
    return values.astype(jnp.bfloat16)


def draw_w_key(key, part):
    pattern = shared_signs(key, 103, DT)
    tangent_vector = shared_signs(key, 102, QW)
    key = jax.random.fold_in(key, 4)
    noise = jnp.clip(jax.random.normal(key, (DT, QW), jnp.float32), -6.0, 6.0) * DT ** (-0.5)
    values = noise + 5.0 / DT * pattern[:, None] * tangent_vector[None, :]
    return values.astype(jnp.bfloat16)


def touch_ends(entries, key, smallest, top_value):
    shape = entries.shape
    index_at = [jax.random.randint(jax.random.fold_in(key, axis), (), 0, shape[axis]) for axis in range(len(shape))]
    entries = entries.at[tuple(index_at)].set(smallest)
    longest = shape.index(max(shape))
    index_at[longest] = (index_at[longest] + 1) % shape[longest]
    return entries.at[tuple(index_at)].set(top_value)


def levels(rng, extent, shards, smallest, top_value):
    level, own = 1.0, jax.random.fold_in(rng, 6)
    for dim, parts in shards:
        heights = jnp.exp(jax.random.uniform(jax.random.fold_in(own, dim), (parts,), jnp.float32, smallest / len(shards), top_value / len(shards)))
        level = level * jnp.repeat(heights, extent[dim] // parts).reshape([-1 if axis == dim else 1 for axis in range(len(extent))])
    return level


def profile(number_of, total, reach, skew):
    portions = [(1 << 20) // math.isqrt(standing ** skew) + 1 for standing in range(2, number_of + 1)]
    surplus, given = total - reach - (number_of - 1), [1] * (number_of - 1)
    while surplus > 0:
        candidates = [i for i in range(number_of - 1) if given[i] < reach]
        mass, left = sum([portions[i] for i in candidates]), surplus
        for i in candidates:
            extra = min(reach - given[i], max(1, left * portions[i] // mass), surplus)
            given[i] = given[i] + extra
            surplus = surplus - extra
    return np.array([reach] + given)


def uneven_parts(key, number_of, total, reach, lean):
    if number_of == 2:
        one = jax.random.randint(key, (), max(1, total - reach), min(reach, total - 1) + 1)
        return jnp.stack([one, total - one])
    sizes = jnp.asarray(profile(number_of, total, reach, lean), jnp.int32)
    pairs = (number_of - 1) // 2
    source_of, taker = sizes[1:1 + 2 * pairs:2], sizes[2:2 + 2 * pairs:2]
    margin = jnp.minimum(source_of - 1, reach - taker)
    passed = jax.random.randint(jax.random.fold_in(key, 1), (pairs,), 0, 1 << 20) % (margin + 1)
    sizes = sizes.at[1:1 + 2 * pairs:2].set(source_of - passed).at[2:2 + 2 * pairs:2].set(taker + passed)
    return sizes[jax.random.permutation(jax.random.fold_in(key, 2), number_of)]


def bell_draw(stream_key, shape, spread, limit, cuts=(), kind=jnp.bfloat16):
    drawn = spread * jax.random.normal(stream_key, shape, jnp.float32)
    if cuts:
        drawn = drawn * levels(stream_key, shape, cuts, -0.22, 0.18)
    return jnp.clip(drawn, -limit, limit).astype(kind)


def setup_inputs(seed: int = 0) -> dict:
    arg_keys = jax.random.split(jax.random.key(seed), 14)
    cap_hidden = draw_cap_hidden(jax.random.fold_in(arg_keys[13], 71), 0)
    t5_norm_gain = jnp.clip(1.0 + 0.1 * jax.random.normal(arg_keys[1], (DT,), jnp.float32), 0.5, 1.5).astype(jnp.bfloat16)
    t5_wi0 = bell_draw(arg_keys[2], (DT, FFT), DT ** -0.5, 0.09375, ((1, 16),))
    t5_wi1 = bell_draw(arg_keys[3], (DT, FFT), DT ** -0.5, 0.09375, ((1, 16),))
    t5_wo = bell_draw(arg_keys[4], (FFT, DT), (FFT // 4) ** -0.5, 0.15625, ((0, 16),))
    t5_final_gain = jnp.clip(1.0 + 0.1 * jax.random.normal(arg_keys[5], (DT,), jnp.float32), 0.5, 1.5).astype(jnp.bfloat16)
    cap_lengths = uneven_parts(arg_keys[6], CAPTIONS, (3 * CAPTIONS * LCAP) // 4, LCAP, 0).astype(jnp.int32)
    latents = draw_latents(jax.random.fold_in(arg_keys[13], 71), 0)
    w_query = draw_w_query(jax.random.fold_in(arg_keys[13], 71), 0)
    w_key = draw_w_key(jax.random.fold_in(arg_keys[13], 71), 0)
    w_value = bell_draw(arg_keys[10], (DT, QW), DT ** -0.5, 0.09375, ((1, 16),))
    caption_of_image = touch_ends(jax.random.randint(arg_keys[11], (IMAGES,), 0, CAPS), jax.random.fold_in(arg_keys[11], 1), 0, CAPS - 1).astype(jnp.int32)
    grad_out = bell_draw(arg_keys[12], (TOKENS, QW), 1.0, 6.0, ((0, 128),))
    return dict(cap_hidden=cap_hidden, t5_norm_gain=t5_norm_gain, t5_wi0=t5_wi0, t5_wi1=t5_wi1, t5_wo=t5_wo, t5_final_gain=t5_final_gain, cap_lengths=cap_lengths, latents=latents, w_query=w_query, w_key=w_key, w_value=w_value, caption_of_image=caption_of_image, grad_out=grad_out)


def rounded(values):
    return lax.optimization_barrier(values.astype(jnp.bfloat16)).astype(jnp.float32)

def rms_scale(values, gain):
    work = values.astype(jnp.float32)
    return work * lax.rsqrt(lax.optimization_barrier(jnp.mean(work * work, axis=-1, keepdims=True)) + 1e-06) * gain.astype(jnp.float32)

def attend(query_rows, grad_rows, key_rows, value_rows, lengths, owner):
    images = owner.shape[0]
    cap_count = lengths.shape[0]
    head_count = query_rows.shape[1] // HD
    inv_root = 1.0 / math.sqrt(HD)
    query_blocks = query_rows.reshape(images, IMG_TOK, head_count, HD).astype(jnp.float32)
    grad_blocks = grad_rows.reshape(images, IMG_TOK, head_count, HD).astype(jnp.float32)
    key_blocks = key_rows.reshape(cap_count, LCAP, head_count, HD).astype(jnp.float32)
    value_blocks = value_rows.reshape(cap_count, LCAP, head_count, HD).astype(jnp.float32)
    chosen = owner[:, None] == jnp.arange(cap_count, dtype=jnp.int32)[None, :]
    picker = chosen.astype(jnp.float32)
    key_img = jnp.einsum('ic,clhd->ilhd', picker, key_blocks, precision=lax.Precision.HIGHEST)
    value_img = jnp.einsum('ic,clhd->ilhd', picker, value_blocks, precision=lax.Precision.HIGHEST)
    live_len = lax.optimization_barrier(jnp.sum(jnp.where(chosen, lengths[None, :], 0), axis=1)).astype(jnp.int32)
    live_mask = jnp.arange(LCAP, dtype=jnp.int32)[None, :] < live_len[:, None]
    scores = jnp.einsum('ithd,ilhd->ihtl', query_blocks, key_img) * inv_root
    scores = jnp.where(live_mask[:, None, None, :], scores, -1e+30)
    row_max = lax.optimization_barrier(jnp.max(scores, axis=-1, keepdims=True))
    weights_exp = jnp.exp(scores - row_max)
    probs = weights_exp / lax.optimization_barrier(jnp.sum(weights_exp, axis=-1, keepdims=True))
    probs_b = rounded(probs)
    attn_blocks = jnp.einsum('ihtl,ilhd->ithd', probs_b, value_img)
    grad_probs = jnp.einsum('ithd,ilhd->ihtl', grad_blocks, value_img)
    grad_scores = rounded(probs * (grad_probs - lax.optimization_barrier(jnp.sum(probs * grad_probs, axis=-1, keepdims=True))))
    grad_queries = (jnp.einsum('ihtl,ilhd->ithd', grad_scores, key_img) * inv_root).astype(jnp.bfloat16)
    grad_key_img = jnp.einsum('ihtl,ithd->ilhd', grad_scores, query_blocks) * inv_root
    grad_value_img = jnp.einsum('ihtl,ithd->ilhd', probs_b, grad_blocks)
    grad_keys = jnp.einsum('ic,ilhd->clhd', picker, grad_key_img, precision=lax.Precision.HIGHEST).astype(jnp.bfloat16)
    grad_values = jnp.einsum('ic,ilhd->clhd', picker, grad_value_img, precision=lax.Precision.HIGHEST).astype(jnp.bfloat16)
    width = head_count * HD
    return (attn_blocks.reshape(images * IMG_TOK, width), grad_queries.reshape(images * IMG_TOK, width), grad_keys.reshape(cap_count * LCAP, width), grad_values.reshape(cap_count * LCAP, width))

def reference(cap_hidden, t5_norm_gain, t5_wi0, t5_wi1, t5_wo, t5_final_gain, cap_lengths, latents, w_query, w_key, w_value, caption_of_image, grad_out):
    normed = rms_scale(cap_hidden, t5_norm_gain).astype(jnp.bfloat16)
    gate_value = jnp.dot(normed, t5_wi0, preferred_element_type=jnp.float32)
    lift_value = jnp.dot(normed, t5_wi1, preferred_element_type=jnp.float32)
    hidden_act = (jax.nn.gelu(gate_value, approximate=True) * lift_value).astype(jnp.bfloat16)
    ff_total = jnp.dot(hidden_act, t5_wo, preferred_element_type=jnp.float32)
    caption = rms_scale(cap_hidden.astype(jnp.float32) + ff_total, t5_final_gain).astype(jnp.bfloat16)
    key_rows = jnp.dot(caption, w_key, preferred_element_type=jnp.float32).astype(jnp.bfloat16)
    value_rows = jnp.dot(caption, w_value, preferred_element_type=jnp.float32).astype(jnp.bfloat16)
    lat = latents.astype(jnp.float32)
    mean_removed_input = lat - lax.optimization_barrier(jnp.mean(lat, axis=-1, keepdims=True))
    reciprocal_deviation = lax.rsqrt(lax.optimization_barrier(jnp.mean(mean_removed_input * mean_removed_input, axis=-1, keepdims=True)) + 1e-06)
    standardized_input = mean_removed_input * reciprocal_deviation
    normalized_latent_rows = standardized_input.astype(jnp.bfloat16)
    queries = jnp.dot(normalized_latent_rows, w_query, preferred_element_type=jnp.float32).astype(jnp.bfloat16)
    group_tok = TOK_DEV * N_FSDP
    group_img = group_tok // IMG_TOK
    caption_token_rows = CAPS * LCAP

    def one_group(group_index):
        group_index = jnp.asarray(group_index).astype(jnp.int32)
        tok_start = group_index * group_tok
        cap_start = group_index * caption_token_rows
        query_rows = lax.dynamic_slice_in_dim(queries, tok_start, group_tok, 0)
        grad_rows = lax.dynamic_slice_in_dim(grad_out, tok_start, group_tok, 0)
        key_group = lax.dynamic_slice_in_dim(key_rows, cap_start, caption_token_rows, 0)
        value_group = lax.dynamic_slice_in_dim(value_rows, cap_start, caption_token_rows, 0)
        lengths = lax.dynamic_slice_in_dim(cap_lengths, group_index * CAPS, CAPS, 0)
        owner = lax.dynamic_slice_in_dim(caption_of_image, group_index * group_img, group_img, 0)
        return attend(query_rows, grad_rows, key_group, value_group, lengths, owner)
    attn_all, grad_all, keys_all, values_all = lax.map(one_group, jnp.arange(N_DP, dtype=jnp.int32))
    attn_out = attn_all.reshape(TOKENS, QW)
    grad_queries = grad_all.reshape(TOKENS, QW)
    grad_keys = keys_all.reshape(CAPTIONS * LCAP, QW)
    grad_values = values_all.reshape(CAPTIONS * LCAP, QW)
    grad_key = lax.dot_general(caption, grad_keys, (((0,), (0,)), ((), ())), preferred_element_type=jnp.float32)
    grad_value = lax.dot_general(caption, grad_values, (((0,), (0,)), ((), ())), preferred_element_type=jnp.float32)
    normalized_input_gradient = lax.dot_general(grad_queries, w_query, (((1,), (1,)), ((), ())), preferred_element_type=jnp.float32)
    latent_token_gradient = reciprocal_deviation * (normalized_input_gradient - lax.optimization_barrier(jnp.mean(normalized_input_gradient, axis=-1, keepdims=True)) - standardized_input * lax.optimization_barrier(jnp.mean(normalized_input_gradient * standardized_input, axis=-1, keepdims=True)))
    grad_query = lax.dot_general(normalized_latent_rows, grad_queries, (((0,), (0,)), ((), ())), preferred_element_type=jnp.float32)
    return (attn_out, latent_token_gradient, grad_query, grad_key, grad_value)
```

```python
import functools
import math

import jax
import jax.numpy as jnp
from jax import lax
from jax.experimental import pallas as pl
from jax.experimental.pallas import tpu as pltpu
from jax.sharding import PartitionSpec as P

HD = 128
LCAP = 256
BF = jnp.bfloat16
F32 = jnp.float32
MESH = pl.DeviceIdType.MESH


def coords():
    d, f = lax.axis_index("dp"), lax.axis_index("fsdp")
    return d // 2, d % 2, f // 8, (f // 2) % 4, f % 2


def device(y, zh, zl, x, c):
    return (y * 2 + zh, zl * 8 + x * 2 + c)


def x_peers(y, zh, zl, x, c):
    return [(device(y, zh, zl, (x + k) % 4, c), (x + k) % 4) for k in (1, 2, 3)]


def y_peers(y, zh, zl, x, c):
    return [(device((y + k) % 4, zh, zl, x, c), (y + k) % 4) for k in (1, 2, 3)]


def z_peers(y, zh, zl, x, c):
    z = zh * 2 + zl
    there = [(z + k) % 4 for k in (1, 2, 3)]
    return [(device(y, t // 2, t % 2, x, c), t) for t in there]


def dp_peers(y, zh, zl, x, c):
    there = [((y + k) % 4, (zh + a) % 2) for a in (0, 1) for k in range(4) if a or k]
    return [(device(v, w, zl, x, c), v * 2 + w) for v, w in there]


def chip_peers(y, zh, zl, x, c):
    there = [((zl + a) % 2, (x + k) % 4) for a in (0, 1) for k in range(4) if a or k]
    return [(device(y, zh, w, v, c), w * 4 + v) for w, v in there]


def quad_peers(y, zh, zl, x, c):
    there = [((zl + a) % 2, (c + b) % 2) for a in (0, 1) for b in (0, 1) if a or b]
    return [(device(y, zh, w, x, b), w * 2 + b) for w, b in there]


def core_peer(y, zh, zl, x, c):
    return [(device(y, zh, zl, x, 1 - c), 1 - c)]


def span(index, size):
    return pl.ds(pl.multiple_of(index * size, size), size)


class Sender:
    def __init__(self, send_sem, recv_sem):
        self.sems, self.count, self.open = (send_sem, recv_sem), 0, []

    def send(self, src, dst, to):
        t = self.count
        self.count += 1
        if to is None:
            copy = pltpu.make_async_copy(src, dst, self.sems[0].at[t])
        else:
            copy = pltpu.make_async_remote_copy(
                src_ref=src,
                dst_ref=dst,
                send_sem=self.sems[0].at[t],
                recv_sem=self.sems[1].at[t],
                device_id=to,
                device_id_type=MESH,
            )
        copy.start()
        self.open.append((copy, to is None))
        return copy

    def finish(self, landed=()):
        for copy, own in self.open:
            if own:
                copy.wait()
            elif any(copy is other for other in landed):
                copy.wait_send()
            else:
                copy.wait()


def exchange(name, cid, copies, body, groups, outs, *ins):
    def kernel(*refs):
        in_refs, out_refs = refs[: len(ins)], refs[len(ins) : len(ins) + len(outs)]
        place = coords()
        barrier = pltpu.get_barrier_semaphore()
        peers = [to for group in groups for to, _ in group(*place)]
        for to in peers:
            pl.semaphore_signal(barrier, inc=1, device_id=to, device_id_type=MESH)
        pl.semaphore_wait(barrier, len(peers))
        sender = Sender(refs[-2], refs[-1])
        landed = body(sender, place, in_refs, out_refs)
        assert sender.count == copies, sender.count
        sender.finish(landed or ())

    return pl.pallas_call(
        kernel,
        out_shape=[jax.ShapeDtypeStruct(shape, BF) for shape in outs],
        in_specs=[pl.BlockSpec(memory_space=pl.ANY)] * len(ins),
        out_specs=[pl.BlockSpec(memory_space=pl.ANY)] * len(outs),
        scratch_shapes=[
            pltpu.SemaphoreType.DMA((copies,)),
            pltpu.SemaphoreType.DMA((copies,)),
        ],
        compiler_params=pltpu.CompilerParams(collective_id=cid, has_side_effects=True),
        name=name,
    )(*ins)


def first_body(s, place, ins, outs):
    xn, go, w = ins
    xs, gs, wx = outs
    y, zh, zl, x, c = place
    mine = zl * 2 + c
    pair = core_peer(*place)[0][0]
    across = device(y, zh, 1 - zl, x, c)
    over = s.send(w, wx.at[span(mine, 256)], across)
    for to, v in x_peers(*place) + [(None, x)]:
        for half in (0, 1):
            s.send(
                xn.at[:, span(half * 4 + v, 512)],
                xs.at[span(x, 128), pl.ds(half * 512, 512)],
                to,
            )
            s.send(
                go.at[:, span(half * 4 + v, 256)],
                gs.at[span(x, 128), pl.ds(half * 256, 256)],
                to,
            )
    s.send(w, wx.at[span(mine, 256)], pair)
    s.send(w, wx.at[span(mine, 256)], None)
    over.wait_recv()
    theirs = (1 - zl) * 2 + c
    s.send(wx.at[span(theirs, 256)], wx.at[span(theirs, 256)], pair)
    return (over,)


def core_body(s, place, ins, outs):
    c = place[4]
    s.send(ins[0].at[1 - c], outs[0], core_peer(*place)[0][0])


def scatter_body(s, place, ins, outs):
    ff, qp = ins
    fr, qr = outs
    y, zh, zl, x, c = place
    here = zl * 4 + x
    for to, j in chip_peers(*place) + [(None, here)]:
        s.send(ff.at[j], fr.at[here], to)
    for to, v in x_peers(*place) + [(None, x)]:
        s.send(qp.at[:, span(v, 512)], qr.at[x], to)


def caption_body(s, place, ins, outs):
    (rows,) = ins
    (full,) = outs
    y, zh, zl, x, c = place
    here = zl * 4 + x
    pair = core_peer(*place)[0][0]
    coming = []
    for a in (0, 1):
        for k in (1, 3, 2, 0):
            if a or k:
                to = device(y, zh, (zl + a) % 2, (x + k) % 4, c)
                coming.append(
                    (s.send(rows, full.at[c, here], to), ((zl + a) % 2) * 4 + (x + 4 - k) % 4)
                )
    s.send(rows, full.at[c, here], pair)
    s.send(rows, full.at[c, here], None)
    for copy, j in coming:
        copy.wait_recv()
        s.send(full.at[c, j], full.at[c, j], pair)
    return tuple(copy for copy, _ in coming)


def quad_body(s, place, ins, outs):
    (sel,) = ins
    (kv,) = outs
    y, zh, zl, x, c = place
    here = zl * 2 + c
    for to, q in quad_peers(*place) + [(None, here)]:
        s.send(sel.at[q // 2], kv.at[here], to)


def attn_back_body(s, place, ins, outs):
    attn, gkv = ins
    tok, parts = outs
    y, zh, zl, x, c = place
    here = zl * 2 + c
    for to, q in quad_peers(*place) + [(None, here)]:
        s.send(gkv.at[q], parts.at[here], to)
    for to, v in x_peers(*place) + [(None, x)]:
        for half in (0, 1):
            s.send(
                attn.at[span(v, 128), pl.ds(half * 256, 256)],
                tok.at[:, span(half * 4 + x, 256)],
                to,
            )


def gather_body(s, place, ins, outs):
    gq, kvp = ins
    gqa, kvr = outs
    y, zh, zl, x, c = place
    here = y * 2 + zh
    for to, v in x_peers(*place) + [(None, x)]:
        s.send(gq, gqa.at[:, span(x, 512)], to)
    for to, j in dp_peers(*place) + [(None, here)]:
        s.send(kvp.at[j], kvr.at[here], to)


def grads_body(s, place, ins, outs):
    dxn, part, kvs = ins
    dtok, r1, r2, kva = outs
    y, zh, zl, x, c = place
    z = zh * 2 + zl
    here = y * 2 + zh
    for to, v in y_peers(*place) + [(None, y)]:
        s.send(part.at[:, v, :, :, pl.ds(0, 1024)], r1.at[y], to)
    for to, t in z_peers(*place) + [(None, z)]:
        s.send(part.at[t % 2, :, t // 2, :, pl.ds(1024, 1024)], r2.at[z], to)
    for to, v in x_peers(*place) + [(None, x)]:
        for half in (0, 1):
            s.send(
                dxn.at[span(v, 128), pl.ds(half * 512, 512)],
                dtok.at[:, span(half * 4 + x, 512)],
                to,
            )
    for to, j in dp_peers(*place) + [(None, here)]:
        s.send(kvs, kva.at[here], to)


def second_body(s, place, ins, outs):
    s1, s2 = ins
    r1, r2 = outs
    y, zh, zl, x, c = place
    z = zh * 2 + zl
    for to, t in z_peers(*place) + [(None, z)]:
        s.send(s1.at[t % 2, t // 2], r1.at[z], to)
    for to, v in y_peers(*place) + [(None, y)]:
        s.send(s2.at[v], r2.at[y], to)


def last_body(s, place, ins, outs):
    y, zh, zl, x, c = place
    here = y * 2 + zh
    for to, j in dp_peers(*place) + [(None, here)]:
        s.send(ins[0], outs[0].at[here], to)


def attend_kernel(live_ref, q_ref, g_ref, kv_ref, attn_ref, gq_ref, gkv_ref):
    inv_root = 1.0 / math.sqrt(HD)
    q, g = q_ref[...], g_ref[...]
    k, v = kv_ref[0, :, :HD], kv_ref[0, :, HD:]
    nt = (((1,), (1,)), ((), ()))
    tn = (((0,), (0,)), ((), ()))
    scores = lax.dot_general(q, k, nt, preferred_element_type=F32) * inv_root
    live = lax.broadcasted_iota(jnp.int32, scores.shape, 1) < live_ref[0]
    scores = jnp.where(live, scores, -1e30)
    e = jnp.exp(scores - jnp.max(scores, axis=-1, keepdims=True))
    probs = e / jnp.sum(e, axis=-1, keepdims=True)
    probs_b = probs.astype(BF)
    attn_ref[...] = jnp.dot(probs_b, v, preferred_element_type=F32).astype(BF)
    gp = lax.dot_general(g, v, nt, preferred_element_type=F32)
    gs = (probs * (gp - jnp.sum(probs * gp, axis=-1, keepdims=True))).astype(BF)
    gq_ref[...] = (jnp.dot(gs, k, preferred_element_type=F32) * inv_root).astype(BF)
    gk = lax.dot_general(gs, q, tn, preferred_element_type=F32) * inv_root
    gv = lax.dot_general(probs_b, g, tn, preferred_element_type=F32)
    gkv_ref[0, :, :HD] = gk.astype(BF)
    gkv_ref[0, :, HD:] = gv.astype(BF)


def attend(live, q, g, kv):
    rows = q.shape[0]
    col = pl.BlockSpec((rows, HD), lambda h: (0, h))
    per = pl.BlockSpec((1, LCAP, 2 * HD), lambda h: (h, 0, 0))
    return pl.pallas_call(
        attend_kernel,
        grid=(4,),
        out_shape=[
            jax.ShapeDtypeStruct(q.shape, BF),
            jax.ShapeDtypeStruct(q.shape, BF),
            jax.ShapeDtypeStruct(kv.shape, BF),
        ],
        in_specs=[pl.BlockSpec(memory_space=pltpu.SMEM), col, col, per],
        out_specs=[col, col, per],
        compiler_params=pltpu.CompilerParams(vmem_limit_bytes=32 * 2**20),
        name="attend",
    )(live, q, g, kv)


def rms_scale(values, gain):
    work = values.astype(F32)
    return (
        work
        * lax.rsqrt(jnp.mean(work * work, axis=-1, keepdims=True) + 1e-06)
        * gain.astype(F32)
    )


def local(
    cap_hidden,
    t5_norm_gain,
    t5_wi0,
    t5_wi1,
    t5_wo,
    t5_final_gain,
    cap_lengths,
    latents,
    w_query,
    w_key,
    w_value,
    caption_of_image,
    grad_out,
):
    y, zh, zl, x, c = coords()

    lat = latents.astype(F32)
    removed = lat - jnp.mean(lat, axis=-1, keepdims=True)
    rstd = lax.rsqrt(jnp.mean(removed * removed, axis=-1, keepdims=True) + 1e-06)
    xhat = removed * rstd
    xn = xhat.astype(BF)
    wq = w_query.reshape(256, 2, 4, 256).transpose(0, 2, 1, 3).reshape(256, 2048)
    xs, gs, wx = exchange(
        "tokens_to_features",
        0,
        20,
        first_body,
        (x_peers, quad_peers),
        [(512, 1024), (512, 512), (1024, 2048)],
        xn,
        grad_out,
        wq,
    )

    normed = rms_scale(cap_hidden, t5_norm_gain).astype(BF)
    gate = jnp.dot(normed, t5_wi0, preferred_element_type=F32)
    lift = jnp.dot(normed, t5_wi1, preferred_element_type=F32)
    hidden = (jax.nn.gelu(gate, approximate=True) * lift).astype(BF)
    term = jnp.dot(hidden, t5_wo, preferred_element_type=F32).astype(BF)
    term = term.reshape(2, 256, 4096)
    (other,) = exchange(
        "ff_core_pair", 1, 1, core_body, (core_peer,), [(256, 4096)], term
    )
    own = lax.dynamic_index_in_dim(term, c, 0, keepdims=False)
    ff_pair = (own.astype(F32) + other.astype(F32)).astype(BF)
    q_part = jnp.dot(xs, wx, preferred_element_type=F32).astype(BF)

    ff_blocks, q_blocks = exchange(
        "ff_and_query_scatter",
        2,
        12,
        scatter_body,
        (chip_peers,),
        [(8, 32, 4096), (4, 512, 512)],
        ff_pair.reshape(8, 32, 4096),
        q_part,
    )
    ff_rows = jnp.sum(ff_blocks.astype(F32), axis=0)
    row = c * 256 + (zl * 4 + x) * 32
    cap_rows = lax.dynamic_slice_in_dim(cap_hidden, row, 32, 0)
    caption_rows = rms_scale(cap_rows.astype(F32) + ff_rows, t5_final_gain).astype(BF)
    queries = jnp.sum(q_blocks.astype(F32), axis=0).astype(BF)

    (caption,) = exchange(
        "caption_gather",
        3,
        16,
        caption_body,
        (chip_peers, core_peer),
        [(2, 8, 32, 4096)],
        caption_rows,
    )
    caption = caption.reshape(512, 4096)
    keys = jnp.dot(caption, w_key, preferred_element_type=F32).astype(BF)
    values = jnp.dot(caption, w_value, preferred_element_type=F32).astype(BF)
    key_value = jnp.concatenate([keys, values], axis=1).reshape(2, LCAP, 256)
    chosen = caption_of_image[:, None, None] == 0
    selected = jnp.where(chosen, key_value[:1], key_value[1:])
    (kv,) = exchange(
        "keys_to_heads", 4, 4, quad_body, (quad_peers,), [(4, LCAP, 256)], selected
    )

    mine = lax.dynamic_index_in_dim(caption_of_image, zl, 0)
    live = jnp.where(mine == 0, cap_lengths[:1], cap_lengths[1:])
    attn, gq, gkv = attend(live, queries, gs, kv)

    attn_tok, gkv_parts = exchange(
        "attn_to_tokens",
        5,
        12,
        attn_back_body,
        (x_peers, quad_peers),
        [(128, 2048), (4, LCAP, 256)],
        attn,
        gkv,
    )
    attn_out = attn_tok.astype(F32)
    per_image = jnp.sum(gkv_parts.reshape(2, 2, LCAP, 256).astype(F32), axis=1)
    grad_kv = jnp.stack(
        [
            jnp.sum(jnp.where(caption_of_image[:, None, None] == i, per_image, 0.0), axis=0)
            for i in (0, 1)
        ]
    )
    grad_kv = grad_kv.astype(BF).reshape(512, 256)
    kv_part = lax.dot_general(
        caption, grad_kv, (((0,), (0,)), ((), ())), preferred_element_type=F32
    ).astype(BF)

    gq_all, kv_blocks = exchange(
        "grad_query_gather",
        6,
        12,
        gather_body,
        (x_peers, dp_peers),
        [(512, 2048), (8, 512, 256)],
        gq,
        kv_part.reshape(8, 512, 256),
    )
    kv_sum = jnp.sum(kv_blocks.astype(F32), axis=0).astype(BF)
    dxn = lax.dot_general(
        gq_all, wx, (((1,), (1,)), ((), ())), preferred_element_type=F32
    ).astype(BF)
    q_grad = lax.dot_general(
        xs, gq_all, (((0,), (0,)), ((), ())), preferred_element_type=F32
    ).astype(BF)
    q_grad = q_grad.reshape(2, 2, 256, 2048).transpose(1, 0, 2, 3)
    (other,) = exchange(
        "grad_query_core_pair", 7, 1, core_body, (core_peer,), [(2, 256, 2048)], q_grad
    )
    own = lax.dynamic_index_in_dim(q_grad, c, 0, keepdims=False)
    pair = (own.astype(F32) + other.astype(F32)).astype(BF).reshape(2, 4, 2, 32, 2048)

    dtok, r1, r2, kv_all = exchange(
        "grads_scatter",
        8,
        24,
        grads_body,
        (x_peers, y_peers, z_peers, dp_peers),
        [(128, 4096), (4, 2, 2, 32, 1024), (4, 4, 32, 1024), (8, 512, 256)],
        dxn,
        pair,
        kv_sum,
    )
    s1 = jnp.sum(r1.astype(F32), axis=0).astype(BF)
    s2 = jnp.sum(r2.astype(F32), axis=0).astype(BF)
    t1, t2 = exchange(
        "grad_query_scatter",
        9,
        8,
        second_body,
        (y_peers, z_peers),
        [(4, 32, 1024), (4, 32, 1024)],
        s1,
        s2,
    )
    block = jnp.concatenate(
        [jnp.sum(t1.astype(F32), axis=0), jnp.sum(t2.astype(F32), axis=0)], axis=1
    ).astype(BF)
    (q_full,) = exchange(
        "grad_query_spread", 10, 8, last_body, (dp_peers,), [(8, 32, 2048)], block
    )

    grad_xn = dtok.astype(F32)
    latent_token_gradient = rstd * (
        grad_xn
        - jnp.mean(grad_xn, axis=-1, keepdims=True)
        - xhat * jnp.mean(grad_xn * xhat, axis=-1, keepdims=True)
    )
    grad_query = (
        q_full.reshape(256, 4, 2, 256).transpose(0, 2, 1, 3).reshape(256, 2048).astype(F32)
    )
    kv_all = kv_all.reshape(4096, 256).astype(F32)
    return (attn_out, latent_token_gradient, grad_query, kv_all[:, :128], kv_all[:, 128:])


def solution(mesh):
    placed = (
        P("dp", None),
        P(),
        P(None, "fsdp"),
        P(None, "fsdp"),
        P("fsdp", None),
        P(),
        P("dp"),
        P(("dp", "fsdp"), None),
        P("fsdp", None),
        P(None, "fsdp"),
        P(None, "fsdp"),
        P("dp"),
        P(("dp", "fsdp"), None),
    )
    return jax.shard_map(
        local,
        mesh=mesh,
        in_specs=placed,
        out_specs=(
            P(("dp", "fsdp"), None),
            P(("dp", "fsdp"), None),
            P("fsdp", None),
            P(None, "fsdp"),
            P(None, "fsdp"),
        ),
        check_vma=False,
    )
```

```python
import functools
import math

import jax
import jax.numpy as jnp
from jax import lax
from jax.experimental import pallas as pl
from jax.experimental.pallas import tpu as pltpu
from jax.sharding import PartitionSpec as P

HD = 128
LCAP = 256
BF = jnp.bfloat16
F32 = jnp.float32
MESH = pl.DeviceIdType.MESH


def coords():
    d, f = lax.axis_index("dp"), lax.axis_index("fsdp")
    return d // 2, d % 2, f // 8, (f // 2) % 4, f % 2


def device(y, zh, zl, x, c):
    return (y * 2 + zh, zl * 8 + x * 2 + c)


def x_peers(y, zh, zl, x, c):
    return [(device(y, zh, zl, (x + k) % 4, c), (x + k) % 4) for k in (1, 2, 3)]


def y_peers(y, zh, zl, x, c):
    return [(device((y + k) % 4, zh, zl, x, c), (y + k) % 4) for k in (1, 2, 3)]


def z_peers(y, zh, zl, x, c):
    z = zh * 2 + zl
    there = [(z + k) % 4 for k in (1, 2, 3)]
    return [(device(y, t // 2, t % 2, x, c), t) for t in there]


def dp_peers(y, zh, zl, x, c):
    there = [((y + k) % 4, (zh + a) % 2) for a in (0, 1) for k in range(4) if a or k]
    return [(device(v, w, zl, x, c), v * 2 + w) for v, w in there]


def chip_peers(y, zh, zl, x, c):
    there = [((zl + a) % 2, (x + k) % 4) for a in (0, 1) for k in range(4) if a or k]
    return [(device(y, zh, w, v, c), w * 4 + v) for w, v in there]


def quad_peers(y, zh, zl, x, c):
    there = [((zl + a) % 2, (c + b) % 2) for a in (0, 1) for b in (0, 1) if a or b]
    return [(device(y, zh, w, x, b), w * 2 + b) for w, b in there]


def core_peer(y, zh, zl, x, c):
    return [(device(y, zh, zl, x, 1 - c), 1 - c)]


def span(index, size):
    return pl.ds(pl.multiple_of(index * size, size), size)


class Sender:
    def __init__(self, send_sem, recv_sem):
        self.sems, self.count, self.open = (send_sem, recv_sem), 0, []

    def send(self, src, dst, to):
        t = self.count
        self.count += 1
        if to is None:
            copy = pltpu.make_async_copy(src, dst, self.sems[0].at[t])
        else:
            copy = pltpu.make_async_remote_copy(
                src_ref=src,
                dst_ref=dst,
                send_sem=self.sems[0].at[t],
                recv_sem=self.sems[1].at[t],
                device_id=to,
                device_id_type=MESH,
            )
        copy.start()
        entry = [copy, to is None, False]
        self.open.append(entry)
        return entry

    def landed(self, entry):
        copy, own, seen = entry
        if not seen:
            copy.wait() if own else copy.wait_recv()
            entry[2] = True

    done = landed

    def finish(self):
        for copy, own, seen in self.open:
            if own and not seen:
                copy.wait()
            elif not own and seen:
                copy.wait_send()
            elif not own:
                copy.wait()


def exchange(name, cid, copies, body, groups, outs, *ins):
    def kernel(*refs):
        in_refs, out_refs = refs[: len(ins)], refs[len(ins) : len(ins) + len(outs)]
        place = coords()
        barrier = pltpu.get_barrier_semaphore()
        peers = [to for group in groups for to, _ in group(*place)]
        for to in peers:
            pl.semaphore_signal(barrier, inc=1, device_id=to, device_id_type=MESH)
        pl.semaphore_wait(barrier, len(peers))
        sender = Sender(refs[-2], refs[-1])
        body(sender, place, in_refs, out_refs)
        assert sender.count == copies, sender.count
        sender.finish()

    return pl.pallas_call(
        kernel,
        out_shape=[jax.ShapeDtypeStruct(shape, BF) for shape in outs],
        in_specs=[pl.BlockSpec(memory_space=pl.ANY)] * len(ins),
        out_specs=[pl.BlockSpec(memory_space=pl.ANY)] * len(outs),
        scratch_shapes=[
            pltpu.SemaphoreType.DMA((copies,)),
            pltpu.SemaphoreType.DMA((copies,)),
        ],
        compiler_params=pltpu.CompilerParams(collective_id=cid, has_side_effects=True),
        name=name,
    )(*ins)


NT = (((1,), (1,)), ((), ()))
TN = (((0,), (0,)), ((), ()))


def front_kernel(
    lat, go, wq, ch, wi0, wi1, wo, wk, wv, gain, gain2, pick, live,
    xs_out, wx_out, cap_out, attn_out, gq_out, gkv_out,
    lat_v, xn_v, wp_v, ch_v, row_v, wi_v, wo_v, wkv_v, wx_v, xs_v, gs_v, gl_v, hid_v,
    give_v, keep_v, rc_v, fr_v, qs_v, qr_v, q_v, cap_v, kv_v, sel_v, kvr_v,
    attn_v, gq_v, gkv_v, sems_a, sems_b,
):
    place = coords()
    y, zh, zl, x, c = place
    pair = core_peer(*place)[0][0]
    across = device(y, zh, 1 - zl, x, c)
    here, mine = zl * 4 + x, zl * 2 + c
    xp = x_peers(*place)
    chips = []
    for a in (0, 1):
        for k in (1, 3, 2, 0):
            if a or k:
                chips.append(
                    (
                        device(y, zh, (zl + a) % 2, (x + k) % 4, c),
                        ((zl + a) % 2) * 4 + (x + k) % 4,
                        ((zl + a) % 2) * 4 + (x + 4 - k) % 4,
                    )
                )
    s = Sender(sems_a, sems_b)

    perm = [
        s.send(wq.at[:, pl.ds(h * 1024 + v * 256, 256)], wp_v.at[:, pl.ds(v * 512 + h * 256, 256)], None)
        for h in (0, 1)
        for v in range(4)
    ]
    lat_in = s.send(lat, lat_v, None)
    ch_in = s.send(ch, ch_v, None)
    wi_in = [
        s.send(wi0, wi_v.at[:, pl.ds(0, 384)], None),
        s.send(wi1, wi_v.at[:, pl.ds(384, 384)], None),
    ]
    wo_in = s.send(wo, wo_v, None)
    wkv_in = [
        s.send(wk, wkv_v.at[:, pl.ds(0, 128)], None),
        s.send(wv, wkv_v.at[:, pl.ds(128, 128)], None),
    ]
    barrier = pltpu.get_barrier_semaphore()
    peers = [to for group in (chip_peers, quad_peers) for to, _ in group(*place)]
    for to in peers:
        pl.semaphore_signal(barrier, inc=1, device_id=to, device_id_type=MESH)
    pl.semaphore_wait(barrier, len(peers))

    for copy in perm:
        s.done(copy)
    w_over = s.send(wp_v, wx_v.at[span(mine, 256)], across)
    w_pair = s.send(wp_v, wx_v.at[span(mine, 256)], pair)
    w_own = s.send(wp_v, wx_v.at[span(mine, 256)], None)

    s.done(lat_in)

    @pl.loop(0, 8)
    def _(i):
        rows = pl.ds(pl.multiple_of(i * 16, 16), 16)
        v = lat_v[rows, :].astype(F32)
        r = v - jnp.mean(v, axis=-1, keepdims=True)
        xn_v[rows, :] = (r * lax.rsqrt(jnp.mean(r * r, axis=-1, keepdims=True) + 1e-06)).astype(BF)

    x_in, g_in = [], []
    for to, v in xp + [(None, x)]:
        for half in (0, 1):
            x_in.append(
                s.send(
                    xn_v.at[:, span(half * 4 + v, 512)],
                    xs_v.at[span(x, 128), pl.ds(half * 512, 512)],
                    to,
                )
            )
    for to, v in xp + [(None, x)]:
        for half in (0, 1):
            g_in.append(
                s.send(
                    go.at[:, span(half * 4 + v, 256)],
                    gs_v.at[span(x, 128), pl.ds(half * 256, 256)],
                    to,
                )
            )

    s.done(ch_in)
    row_v[...] = ch_v[span(c * 8 + here, 32), :]

    @pl.loop(0, 32)
    def _(i):
        rows = pl.ds(pl.multiple_of(i * 16, 16), 16)
        v = ch_v[rows, :].astype(F32)
        v = v * lax.rsqrt(jnp.mean(v * v, axis=-1, keepdims=True) + 1e-06) * gain[:1, :].astype(F32)
        ch_v[rows, :] = v.astype(BF)

    for copy in wi_in:
        s.done(copy)

    @pl.loop(0, 6)
    def _(i):
        rows = pl.ds(pl.multiple_of((i // 3) * 256, 256), 256)
        cols = pl.ds(pl.multiple_of((i % 3) * 256, 256), 256)
        gl_v[rows, cols] = jnp.dot(ch_v[rows, :], wi_v[:, cols], preferred_element_type=F32)

    @pl.loop(0, 8)
    def _(i):
        rows = pl.ds(pl.multiple_of(i * 64, 64), 64)
        g, u = gl_v[rows, :384], gl_v[rows, 384:]
        hid_v[rows, :] = (jax.nn.gelu(g, approximate=True) * u).astype(BF)

    s.done(wo_in)

    def term(which, out):
        rows = span(which, 256)

        @pl.loop(0, 8)
        def _(i):
            cols = pl.ds(pl.multiple_of(i * 512, 512), 512)
            out[:, cols] = jnp.dot(
                hid_v[rows, :], wo_v[:, cols], preferred_element_type=F32
            ).astype(BF)

    term(1 - c, give_v)
    ff_pair = s.send(give_v, rc_v, pair)
    term(c, keep_v)
    s.landed(ff_pair)

    @pl.loop(0, 16)
    def _(i):
        rows = pl.ds(pl.multiple_of(i * 16, 16), 16)
        keep_v[rows, :] = (keep_v[rows, :].astype(F32) + rc_v[rows, :].astype(F32)).astype(BF)

    ff_in = [s.send(keep_v.at[span(j, 32)], fr_v.at[here], to) for to, j, _ in chips]
    fr_v[here] = keep_v[span(here, 32), :]

    s.landed(w_over)
    theirs = (1 - zl) * 2 + c
    w_far = s.send(wx_v.at[span(theirs, 256)], wx_v.at[span(theirs, 256)], pair)
    for copy in x_in + [w_pair, w_own, w_far]:
        s.landed(copy)

    def query_block(v, out, at):
        @pl.loop(0, 4)
        def _(i):
            rows = pl.ds(pl.multiple_of((i // 2) * 256, 256), 256)
            cols = pl.ds(pl.multiple_of((i % 2) * 256, 256), 256)
            from_cols = pl.ds(pl.multiple_of(v * 512 + (i % 2) * 256, 256), 256)
            out[at, rows, cols] = jnp.dot(
                xs_v[rows, :], wx_v[:, from_cols], preferred_element_type=F32
            ).astype(BF)

    q_in = []
    for k, (to, v) in enumerate(xp):
        query_block(v, qs_v, k)
        q_in.append(s.send(qs_v.at[k], qr_v.at[x], to))
    query_block(x, qr_v, x)
    s.send(xs_v, xs_out, None)
    s.send(wx_v, wx_out, None)

    for copy in ff_in:
        s.landed(copy)
    ff = fr_v[0].astype(F32)
    for j in range(1, 8):
        ff = ff + fr_v[j].astype(F32)
    r = row_v[...].astype(F32) + ff
    r = r * lax.rsqrt(jnp.mean(r * r, axis=-1, keepdims=True) + 1e-06) * gain2[:1, :].astype(F32)
    cap_v[c, here] = r.astype(BF)
    own = cap_v.at[c, here]
    cap_in = [(s.send(own, own, to), j) for to, _, j in chips]
    cap_pair = [s.send(own, own, pair)]

    for copy in q_in:
        s.landed(copy)

    @pl.loop(0, 8)
    def _(i):
        rows = pl.ds(pl.multiple_of(i * 64, 64), 64)
        q = qr_v[0, rows, :].astype(F32) + qr_v[1, rows, :].astype(F32)
        q = q + qr_v[2, rows, :].astype(F32) + qr_v[3, rows, :].astype(F32)
        q_v[rows, :] = q.astype(BF)

    for copy, j in cap_in:
        s.landed(copy)
        block = cap_v.at[c, j]
        cap_pair.append(s.send(block, block, pair))
    for copy in wkv_in:
        s.done(copy)

    def key_value(which):
        rows = cap_v[which].reshape(256, 4096)
        kv_v[which] = jnp.dot(rows, wkv_v[...], preferred_element_type=F32).astype(BF)

    key_value(c)
    for copy in cap_pair:
        s.landed(copy)
    key_value(1 - c)
    s.send(cap_v, cap_out, None)
    for i in (0, 1):
        p = pick[i, :1, :]
        both = kv_v[0].astype(F32) * p + kv_v[1].astype(F32) * (1.0 - p)
        sel_v[i] = both.astype(BF)
    kv_in = [s.send(sel_v.at[q // 2], kvr_v.at[mine], to) for to, q in quad_peers(*place)]
    kvr_v[mine] = sel_v[zl]
    for copy in g_in + kv_in:
        s.landed(copy)

    inv_root = 1.0 / math.sqrt(HD)

    @pl.loop(0, 4)
    def _(h):
        cols = pl.ds(pl.multiple_of(h * HD, HD), HD)
        q, g = q_v[:, cols], gs_v[:, cols]
        k, v = kvr_v[h, :, :HD], kvr_v[h, :, HD:]
        scores = lax.dot_general(q, k, NT, preferred_element_type=F32) * inv_root
        scores = jnp.where(live[:1, :] > 0.5, scores, -1e30)
        e = jnp.exp(scores - jnp.max(scores, axis=-1, keepdims=True))
        probs = e / jnp.sum(e, axis=-1, keepdims=True)
        probs_b = probs.astype(BF)
        attn_v[:, cols] = jnp.dot(probs_b, v, preferred_element_type=F32).astype(BF)
        gp = lax.dot_general(g, v, NT, preferred_element_type=F32)
        gs = (probs * (gp - jnp.sum(probs * gp, axis=-1, keepdims=True))).astype(BF)
        gq_v[:, cols] = (jnp.dot(gs, k, preferred_element_type=F32) * inv_root).astype(BF)
        gk = lax.dot_general(gs, q, TN, preferred_element_type=F32) * inv_root
        gv = lax.dot_general(probs_b, g, TN, preferred_element_type=F32)
        gkv_v[h, :, :HD] = gk.astype(BF)
        gkv_v[h, :, HD:] = gv.astype(BF)

    s.send(attn_v, attn_out, None)
    s.send(gq_v, gq_out, None)
    s.send(gkv_v, gkv_out, None)
    s.finish()


FRONT_COPIES = 76


def front(*ins):
    anys, vmem = pl.BlockSpec(memory_space=pl.ANY), pl.BlockSpec(memory_space=pltpu.VMEM)
    shapes = [(512, 1024), (1024, 2048), (2, 8, 32, 4096), (512, 512), (512, 512), (4, LCAP, 256)]
    scratch = [
        (128, 4096), (128, 4096), (256, 2048), (512, 4096), (32, 4096), (4096, 768), (384, 4096),
        (4096, 256), (1024, 2048), (512, 1024), (512, 512), None, (512, 384),
        (256, 4096), (256, 4096), (256, 4096), (8, 32, 4096), (3, 512, 512), (4, 512, 512),
        (512, 512), (2, 8, 32, 4096), (2, LCAP, 256), (2, LCAP, 256), (4, LCAP, 256),
        (512, 512), (512, 512), (4, LCAP, 256),
    ]
    return pl.pallas_call(
        front_kernel,
        out_shape=[jax.ShapeDtypeStruct(shape, BF) for shape in shapes],
        in_specs=[anys] * 9 + [vmem] * 4,
        out_specs=[anys] * 6,
        scratch_shapes=[
            pltpu.VMEM((512, 768), F32) if shape is None else pltpu.VMEM(shape, BF)
            for shape in scratch
        ]
        + [pltpu.SemaphoreType.DMA((FRONT_COPIES,))] * 2,
        compiler_params=pltpu.CompilerParams(
            collective_id=0, has_side_effects=True, vmem_limit_bytes=62 * 2**20
        ),
        name="front",
    )(*ins)


def core_body(s, place, ins, outs):
    c = place[4]
    s.send(ins[0].at[1 - c], outs[0], core_peer(*place)[0][0])


def attn_back_body(s, place, ins, outs):
    attn, gkv = ins
    tok, parts = outs
    y, zh, zl, x, c = place
    here = zl * 2 + c
    for to, q in quad_peers(*place) + [(None, here)]:
        s.send(gkv.at[q], parts.at[here], to)
    for to, v in x_peers(*place) + [(None, x)]:
        for half in (0, 1):
            s.send(
                attn.at[span(v, 128), pl.ds(half * 256, 256)],
                tok.at[:, span(half * 4 + x, 256)],
                to,
            )


def gather_body(s, place, ins, outs):
    gq, kvp = ins
    gqa, kvr = outs
    y, zh, zl, x, c = place
    here = y * 2 + zh
    for to, v in x_peers(*place) + [(None, x)]:
        s.send(gq, gqa.at[:, span(x, 512)], to)
    for to, j in dp_peers(*place) + [(None, here)]:
        s.send(kvp.at[j], kvr.at[here], to)


def grads_body(s, place, ins, outs):
    dxn, part, kvs = ins
    dtok, r1, r2, kva = outs
    y, zh, zl, x, c = place
    z = zh * 2 + zl
    here = y * 2 + zh
    for to, v in y_peers(*place) + [(None, y)]:
        s.send(part.at[:, v, :, :, pl.ds(0, 1024)], r1.at[y], to)
    for to, t in z_peers(*place) + [(None, z)]:
        s.send(part.at[t % 2, :, t // 2, :, pl.ds(1024, 1024)], r2.at[z], to)
    for to, v in x_peers(*place) + [(None, x)]:
        for half in (0, 1):
            s.send(
                dxn.at[span(v, 128), pl.ds(half * 512, 512)],
                dtok.at[:, span(half * 4 + x, 512)],
                to,
            )
    for to, j in dp_peers(*place) + [(None, here)]:
        s.send(kvs, kva.at[here], to)


def second_body(s, place, ins, outs):
    s1, s2 = ins
    r1, r2 = outs
    y, zh, zl, x, c = place
    z = zh * 2 + zl
    for to, t in z_peers(*place) + [(None, z)]:
        s.send(s1.at[t % 2, t // 2], r1.at[z], to)
    for to, v in y_peers(*place) + [(None, y)]:
        s.send(s2.at[v], r2.at[y], to)


def last_body(s, place, ins, outs):
    y, zh, zl, x, c = place
    here = y * 2 + zh
    for to, j in dp_peers(*place) + [(None, here)]:
        s.send(ins[0], outs[0].at[here], to)


def local(
    cap_hidden,
    t5_norm_gain,
    t5_wi0,
    t5_wi1,
    t5_wo,
    t5_final_gain,
    cap_lengths,
    latents,
    w_query,
    w_key,
    w_value,
    caption_of_image,
    grad_out,
):
    y, zh, zl, x, c = coords()

    lat = latents.astype(F32)
    removed = lat - jnp.mean(lat, axis=-1, keepdims=True)
    rstd = lax.rsqrt(jnp.mean(removed * removed, axis=-1, keepdims=True) + 1e-06)
    xhat = removed * rstd
    pick = jnp.where(caption_of_image == 0, 1.0, 0.0).astype(F32)
    pick = jnp.broadcast_to(pick[:, None, None], (2, 8, 256))
    mine = lax.dynamic_index_in_dim(caption_of_image, zl, 0)
    length = jnp.where(mine == 0, cap_lengths[:1], cap_lengths[1:])
    live = (jnp.arange(LCAP, dtype=jnp.int32) < length).astype(F32)
    live = jnp.broadcast_to(live[None], (8, LCAP))
    xs, wx, caption, attn, gq, gkv = front(
        latents,
        grad_out,
        w_query,
        cap_hidden,
        t5_wi0,
        t5_wi1,
        t5_wo,
        w_key,
        w_value,
        jnp.broadcast_to(t5_norm_gain[None], (8, 4096)).astype(F32),
        jnp.broadcast_to(t5_final_gain[None], (8, 4096)).astype(F32),
        pick,
        live,
    )
    caption = caption.reshape(512, 4096)

    attn_tok, gkv_parts = exchange(
        "attn_to_tokens",
        5,
        12,
        attn_back_body,
        (x_peers, quad_peers),
        [(128, 2048), (4, LCAP, 256)],
        attn,
        gkv,
    )
    attn_out = attn_tok.astype(F32)
    per_image = jnp.sum(gkv_parts.reshape(2, 2, LCAP, 256).astype(F32), axis=1)
    grad_kv = jnp.stack(
        [
            jnp.sum(jnp.where(caption_of_image[:, None, None] == i, per_image, 0.0), axis=0)
            for i in (0, 1)
        ]
    )
    grad_kv = grad_kv.astype(BF).reshape(512, 256)
    kv_part = lax.dot_general(
        caption, grad_kv, (((0,), (0,)), ((), ())), preferred_element_type=F32
    ).astype(BF)

    gq_all, kv_blocks = exchange(
        "grad_query_gather",
        6,
        12,
        gather_body,
        (x_peers, dp_peers),
        [(512, 2048), (8, 512, 256)],
        gq,
        kv_part.reshape(8, 512, 256),
    )
    kv_sum = jnp.sum(kv_blocks.astype(F32), axis=0).astype(BF)
    dxn = lax.dot_general(
        gq_all, wx, (((1,), (1,)), ((), ())), preferred_element_type=F32
    ).astype(BF)
    q_grad = lax.dot_general(
        xs, gq_all, (((0,), (0,)), ((), ())), preferred_element_type=F32
    ).astype(BF)
    q_grad = q_grad.reshape(2, 2, 256, 2048).transpose(1, 0, 2, 3)
    (other,) = exchange(
        "grad_query_core_pair", 7, 1, core_body, (core_peer,), [(2, 256, 2048)], q_grad
    )
    own = lax.dynamic_index_in_dim(q_grad, c, 0, keepdims=False)
    pair = (own.astype(F32) + other.astype(F32)).astype(BF).reshape(2, 4, 2, 32, 2048)

    dtok, r1, r2, kv_all = exchange(
        "grads_scatter",
        8,
        24,
        grads_body,
        (x_peers, y_peers, z_peers, dp_peers),
        [(128, 4096), (4, 2, 2, 32, 1024), (4, 4, 32, 1024), (8, 512, 256)],
        dxn,
        pair,
        kv_sum,
    )
    s1 = jnp.sum(r1.astype(F32), axis=0).astype(BF)
    s2 = jnp.sum(r2.astype(F32), axis=0).astype(BF)
    t1, t2 = exchange(
        "grad_query_scatter",
        9,
        8,
        second_body,
        (y_peers, z_peers),
        [(4, 32, 1024), (4, 32, 1024)],
        s1,
        s2,
    )
    block = jnp.concatenate(
        [jnp.sum(t1.astype(F32), axis=0), jnp.sum(t2.astype(F32), axis=0)], axis=1
    ).astype(BF)
    (q_full,) = exchange(
        "grad_query_spread", 10, 8, last_body, (dp_peers,), [(8, 32, 2048)], block
    )

    grad_xn = dtok.astype(F32)
    latent_token_gradient = rstd * (
        grad_xn
        - jnp.mean(grad_xn, axis=-1, keepdims=True)
        - xhat * jnp.mean(grad_xn * xhat, axis=-1, keepdims=True)
    )
    grad_query = (
        q_full.reshape(256, 4, 2, 256).transpose(0, 2, 1, 3).reshape(256, 2048).astype(F32)
    )
    kv_all = kv_all.reshape(4096, 256).astype(F32)
    return (attn_out, latent_token_gradient, grad_query, kv_all[:, :128], kv_all[:, 128:])


def solution(mesh):
    placed = (
        P("dp", None),
        P(),
        P(None, "fsdp"),
        P(None, "fsdp"),
        P("fsdp", None),
        P(),
        P("dp"),
        P(("dp", "fsdp"), None),
        P("fsdp", None),
        P(None, "fsdp"),
        P(None, "fsdp"),
        P("dp"),
        P(("dp", "fsdp"), None),
    )
    return jax.shard_map(
        local,
        mesh=mesh,
        in_specs=placed,
        out_specs=(
            P(("dp", "fsdp"), None),
            P(("dp", "fsdp"), None),
            P("fsdp", None),
            P(None, "fsdp"),
            P(None, "fsdp"),
        ),
        check_vma=False,
    )
```

```python
import functools
import math

import jax
import jax.numpy as jnp
from jax import lax
from jax.experimental import pallas as pl
from jax.experimental.pallas import tpu as pltpu
from jax.sharding import PartitionSpec as P

HD = 128
LCAP = 256
BF = jnp.bfloat16
F32 = jnp.float32
MESH = pl.DeviceIdType.MESH


def coords():
    d, f = lax.axis_index("dp"), lax.axis_index("fsdp")
    return d // 2, d % 2, f // 8, (f // 2) % 4, f % 2


def device(y, zh, zl, x, c):
    return (y * 2 + zh, zl * 8 + x * 2 + c)


def x_peers(y, zh, zl, x, c):
    return [(device(y, zh, zl, (x + k) % 4, c), (x + k) % 4) for k in (1, 2, 3)]


def y_peers(y, zh, zl, x, c):
    return [(device((y + k) % 4, zh, zl, x, c), (y + k) % 4) for k in (1, 2, 3)]


def z_peers(y, zh, zl, x, c):
    z = zh * 2 + zl
    there = [(z + k) % 4 for k in (1, 2, 3)]
    return [(device(y, t // 2, t % 2, x, c), t) for t in there]


def dp_peers(y, zh, zl, x, c):
    there = [((y + k) % 4, (zh + a) % 2) for a in (0, 1) for k in range(4) if a or k]
    return [(device(v, w, zl, x, c), v * 2 + w) for v, w in there]


def chip_peers(y, zh, zl, x, c):
    there = [((zl + a) % 2, (x + k) % 4) for a in (0, 1) for k in range(4) if a or k]
    return [(device(y, zh, w, v, c), w * 4 + v) for w, v in there]


def quad_peers(y, zh, zl, x, c):
    there = [((zl + a) % 2, (c + b) % 2) for a in (0, 1) for b in (0, 1) if a or b]
    return [(device(y, zh, w, x, b), w * 2 + b) for w, b in there]


def core_peer(y, zh, zl, x, c):
    return [(device(y, zh, zl, x, 1 - c), 1 - c)]


def span(index, size):
    return pl.ds(pl.multiple_of(index * size, size), size)


class Sender:
    def __init__(self, send_sem, recv_sem):
        self.sems, self.count, self.open = (send_sem, recv_sem), 0, []

    def send(self, src, dst, to):
        t = self.count
        self.count += 1
        if to is None:
            copy = pltpu.make_async_copy(src, dst, self.sems[0].at[t])
        else:
            copy = pltpu.make_async_remote_copy(
                src_ref=src,
                dst_ref=dst,
                send_sem=self.sems[0].at[t],
                recv_sem=self.sems[1].at[t],
                device_id=to,
                device_id_type=MESH,
            )
        copy.start()
        entry = [copy, to is None, False]
        self.open.append(entry)
        return entry

    def landed(self, entry):
        copy, own, seen = entry
        if not seen:
            copy.wait() if own else copy.wait_recv()
            entry[2] = True

    done = landed

    def finish(self):
        for copy, own, seen in self.open:
            if own and not seen:
                copy.wait()
            elif not own and seen:
                copy.wait_send()
            elif not own:
                copy.wait()


NT = (((1,), (1,)), ((), ()))
TN = (((0,), (0,)), ((), ()))


def kernel(
    lat, go, wq, ch, wi0, wi1, wo, wk, wv, gain, gain2, flags,
    attn_out, dxn_out, gq_out, gkv_out,
    lat_v, xn_v, wp_v, ch_v, row_v, wi_v, wo_v, wkv_v, wx_v, xs_v, gs_v, gl_v, hid_v,
    give_v, keep_v, rc_v, fr_v, qs_v, qr_v, q_v, cap_v, kv_v, sel_v, kvr_v,
    attn_v, gq_v, gkv_v, gkvr_v, gkvs_v, kvp_v, gqa_v, grc_v, r1_v, r2_v, s1_v, s2_v, t1_v, t2_v,
    fin_v, kvs_v, sems_a, sems_b,
):
    place = coords()
    y, zh, zl, x, c = place
    pair = core_peer(*place)[0][0]
    across = device(y, zh, 1 - zl, x, c)
    here, mine = zl * 4 + x, zl * 2 + c
    xp = x_peers(*place)
    chips = []
    for a in (0, 1):
        for k in (1, 3, 2, 0):
            if a or k:
                chips.append(
                    (
                        device(y, zh, (zl + a) % 2, (x + k) % 4, c),
                        ((zl + a) % 2) * 4 + (x + k) % 4,
                        ((zl + a) % 2) * 4 + (x + 4 - k) % 4,
                    )
                )
    s = Sender(sems_a, sems_b)

    perm = [
        s.send(wq.at[:, pl.ds(h * 1024 + v * 256, 256)], wp_v.at[:, pl.ds(v * 512 + h * 256, 256)], None)
        for h in (0, 1)
        for v in range(4)
    ]
    lat_in = s.send(lat, lat_v, None)
    ch_in = [s.send(ch.at[pl.ds(i * 128, 128)], ch_v.at[i], None) for i in range(4)]
    wi_in = [
        s.send(wi0, wi_v.at[:, pl.ds(0, 384)], None),
        s.send(wi1, wi_v.at[:, pl.ds(384, 384)], None),
    ]
    wo_in = s.send(wo, wo_v, None)
    wkv_in = [
        s.send(wk, wkv_v.at[:, pl.ds(0, 128)], None),
        s.send(wv, wkv_v.at[:, pl.ds(128, 128)], None),
    ]
    barrier = pltpu.get_barrier_semaphore()
    peers = [to for group in GROUPS for to, _ in group(*place)]
    for to in peers:
        pl.semaphore_signal(barrier, inc=1, device_id=to, device_id_type=MESH)
    pl.semaphore_wait(barrier, len(peers))

    for copy in perm:
        s.done(copy)
    w_over = s.send(wp_v, wx_v.at[span(mine, 256)], across)
    w_pair = s.send(wp_v, wx_v.at[span(mine, 256)], pair)
    w_own = s.send(wp_v, wx_v.at[span(mine, 256)], None)

    s.done(lat_in)

    @pl.loop(0, 8)
    def _(i):
        rows = pl.ds(pl.multiple_of(i * 16, 16), 16)
        v = lat_v[rows, :].astype(F32)
        r = v - jnp.mean(v, axis=-1, keepdims=True)
        xn_v[rows, :] = (r * lax.rsqrt(jnp.mean(r * r, axis=-1, keepdims=True) + 1e-06)).astype(BF)

    x_in, g_in = [], []
    for to, v in xp + [(None, x)]:
        for half in (0, 1):
            x_in.append(
                s.send(
                    xn_v.at[:, span(half * 4 + v, 512)],
                    xs_v.at[span(x, 128), pl.ds(half * 512, 512)],
                    to,
                )
            )
    for to, v in xp + [(None, x)]:
        for half in (0, 1):
            g_in.append(
                s.send(
                    go.at[:, span(half * 4 + v, 256)],
                    gs_v.at[span(x, 128), pl.ds(half * 256, 256)],
                    to,
                )
            )

    for copy in ch_in:
        s.done(copy)
    row_v[...] = ch_v[c * 2 + here // 4, span(here % 4, 32), :]

    @pl.loop(0, 32)
    def _(i):
        rows = pl.ds(pl.multiple_of((i % 8) * 16, 16), 16)
        v = ch_v[i // 8, rows, :].astype(F32)
        v = v * lax.rsqrt(jnp.mean(v * v, axis=-1, keepdims=True) + 1e-06) * gain[...].astype(F32)
        ch_v[i // 8, rows, :] = v.astype(BF)

    for copy in wi_in:
        s.done(copy)

    @pl.loop(0, 6)
    def _(i):
        rows = pl.ds(pl.multiple_of((i // 3) * 256, 256), 256)
        cols = pl.ds(pl.multiple_of((i % 3) * 256, 256), 256)
        normed = ch_v[pl.ds((i // 3) * 2, 2)].reshape(256, 4096)
        gl_v[rows, cols] = jnp.dot(normed, wi_v[:, cols], preferred_element_type=F32)

    @pl.loop(0, 8)
    def _(i):
        rows = pl.ds(pl.multiple_of(i * 64, 64), 64)
        g, u = gl_v[rows, :384], gl_v[rows, 384:]
        hid_v[rows, :] = (jax.nn.gelu(g, approximate=True) * u).astype(BF)

    s.done(wo_in)

    def term(which, out):
        rows = span(which, 256)

        @pl.loop(0, 8)
        def _(i):
            cols = pl.ds(pl.multiple_of(i * 512, 512), 512)
            out[:, cols] = jnp.dot(
                hid_v[rows, :], wo_v[:, cols], preferred_element_type=F32
            ).astype(BF)

    term(1 - c, give_v)
    ff_pair = s.send(give_v, rc_v, pair)
    term(c, keep_v)
    s.landed(ff_pair)

    @pl.loop(0, 16)
    def _(i):
        rows = pl.ds(pl.multiple_of(i * 16, 16), 16)
        keep_v[rows, :] = (keep_v[rows, :].astype(F32) + rc_v[rows, :].astype(F32)).astype(BF)

    ff_in = [s.send(keep_v.at[span(j, 32)], fr_v.at[here], to) for to, j, _ in chips]
    fr_v[here] = keep_v[span(here, 32), :]

    s.landed(w_over)
    theirs = (1 - zl) * 2 + c
    w_far = s.send(wx_v.at[span(theirs, 256)], wx_v.at[span(theirs, 256)], pair)
    for copy in x_in + [w_pair, w_own, w_far]:
        s.landed(copy)

    def query_block(v, out, at):
        @pl.loop(0, 4)
        def _(i):
            rows = pl.ds(pl.multiple_of((i // 2) * 256, 256), 256)
            cols = pl.ds(pl.multiple_of((i % 2) * 256, 256), 256)
            from_cols = pl.ds(pl.multiple_of(v * 512 + (i % 2) * 256, 256), 256)
            out[at, rows, cols] = jnp.dot(
                xs_v[rows, :], wx_v[:, from_cols], preferred_element_type=F32
            ).astype(BF)

    q_in = []
    for k, (to, v) in enumerate(xp):
        query_block(v, qs_v, k)
        q_in.append(s.send(qs_v.at[k], qr_v.at[x], to))
    query_block(x, qr_v, x)

    for copy in ff_in:
        s.landed(copy)
    ff = fr_v[0].astype(F32)
    for j in range(1, 8):
        ff = ff + fr_v[j].astype(F32)
    r = row_v[...].astype(F32) + ff
    r = r * lax.rsqrt(jnp.mean(r * r, axis=-1, keepdims=True) + 1e-06) * gain2[...].astype(F32)
    cap_v[c, here] = r.astype(BF)
    own = cap_v.at[c, here]
    cap_in = [(s.send(own, own, to), j) for to, _, j in chips]
    cap_pair = [s.send(own, own, pair)]

    for copy in q_in:
        s.landed(copy)

    @pl.loop(0, 8)
    def _(i):
        rows = pl.ds(pl.multiple_of(i * 64, 64), 64)
        q = qr_v[0, rows, :].astype(F32) + qr_v[1, rows, :].astype(F32)
        q = q + qr_v[2, rows, :].astype(F32) + qr_v[3, rows, :].astype(F32)
        q_v[rows, :] = q.astype(BF)

    for copy, j in cap_in:
        s.landed(copy)
        block = cap_v.at[c, j]
        cap_pair.append(s.send(block, block, pair))
    for copy in wkv_in:
        s.done(copy)

    def key_value(which):
        rows = cap_v[which].reshape(256, 4096)
        kv_v[which] = jnp.dot(rows, wkv_v[...], preferred_element_type=F32).astype(BF)

    key_value(c)
    for copy in cap_pair:
        s.landed(copy)
    key_value(1 - c)
    for i in (0, 1):
        p = flags[i : i + 1, :]
        both = kv_v[0].astype(F32) * p + kv_v[1].astype(F32) * (1.0 - p)
        sel_v[i] = both.astype(BF)
    kv_in = [s.send(sel_v.at[q // 2], kvr_v.at[mine], to) for to, q in quad_peers(*place)]
    kvr_v[mine] = sel_v[zl]
    for copy in g_in + kv_in:
        s.landed(copy)

    inv_root = 1.0 / math.sqrt(HD)

    @pl.loop(0, 4)
    def _(h):
        cols = pl.ds(pl.multiple_of(h * HD, HD), HD)
        q, g = q_v[:, cols], gs_v[:, cols]
        k, v = kvr_v[h, :, :HD], kvr_v[h, :, HD:]
        scores = lax.dot_general(q, k, NT, preferred_element_type=F32) * inv_root
        scores = jnp.where(flags[2:3, :] > 0.5, scores, -1e30)
        e = jnp.exp(scores - jnp.max(scores, axis=-1, keepdims=True))
        probs = e / jnp.sum(e, axis=-1, keepdims=True)
        probs_b = probs.astype(BF)
        attn_v[:, cols] = jnp.dot(probs_b, v, preferred_element_type=F32).astype(BF)
        gp = lax.dot_general(g, v, NT, preferred_element_type=F32)
        gs = (probs * (gp - jnp.sum(probs * gp, axis=-1, keepdims=True))).astype(BF)
        gq_v[:, cols] = (jnp.dot(gs, k, preferred_element_type=F32) * inv_root).astype(BF)
        gk = lax.dot_general(gs, q, TN, preferred_element_type=F32) * inv_root
        gv = lax.dot_general(probs_b, g, TN, preferred_element_type=F32)
        gkv_v[h, :, :HD] = gk.astype(BF)
        gkv_v[h, :, HD:] = gv.astype(BF)

    gq_in = [s.send(gq_v, gqa_v.at[:, span(x, 512)], to) for to, _ in xp]
    gq_in.append(s.send(gq_v, gqa_v.at[:, span(x, 512)], None))
    gkv_in = [
        s.send(gkv_v.at[q], gkvr_v.at[mine], to) for to, q in quad_peers(*place)
    ]
    gkvr_v[mine] = gkv_v[mine]
    for to, v in xp + [(None, x)]:
        for half in (0, 1):
            s.send(
                attn_v.at[span(v, 128), pl.ds(half * 256, 256)],
                attn_out.at[:, span(half * 4 + x, 256)],
                to,
            )
    for copy in gkv_in:
        s.landed(copy)
    im0 = gkvr_v[0].astype(F32) + gkvr_v[1].astype(F32)
    im1 = gkvr_v[2].astype(F32) + gkvr_v[3].astype(F32)
    p0, p1 = flags[0:1, :], flags[1:2, :]
    gkvs_v[:LCAP, :] = (im0 * p0 + im1 * p1).astype(BF)
    gkvs_v[LCAP:, :] = (im0 * (1.0 - p0) + im1 * (1.0 - p1)).astype(BF)

    def kv_block(j):
        cols = span(j, 512)
        rows = cap_v[:, :, :, cols].reshape(512, 512)
        kvp_v[j] = lax.dot_general(rows, gkvs_v[...], TN, preferred_element_type=F32).astype(BF)

    kv_sum_in = []
    here_dp = y * 2 + zh
    for k, (to, j) in enumerate(dp_peers(*place)):
        kv_block(j)
        kv_sum_in.append(s.send(kvp_v.at[j], kvs_v.at[k], to))
    kv_block(here_dp)

    for copy in gq_in:
        s.landed(copy)

    def q_grad(which, at):
        @pl.loop(0, 8)
        def _(i):
            f = i // 4
            cols = pl.ds(pl.multiple_of((i % 4) * 512, 512), 512)
            to_cols = pl.ds(pl.multiple_of(at + (i % 4) * 512, 512), 512)
            from_rows = pl.ds(pl.multiple_of(f * 512 + which * 256, 256), 256)
            part = lax.dot_general(
                xs_v[:, from_rows], gqa_v[:, cols], TN, preferred_element_type=F32
            ).astype(BF)
            ch_v[f * 2, :, to_cols] = part[:128]
            ch_v[f * 2 + 1, :, to_cols] = part[128:]

    q_grad(1 - c, 0)
    qg_pair = s.send(ch_v.at[:, :, pl.ds(0, 2048)], grc_v, pair)
    q_grad(c, 2048)

    @pl.loop(0, 4)
    def _(i):
        rows = pl.ds(pl.multiple_of(i * 256, 256), 256)
        part = lax.dot_general(
            gqa_v[...], wx_v[rows, :], NT, preferred_element_type=F32
        ).astype(BF)
        for v in range(4):
            lat_v[:, pl.ds(pl.multiple_of(v * 1024 + i * 256, 256), 256)] = part[
                v * 128 : (v + 1) * 128
            ]

    for to, v in xp + [(None, x)]:
        for half in (0, 1):
            s.send(
                lat_v.at[:, span(v * 2 + half, 512)],
                dxn_out.at[:, span(half * 4 + x, 512)],
                to,
            )
    s.landed(qg_pair)

    @pl.loop(0, 32)
    def _(i):
        rows = pl.ds(pl.multiple_of((i % 8) * 16, 16), 16)
        keep = ch_v[i // 8, rows, 2048:].astype(F32) + grc_v[i // 8, rows, :].astype(F32)
        ch_v[i // 8, rows, 2048:] = keep.astype(BF)

    yp, zp = y_peers(*place), z_peers(*place)
    r1_in = [
        s.send(ch_v.at[:, span(v, 32), pl.ds(2048, 1024)], r1_v.at[k], to)
        for k, (to, v) in enumerate(yp)
    ]
    r2_in = [
        s.send(ch_v.at[(t % 2) * 2 + t // 2, :, pl.ds(3072, 1024)], r2_v.at[k], to)
        for k, (to, t) in enumerate(zp)
    ]

    for copy in kv_sum_in:
        s.landed(copy)

    @pl.loop(0, 8)
    def _(i):
        rows = pl.ds(pl.multiple_of(i * 64, 64), 64)
        total = kvp_v[here_dp, rows, :].astype(F32)
        for k in range(7):
            total = total + kvs_v[k, rows, :].astype(F32)
        kvp_v[here_dp, rows, :] = total.astype(BF)

    for to, _ in dp_peers(*place) + [(None, 0)]:
        s.send(kvp_v.at[here_dp], gkv_out.at[here_dp], to)

    for copy in r1_in + r2_in:
        s.landed(copy)
    for i in range(4):
        total = ch_v[i, span(y, 32), 2048:3072].astype(F32)
        for k in range(3):
            total = total + r1_v[k, i].astype(F32)
        s1_v[i] = total.astype(BF)
    at = zl * 2 + zh
    for i in range(4):
        rows = pl.ds(i * 32, 32)
        total = ch_v[at, rows, 3072:].astype(F32)
        for k in range(3):
            total = total + r2_v[k, rows, :].astype(F32)
        s2_v[i] = total.astype(BF)
    t_in = [
        s.send(s1_v.at[(t % 2) * 2 + t // 2], t1_v.at[k], to) for k, (to, t) in enumerate(zp)
    ]
    t_in += [s.send(s2_v.at[v], t2_v.at[k], to) for k, (to, v) in enumerate(yp)]
    for copy in t_in:
        s.landed(copy)
    left, right = s1_v[at].astype(F32), s2_v[y].astype(F32)
    for k in range(3):
        left = left + t1_v[k].astype(F32)
        right = right + t2_v[k].astype(F32)
    fin_v[:, :1024] = left.astype(BF)
    fin_v[:, 1024:] = right.astype(BF)
    for to, _ in dp_peers(*place) + [(None, 0)]:
        s.send(fin_v, gq_out.at[zh * 4 + y], to)
    s.finish()


GROUPS = (chip_peers, quad_peers, dp_peers, z_peers)
COPIES = 150


def main(*ins):
    anys, vmem = pl.BlockSpec(memory_space=pl.ANY), pl.BlockSpec(memory_space=pltpu.VMEM)
    shapes = [(128, 2048), (128, 4096), (8, 32, 2048), (8, 512, 256)]
    scratch = [
        (128, 4096), (128, 4096), (256, 2048), (4, 128, 4096), (32, 4096), (4096, 768), (384, 4096),
        (4096, 256), (1024, 2048), (512, 1024), (512, 512), None, (512, 384),
        (256, 4096), (256, 4096), (256, 4096), (8, 32, 4096), (3, 512, 512), (4, 512, 512),
        (512, 512), (2, 8, 32, 4096), (2, LCAP, 256), (2, LCAP, 256), (4, LCAP, 256),
        (512, 512), (512, 512), (4, LCAP, 256), (4, LCAP, 256), (512, 256), (8, 512, 256),
        (512, 2048), (4, 128, 2048), (3, 4, 32, 1024), (3, 128, 1024), (4, 32, 1024), (4, 32, 1024),
        (3, 32, 1024), (3, 32, 1024), (32, 2048), (7, 512, 256),
    ]
    return pl.pallas_call(
        kernel,
        out_shape=[jax.ShapeDtypeStruct(shape, BF) for shape in shapes],
        in_specs=[anys] * 9 + [vmem] * 3,
        out_specs=[anys] * 4,
        scratch_shapes=[
            pltpu.VMEM((512, 768), F32) if shape is None else pltpu.VMEM(shape, BF)
            for shape in scratch
        ]
        + [pltpu.SemaphoreType.DMA((COPIES,))] * 2,
        compiler_params=pltpu.CompilerParams(
            collective_id=0, has_side_effects=True, vmem_limit_bytes=63 * 2**20
        ),
        name="main",
    )(*ins)


def last_kernel(attn, dxn, lat, gq, gkv, attn_o, lat_o, gq_o, gk_o, gv_o):
    attn_o[...] = attn[...].astype(F32)
    v = lat[...].astype(F32)
    r = v - jnp.mean(v, axis=-1, keepdims=True)
    rstd = lax.rsqrt(jnp.mean(r * r, axis=-1, keepdims=True) + 1e-06)
    xhat = r * rstd
    g = dxn[...].astype(F32)
    lat_o[...] = rstd * (
        g
        - jnp.mean(g, axis=-1, keepdims=True)
        - xhat * jnp.mean(g * xhat, axis=-1, keepdims=True)
    )
    for w in range(4):
        for h in (0, 1):
            there, here = h * 1024 + w * 256, w * 512 + h * 256
            gq_o[:, there : there + 256] = gq[0, :, here : here + 256].astype(F32)
    gk_o[...] = gkv[0, :, :HD].astype(F32)
    gv_o[...] = gkv[0, :, HD:].astype(F32)


def last(attn, dxn, lat, gq, gkv):
    def rows(count, width):
        return pl.BlockSpec((count, width), lambda i: (i, 0))

    return pl.pallas_call(
        last_kernel,
        grid=(8,),
        out_shape=[
            jax.ShapeDtypeStruct(shape, F32)
            for shape in [(128, 2048), (128, 4096), (256, 2048), (4096, HD), (4096, HD)]
        ],
        in_specs=[
            rows(16, 2048),
            rows(16, 4096),
            rows(16, 4096),
            pl.BlockSpec((1, 32, 2048), lambda i: (i, 0, 0)),
            pl.BlockSpec((1, 512, 256), lambda i: (i, 0, 0)),
        ],
        out_specs=[
            rows(16, 2048),
            rows(16, 4096),
            rows(32, 2048),
            rows(512, HD),
            rows(512, HD),
        ],
        compiler_params=pltpu.CompilerParams(vmem_limit_bytes=32 * 2**20),
        name="last",
    )(attn, dxn, lat, gq, gkv)


def local(
    cap_hidden,
    t5_norm_gain,
    t5_wi0,
    t5_wi1,
    t5_wo,
    t5_final_gain,
    cap_lengths,
    latents,
    w_query,
    w_key,
    w_value,
    caption_of_image,
    grad_out,
):
    zl = lax.axis_index("fsdp") // 8
    first = (caption_of_image == 0).astype(F32)
    mine = lax.dynamic_index_in_dim(caption_of_image, zl, 0)
    length = jnp.where(mine == 0, cap_lengths[:1], cap_lengths[1:])
    live = (jnp.arange(LCAP, dtype=jnp.int32) < length).astype(F32)
    flags = jnp.concatenate([jnp.broadcast_to(first[:, None], (2, LCAP)), live[None]])
    attn, dxn, gq, gkv = main(
        latents,
        grad_out,
        w_query,
        cap_hidden,
        t5_wi0,
        t5_wi1,
        t5_wo,
        w_key,
        w_value,
        t5_norm_gain[None],
        t5_final_gain[None],
        flags,
    )
    return last(attn, dxn, latents, gq, gkv)


def solution(mesh):
    placed = (
        P("dp", None),
        P(),
        P(None, "fsdp"),
        P(None, "fsdp"),
        P("fsdp", None),
        P(),
        P("dp"),
        P(("dp", "fsdp"), None),
        P("fsdp", None),
        P(None, "fsdp"),
        P(None, "fsdp"),
        P("dp"),
        P(("dp", "fsdp"), None),
    )
    return jax.shard_map(
        local,
        mesh=mesh,
        in_specs=placed,
        out_specs=(
            P(("dp", "fsdp"), None),
            P(("dp", "fsdp"), None),
            P("fsdp", None),
            P(None, "fsdp"),
            P(None, "fsdp"),
        ),
        check_vma=False,
    )
```

```python
import functools
import math

import jax
import jax.numpy as jnp
from jax import lax
from jax.experimental import pallas as pl
from jax.experimental.pallas import tpu as pltpu
from jax.sharding import PartitionSpec as P

HD = 128
LCAP = 256
BF = jnp.bfloat16
F32 = jnp.float32
MESH = pl.DeviceIdType.MESH


def coords():
    d, f = lax.axis_index("dp"), lax.axis_index("fsdp")
    return d // 2, d % 2, f // 8, (f // 2) % 4, f % 2


def device(y, zh, zl, x, c):
    return (y * 2 + zh, zl * 8 + x * 2 + c)


def x_peers(y, zh, zl, x, c):
    return [(device(y, zh, zl, (x + k) % 4, c), (x + k) % 4) for k in (1, 2, 3)]


def y_peers(y, zh, zl, x, c):
    return [(device((y + k) % 4, zh, zl, x, c), (y + k) % 4) for k in (1, 2, 3)]


def z_peers(y, zh, zl, x, c):
    z = zh * 2 + zl
    there = [(z + k) % 4 for k in (1, 2, 3)]
    return [(device(y, t // 2, t % 2, x, c), t) for t in there]


def dp_peers(y, zh, zl, x, c):
    there = [((y + k) % 4, (zh + a) % 2) for a in (0, 1) for k in range(4) if a or k]
    return [(device(v, w, zl, x, c), v * 2 + w) for v, w in there]


def chip_peers(y, zh, zl, x, c):
    there = [((zl + a) % 2, (x + k) % 4) for a in (0, 1) for k in range(4) if a or k]
    return [(device(y, zh, w, v, c), w * 4 + v) for w, v in there]


def quad_peers(y, zh, zl, x, c):
    there = [((zl + a) % 2, (c + b) % 2) for a in (0, 1) for b in (0, 1) if a or b]
    return [(device(y, zh, w, x, b), w * 2 + b) for w, b in there]


def core_peer(y, zh, zl, x, c):
    return [(device(y, zh, zl, x, 1 - c), 1 - c)]


def span(index, size):
    return pl.ds(pl.multiple_of(index * size, size), size)


class Sender:
    def __init__(self, send_sem, recv_sem):
        self.sems, self.count, self.open = (send_sem, recv_sem), 0, []

    def send(self, src, dst, to):
        t = self.count
        self.count += 1
        if to is None:
            copy = pltpu.make_async_copy(src, dst, self.sems[0].at[t])
        else:
            copy = pltpu.make_async_remote_copy(
                src_ref=src,
                dst_ref=dst,
                send_sem=self.sems[0].at[t],
                recv_sem=self.sems[1].at[t],
                device_id=to,
                device_id_type=MESH,
            )
        copy.start()
        entry = [copy, to is None, False]
        self.open.append(entry)
        return entry

    def landed(self, entry):
        copy, own, seen = entry
        if not seen:
            copy.wait() if own else copy.wait_recv()
            entry[2] = True

    done = landed

    def finish(self):
        for copy, own, seen in self.open:
            if own and not seen:
                copy.wait()
            elif not own and seen:
                copy.wait_send()
            elif not own:
                copy.wait()


NT = (((1,), (1,)), ((), ()))
TN = (((0,), (0,)), ((), ()))


def kernel(
    lat, go, wq, ch, wi0, wi1, wo, wk, wv, gain, gain2, lengths, owner,
    attn_out, dxn_out, gq_out, gkv_out,
    lat_v, xn_v, wp_v, ch_v, row_v, wi_v, wo_v, wkv_v, wx_v, xs_v, gs_v, gl_v, hid_v,
    give_v, keep_v, rc_v, fz_v, fr_v, qs_v, qr_v, q_v, cap_v, kv_v, sel_v, kvr_v,
    attn_v, gq_v, gkv_v, gkvr_v, gkvs_v, kvp_v, gqa_v, grc_v, r1_v, r2_v, s1_v, s2_v, t1_v, t2_v,
    fin_v, kvs_v, sems_a, sems_b,
):
    place = coords()
    y, zh, zl, x, c = place
    pair = core_peer(*place)[0][0]
    across = device(y, zh, 1 - zl, x, c)
    behind = device(y, 1 - zh, 1 - zl, x, c)
    here, mine = zl * 4 + x, zl * 2 + c
    xp = x_peers(*place)
    s = Sender(sems_a, sems_b)
    one = [1.0 - jnp.minimum(owner[i], 1).astype(F32) for i in (0, 1)]
    mine_first = 1 - jnp.minimum(owner[zl], 1)
    length = lengths[0] * mine_first + lengths[1] * (1 - mine_first)

    perm = [
        s.send(wq.at[:, pl.ds(h * 1024 + v * 256, 256)], wp_v.at[:, pl.ds(v * 512 + h * 256, 256)], None)
        for h in (0, 1)
        for v in range(4)
    ]
    lat_in = s.send(lat, lat_v, None)
    ch_in = [s.send(ch.at[pl.ds(i * 128, 128)], ch_v.at[i], None) for i in range(4)]
    wi_in = [
        s.send(wi0, wi_v.at[:, pl.ds(0, 384)], None),
        s.send(wi1, wi_v.at[:, pl.ds(384, 384)], None),
    ]
    wo_in = s.send(wo, wo_v, None)
    wkv_in = [
        s.send(wk, wkv_v.at[:, pl.ds(0, 128)], None),
        s.send(wv, wkv_v.at[:, pl.ds(128, 128)], None),
    ]
    barrier = pltpu.get_barrier_semaphore()
    peers = [to for group in GROUPS for to, _ in group(*place)]
    for to in peers:
        pl.semaphore_signal(barrier, inc=1, device_id=to, device_id_type=MESH)
    pl.semaphore_wait(barrier, len(peers))

    for copy in perm:
        s.done(copy)
    w_over = [
        s.send(wp_v.at[pl.ds(i * 128, 128)], wx_v.at[span(mine * 2 + i, 128)], to)
        for i, to in enumerate((across, behind))
    ]
    w_pair = s.send(wp_v, wx_v.at[span(mine, 256)], pair)
    w_own = s.send(wp_v, wx_v.at[span(mine, 256)], None)

    s.done(lat_in)

    @pl.loop(0, 8)
    def _(i):
        rows = pl.ds(pl.multiple_of(i * 16, 16), 16)
        v = lat_v[rows, :].astype(F32)
        r = v - jnp.mean(v, axis=-1, keepdims=True)
        xn_v[rows, :] = (r * lax.rsqrt(jnp.mean(r * r, axis=-1, keepdims=True) + 1e-06)).astype(BF)

    x_in, g_in = [], []
    for to, v in xp + [(None, x)]:
        for half in (0, 1):
            x_in.append(
                s.send(
                    xn_v.at[:, span(half * 4 + v, 512)],
                    xs_v.at[span(x, 128), pl.ds(half * 512, 512)],
                    to,
                )
            )
    for to, v in xp + [(None, x)]:
        for half in (0, 1):
            g_in.append(
                s.send(
                    go.at[:, span(half * 4 + v, 256)],
                    gs_v.at[span(x, 128), pl.ds(half * 256, 256)],
                    to,
                )
            )

    for copy in ch_in:
        s.done(copy)
    row_v[...] = ch_v[c * 2 + here // 4, span(here % 4, 32), :]

    gain_row = gain[...].astype(F32).reshape(1, 4096)

    @pl.loop(0, 32)
    def _(i):
        rows = pl.ds(pl.multiple_of((i % 8) * 16, 16), 16)
        v = ch_v[i // 8, rows, :].astype(F32)
        v = v * lax.rsqrt(jnp.mean(v * v, axis=-1, keepdims=True) + 1e-06) * gain_row
        ch_v[i // 8, rows, :] = v.astype(BF)

    for copy in wi_in:
        s.done(copy)

    @pl.loop(0, 6)
    def _(i):
        rows = pl.ds(pl.multiple_of((i // 3) * 256, 256), 256)
        cols = pl.ds(pl.multiple_of((i % 3) * 256, 256), 256)
        normed = ch_v[pl.ds((i // 3) * 2, 2)].reshape(256, 4096)
        gl_v[rows, cols] = jnp.dot(normed, wi_v[:, cols], preferred_element_type=F32)

    @pl.loop(0, 8)
    def _(i):
        rows = pl.ds(pl.multiple_of(i * 64, 64), 64)
        g, u = gl_v[rows, :384], gl_v[rows, 384:]
        hid_v[rows, :] = (jax.nn.gelu(g, approximate=True) * u).astype(BF)

    s.done(wo_in)

    def term(which, out):
        rows = span(which, 256)

        @pl.loop(0, 8)
        def _(i):
            cols = pl.ds(pl.multiple_of(i * 512, 512), 512)
            out[:, cols] = jnp.dot(
                hid_v[rows, :], wo_v[:, cols], preferred_element_type=F32
            ).astype(BF)

    term(1 - c, give_v)
    ff_pair = s.send(give_v, rc_v, pair)
    term(c, keep_v)
    s.landed(ff_pair)

    def add_core(z):
        @pl.loop(0, 8)
        def _(i):
            rows = pl.ds(pl.multiple_of(z * 128 + i * 16, 16), 16)
            total = keep_v[rows, :].astype(F32) + rc_v[rows, :].astype(F32)
            keep_v[rows, :] = total.astype(BF)

    add_core(1 - zl)
    order = [1, 3, 2, 0]
    fz_in = [
        s.send(keep_v.at[span((1 - zl) * 4 + (x + k) % 4, 32)], fz_v.at[(x + k) % 4], across)
        for k in order
    ]
    add_core(zl)

    for copy in w_over:
        s.landed(copy)
    theirs = (1 - zl) * 2 + c
    w_far = s.send(wx_v.at[span(theirs, 256)], wx_v.at[span(theirs, 256)], pair)
    for copy in x_in + [w_pair, w_own, w_far]:
        s.landed(copy)

    def query_block(v, out, at):
        @pl.loop(0, 4)
        def _(i):
            rows = pl.ds(pl.multiple_of((i // 2) * 256, 256), 256)
            cols = pl.ds(pl.multiple_of((i % 2) * 256, 256), 256)
            from_cols = pl.ds(pl.multiple_of(v * 512 + (i % 2) * 256, 256), 256)
            out[at, rows, cols] = jnp.dot(
                xs_v[rows, :], wx_v[:, from_cols], preferred_element_type=F32
            ).astype(BF)

    q_in = []
    for k in (0, 2):
        query_block(xp[k][1], qs_v, k)
        q_in.append(s.send(qs_v.at[k], qr_v.at[x], xp[k][0]))

    ff_in = []

    def add_across(n):
        k = order[n]
        s.landed(fz_in[n])
        v = (x + k) % 4
        rows = span(zl * 4 + v, 32)
        total = keep_v[rows, :].astype(F32) + fz_v[v].astype(F32)
        if k:
            keep_v[rows, :] = total.astype(BF)
            ff_in.append(s.send(keep_v.at[rows], fr_v.at[k - 1], xp[k - 1][0]))
        return total

    add_across(0)
    query_block(xp[1][1], qs_v, 1)
    add_across(1)
    query_block(x, qr_v, x)
    add_across(2)
    ff = add_across(3)
    q_in.append(s.send(qs_v.at[1], qr_v.at[x], xp[1][0]))

    for copy in ff_in:
        s.landed(copy)
    for k in range(3):
        ff = ff + fr_v[k].astype(F32)
    r = row_v[...].astype(F32) + ff
    r = r * lax.rsqrt(jnp.mean(r * r, axis=-1, keepdims=True) + 1e-06) * gain2[...].astype(F32).reshape(1, 4096)
    cap_v[c, here] = r.astype(BF)
    own = cap_v.at[c, here]
    there = (1 - zl) * 4 + x

    def piece(j, half):
        return cap_v.at[c, j, pl.ds(half * 16, 16)]

    def pass_on(ref, to):
        return s.send(ref, ref, to)

    z_own = [pass_on(piece(here, half), across) for half in (0, 1)]
    x_own = [(k, pass_on(own, xp[k - 1][0])) for k in (1, 3, 2)]
    cap_pair = [pass_on(own, pair)]
    s.landed(z_own[0])
    x_far = [(k, pass_on(piece(there, 0), xp[k - 1][0])) for k in (1, 3, 2)]
    cap_pair.append(pass_on(piece(there, 0), pair))
    z_far = []
    for k, copy in x_own:
        s.landed(copy)
        j = zl * 4 + (x + 4 - k) % 4
        z_far.append((k, pass_on(piece(j, 1), across)))
        cap_pair.append(pass_on(cap_v.at[c, j], pair))
    s.landed(z_own[1])
    cap_pair.append(pass_on(piece(there, 1), pair))
    for half, group in ((0, x_far), (1, z_far)):
        for k, copy in group:
            s.landed(copy)
            cap_pair.append(pass_on(piece((1 - zl) * 4 + (x + 4 - k) % 4, half), pair))
    for copy in q_in:
        s.landed(copy)

    @pl.loop(0, 8)
    def _(i):
        rows = pl.ds(pl.multiple_of(i * 64, 64), 64)
        q = qr_v[0, rows, :].astype(F32) + qr_v[1, rows, :].astype(F32)
        q = q + qr_v[2, rows, :].astype(F32) + qr_v[3, rows, :].astype(F32)
        q_v[rows, :] = q.astype(BF)

    for copy in wkv_in:
        s.done(copy)

    def key_value(which):
        rows = cap_v[which].reshape(256, 4096)
        kv_v[which] = jnp.dot(rows, wkv_v[...], preferred_element_type=F32).astype(BF)

    key_value(c)
    for copy in cap_pair:
        s.landed(copy)
    key_value(1 - c)
    for i in (0, 1):
        p = one[i]
        both = kv_v[0].astype(F32) * p + kv_v[1].astype(F32) * (1.0 - p)
        sel_v[i] = both.astype(BF)
    kv_in = [s.send(sel_v.at[q // 2], kvr_v.at[mine], to) for to, q in quad_peers(*place)]
    kvr_v[mine] = sel_v[zl]
    for copy in g_in + kv_in:
        s.landed(copy)

    inv_root = 1.0 / math.sqrt(HD)

    @pl.loop(0, 4)
    def _(h):
        cols = pl.ds(pl.multiple_of(h * HD, HD), HD)
        q, g = q_v[:, cols], gs_v[:, cols]
        k, v = kvr_v[h, :, :HD], kvr_v[h, :, HD:]
        scores = lax.dot_general(q, k, NT, preferred_element_type=F32) * inv_root
        live = lax.broadcasted_iota(jnp.int32, scores.shape, 1) < length
        scores = jnp.where(live, scores, -1e30)
        e = jnp.exp(scores - jnp.max(scores, axis=-1, keepdims=True))
        probs = e / jnp.sum(e, axis=-1, keepdims=True)
        probs_b = probs.astype(BF)
        attn_v[:, cols] = jnp.dot(probs_b, v, preferred_element_type=F32).astype(BF)
        gp = lax.dot_general(g, v, NT, preferred_element_type=F32)
        gs = (probs * (gp - jnp.sum(probs * gp, axis=-1, keepdims=True))).astype(BF)
        gq_v[:, cols] = (jnp.dot(gs, k, preferred_element_type=F32) * inv_root).astype(BF)
        gk = lax.dot_general(gs, q, TN, preferred_element_type=F32) * inv_root
        gv = lax.dot_general(probs_b, g, TN, preferred_element_type=F32)
        gkv_v[h, :, :HD] = gk.astype(BF)
        gkv_v[h, :, HD:] = gv.astype(BF)

    right, left = xp[0][0], xp[2][0]

    def part(who, half):
        return gqa_v.at[pl.ds(half * 256, 256), span(who, 512)]

    def own_part(half):
        return gq_v.at[pl.ds(half * 256, 256)]

    to_right = [s.send(own_part(h), part(x, h), right) for h in (0, 1)]
    to_left = [s.send(own_part(h), part(x, h), left) for h in (1, 0)]
    gq_in = [s.send(gq_v, gqa_v.at[:, span(x, 512)], None), to_right[1], to_left[1]]
    gkv_in = [
        s.send(gkv_v.at[q], gkvr_v.at[mine], to) for to, q in quad_peers(*place)
    ]
    gkvr_v[mine] = gkv_v[mine]
    for copy in gkv_in:
        s.landed(copy)
    im0 = gkvr_v[0].astype(F32) + gkvr_v[1].astype(F32)
    im1 = gkvr_v[2].astype(F32) + gkvr_v[3].astype(F32)
    p0, p1 = one
    gkvs_v[:LCAP, :] = (im0 * p0 + im1 * p1).astype(BF)
    gkvs_v[LCAP:, :] = (im0 * (1.0 - p0) + im1 * (1.0 - p1)).astype(BF)

    def kv_block(j):
        cols = span(j, 512)
        rows = cap_v[:, :, :, cols].reshape(512, 512)
        kvp_v[j] = lax.dot_general(rows, gkvs_v[...], TN, preferred_element_type=F32).astype(BF)

    kv_sum_in = []
    here_dp = y * 2 + zh
    for k, (to, j) in enumerate(dp_peers(*place)):
        kv_block(j)
        kv_sum_in.append(s.send(kvp_v.at[j], kvs_v.at[k], to))
    kv_block(here_dp)

    s.landed(to_right[0])
    gq_in.append(s.send(part((x + 3) % 4, 0), part((x + 3) % 4, 0), right))
    s.landed(to_left[0])
    gq_in.append(s.send(part((x + 1) % 4, 1), part((x + 1) % 4, 1), left))
    for to, v in xp + [(None, x)]:
        for half in (0, 1):
            s.send(
                attn_v.at[span(v, 128), pl.ds(half * 256, 256)],
                attn_out.at[:, span(half * 4 + x, 256)],
                to,
            )

    for copy in gq_in:
        s.landed(copy)

    def q_grad(which, at):
        @pl.loop(0, 8)
        def _(i):
            f = i // 4
            cols = pl.ds(pl.multiple_of((i % 4) * 512, 512), 512)
            to_cols = pl.ds(pl.multiple_of(at + (i % 4) * 512, 512), 512)
            from_rows = pl.ds(pl.multiple_of(f * 512 + which * 256, 256), 256)
            part = lax.dot_general(
                xs_v[:, from_rows], gqa_v[:, cols], TN, preferred_element_type=F32
            ).astype(BF)
            ch_v[f * 2, :, to_cols] = part[:128]
            ch_v[f * 2 + 1, :, to_cols] = part[128:]

    q_grad(1 - c, 0)
    qg_pair = s.send(ch_v.at[:, :, pl.ds(0, 2048)], grc_v, pair)
    q_grad(c, 2048)

    @pl.loop(0, 4)
    def _(i):
        rows = pl.ds(pl.multiple_of(i * 256, 256), 256)
        part = lax.dot_general(
            gqa_v[...], wx_v[rows, :], NT, preferred_element_type=F32
        ).astype(BF)
        for v in range(4):
            lat_v[:, pl.ds(pl.multiple_of(v * 1024 + i * 256, 256), 256)] = part[
                v * 128 : (v + 1) * 128
            ]

    for to, v in xp + [(None, x)]:
        for half in (0, 1):
            s.send(
                lat_v.at[:, span(v * 2 + half, 512)],
                dxn_out.at[:, span(half * 4 + x, 512)],
                to,
            )
    s.landed(qg_pair)

    @pl.loop(0, 32)
    def _(i):
        rows = pl.ds(pl.multiple_of((i % 8) * 16, 16), 16)
        keep = ch_v[i // 8, rows, 2048:].astype(F32) + grc_v[i // 8, rows, :].astype(F32)
        ch_v[i // 8, rows, 2048:] = keep.astype(BF)

    yp, zp = y_peers(*place), z_peers(*place)
    r1_in = [
        s.send(ch_v.at[:, span(v, 32), pl.ds(2048, 1024)], r1_v.at[k], to)
        for k, (to, v) in enumerate(yp)
    ]
    r2_in = [
        s.send(ch_v.at[(t % 2) * 2 + t // 2, :, pl.ds(3072, 1024)], r2_v.at[k], to)
        for k, (to, t) in enumerate(zp)
    ]

    for copy in kv_sum_in:
        s.landed(copy)

    @pl.loop(0, 8)
    def _(i):
        rows = pl.ds(pl.multiple_of(i * 64, 64), 64)
        total = kvp_v[here_dp, rows, :].astype(F32)
        for k in range(7):
            total = total + kvs_v[k, rows, :].astype(F32)
        kvp_v[here_dp, rows, :] = total.astype(BF)

    spread = [to for to, _ in dp_peers(*place)] + [None]
    for to in spread[:3]:
        s.send(kvp_v.at[here_dp], gkv_out.at[here_dp], to)

    for copy in r1_in + r2_in:
        s.landed(copy)
    for i in range(4):
        total = ch_v[i, span(y, 32), 2048:3072].astype(F32)
        for k in range(3):
            total = total + r1_v[k, i].astype(F32)
        s1_v[i] = total.astype(BF)
    at = zl * 2 + zh
    for i in range(4):
        rows = pl.ds(i * 32, 32)
        total = ch_v[at, rows, 3072:].astype(F32)
        for k in range(3):
            total = total + r2_v[k, rows, :].astype(F32)
        s2_v[i] = total.astype(BF)
    t_in = [
        s.send(s1_v.at[(t % 2) * 2 + t // 2], t1_v.at[k], to) for k, (to, t) in enumerate(zp)
    ]
    t_in += [s.send(s2_v.at[v], t2_v.at[k], to) for k, (to, v) in enumerate(yp)]
    for to in spread[3:]:
        s.send(kvp_v.at[here_dp], gkv_out.at[here_dp], to)
    for copy in t_in:
        s.landed(copy)
    left, right = s1_v[at].astype(F32), s2_v[y].astype(F32)
    for k in range(3):
        left = left + t1_v[k].astype(F32)
        right = right + t2_v[k].astype(F32)
    fin_v[:, :1024] = left.astype(BF)
    fin_v[:, 1024:] = right.astype(BF)
    for to, _ in dp_peers(*place) + [(None, 0)]:
        s.send(fin_v, gq_out.at[zh * 4 + y], to)
    s.finish()


GROUPS = (chip_peers, quad_peers, dp_peers, z_peers)
COPIES = 180


def main(*ins):
    anys, vmem = pl.BlockSpec(memory_space=pl.ANY), pl.BlockSpec(memory_space=pltpu.VMEM)
    shapes = [(128, 2048), (128, 4096), (8, 32, 2048), (8, 512, 256)]
    scratch = [
        (128, 4096), (128, 4096), (256, 2048), (4, 128, 4096), (32, 4096), (4096, 768), (384, 4096),
        (4096, 256), (1024, 2048), (512, 1024), (512, 512), None, (512, 384),
        (256, 4096), (256, 4096), (256, 4096), (4, 32, 4096), (3, 32, 4096), (3, 512, 512), (4, 512, 512),
        (512, 512), (2, 8, 32, 4096), (2, LCAP, 256), (2, LCAP, 256), (4, LCAP, 256),
        (512, 512), (512, 512), (4, LCAP, 256), (4, LCAP, 256), (512, 256), (8, 512, 256),
        (512, 2048), (4, 128, 2048), (3, 4, 32, 1024), (3, 128, 1024), (4, 32, 1024), (4, 32, 1024),
        (3, 32, 1024), (3, 32, 1024), (32, 2048), (7, 512, 256),
    ]
    return pl.pallas_call(
        kernel,
        out_shape=[jax.ShapeDtypeStruct(shape, BF) for shape in shapes],
        in_specs=[anys] * 9 + [vmem] * 2 + [pl.BlockSpec(memory_space=pltpu.SMEM)] * 2,
        out_specs=[anys] * 4,
        scratch_shapes=[
            pltpu.VMEM((512, 768), F32) if shape is None else pltpu.VMEM(shape, BF)
            for shape in scratch
        ]
        + [pltpu.SemaphoreType.DMA((COPIES,))] * 2,
        compiler_params=pltpu.CompilerParams(
            collective_id=0, has_side_effects=True, vmem_limit_bytes=63 * 2**20
        ),
        name="main",
    )(*ins)


def last_kernel(
    attn, dxn, lat, gq, gkv, attn_o, lat_o, gq_o, gk_o, gv_o,
    attn_v, dxn_v, lat_v, gq_v, gkv_v, attn_f, lat_f, gq_f, gk_f, gv_f, sems,
):
    copies = []

    def move(src, dst):
        copy = pltpu.make_async_copy(src, dst, sems.at[len(copies)])
        copy.start()
        copies.append(copy)
        return copy

    def part(i, size):
        return pl.ds(i * size, size)

    outs = []
    kv_in = [move(gkv.at[part(i, 2)], gkv_v.at[part(i, 2)]) for i in range(4)]
    lat_in = []
    for i in range(4):
        rows = part(i, 32)
        lat_in.append(
            (move(lat.at[rows], lat_v.at[rows]), move(dxn.at[rows], dxn_v.at[rows]))
        )
    gq_in = [move(gq.at[part(i, 4)], gq_v.at[part(i, 4)]) for i in (0, 1)]
    attn_in = move(attn, attn_v)
    for i in range(4):
        kv_in[i].wait()

        @pl.loop(0, 8)
        def _(n, i=i):
            at, rows = i * 2 + n // 4, pl.ds(pl.multiple_of((n % 4) * 128, 128), 128)
            to = pl.ds(pl.multiple_of(i * 1024 + n * 128, 128), 128)
            gk_f[to, :] = gkv_v[at, rows, :HD].astype(F32)
            gv_f[to, :] = gkv_v[at, rows, HD:].astype(F32)

        rows = part(i, 1024)
        outs += [move(gk_f.at[rows], gk_o.at[rows]), move(gv_f.at[rows], gv_o.at[rows])]
    for i in range(4):
        for copy in lat_in[i]:
            copy.wait()

        @pl.loop(0, 2)
        def _(n, i=i):
            rows = pl.ds(pl.multiple_of(i * 32 + n * 16, 16), 16)
            v = lat_v[rows, :].astype(F32)
            r = v - jnp.mean(v, axis=-1, keepdims=True)
            rstd = lax.rsqrt(jnp.mean(r * r, axis=-1, keepdims=True) + 1e-06)
            xhat = r * rstd
            g = dxn_v[rows, :].astype(F32)
            lat_f[rows, :] = rstd * (
                g
                - jnp.mean(g, axis=-1, keepdims=True)
                - xhat * jnp.mean(g * xhat, axis=-1, keepdims=True)
            )

        rows = part(i, 32)
        outs.append(move(lat_f.at[rows], lat_o.at[rows]))
    for i in (0, 1):
        gq_in[i].wait()

        @pl.loop(0, 4)
        def _(n, i=i):
            rows = pl.ds(pl.multiple_of((i * 4 + n) * 32, 32), 32)
            for w in range(4):
                for h in (0, 1):
                    there, here = h * 1024 + w * 256, w * 512 + h * 256
                    gq_f[rows, there : there + 256] = gq_v[i * 4 + n, :, here : here + 256].astype(
                        F32
                    )

        rows = part(i, 128)
        outs.append(move(gq_f.at[rows], gq_o.at[rows]))
    attn_in.wait()

    @pl.loop(0, 4)
    def _(n):
        rows = pl.ds(pl.multiple_of(n * 32, 32), 32)
        attn_f[rows, :] = attn_v[rows, :].astype(F32)

    outs.append(move(attn_f, attn_o))
    for copy in outs:
        copy.wait()


def last(*ins):
    anys = pl.BlockSpec(memory_space=pl.ANY)
    shapes = [(128, 2048), (128, 4096), (256, 2048), (4096, HD), (4096, HD)]
    return pl.pallas_call(
        last_kernel,
        out_shape=[jax.ShapeDtypeStruct(shape, F32) for shape in shapes],
        in_specs=[anys] * 5,
        out_specs=[anys] * 5,
        scratch_shapes=[pltpu.VMEM(a.shape, BF) for a in ins]
        + [pltpu.VMEM(shape, F32) for shape in shapes]
        + [pltpu.SemaphoreType.DMA((40,))],
        compiler_params=pltpu.CompilerParams(vmem_limit_bytes=63 * 2**20),
        name="last",
    )(*ins)


def local(
    cap_hidden,
    t5_norm_gain,
    t5_wi0,
    t5_wi1,
    t5_wo,
    t5_final_gain,
    cap_lengths,
    latents,
    w_query,
    w_key,
    w_value,
    caption_of_image,
    grad_out,
):
    attn, dxn, gq, gkv = main(
        latents,
        grad_out,
        w_query,
        cap_hidden,
        t5_wi0,
        t5_wi1,
        t5_wo,
        w_key,
        w_value,
        t5_norm_gain,
        t5_final_gain,
        cap_lengths,
        caption_of_image,
    )
    return last(attn, dxn, latents, gq, gkv)


def solution(mesh):
    placed = (
        P("dp", None),
        P(),
        P(None, "fsdp"),
        P(None, "fsdp"),
        P("fsdp", None),
        P(),
        P("dp"),
        P(("dp", "fsdp"), None),
        P("fsdp", None),
        P(None, "fsdp"),
        P(None, "fsdp"),
        P("dp"),
        P(("dp", "fsdp"), None),
    )
    return jax.shard_map(
        local,
        mesh=mesh,
        in_specs=placed,
        out_specs=(
            P(("dp", "fsdp"), None),
            P(("dp", "fsdp"), None),
            P("fsdp", None),
            P(None, "fsdp"),
            P(None, "fsdp"),
        ),
        check_vma=False,
    )
```

```python
import functools
import math

import jax
import jax.numpy as jnp
from jax import lax
from jax.experimental import pallas as pl
from jax.experimental.pallas import tpu as pltpu
from jax.sharding import PartitionSpec as P

HD = 128
LCAP = 256
BF = jnp.bfloat16
F32 = jnp.float32
MESH = pl.DeviceIdType.MESH


def coords():
    d, f = lax.axis_index("dp"), lax.axis_index("fsdp")
    return d // 2, d % 2, f // 8, (f // 2) % 4, f % 2


def device(y, zh, zl, x, c):
    return (y * 2 + zh, zl * 8 + x * 2 + c)


def x_peers(y, zh, zl, x, c):
    return [(device(y, zh, zl, (x + k) % 4, c), (x + k) % 4) for k in (1, 2, 3)]


def y_peers(y, zh, zl, x, c):
    return [(device((y + k) % 4, zh, zl, x, c), (y + k) % 4) for k in (1, 2, 3)]


def z_peers(y, zh, zl, x, c):
    z = zh * 2 + zl
    there = [(z + k) % 4 for k in (1, 2, 3)]
    return [(device(y, t // 2, t % 2, x, c), t) for t in there]


def quad_peers(y, zh, zl, x, c):
    there = [((zl + a) % 2, (c + b) % 2) for a in (0, 1) for b in (0, 1) if a or b]
    return [(device(y, zh, w, x, b), w * 2 + b) for w, b in there]


def core_peer(y, zh, zl, x, c):
    return [(device(y, zh, zl, x, 1 - c), 1 - c)]


def span(index, size):
    return pl.ds(pl.multiple_of(index * size, size), size)


class Sender:
    def __init__(self, send_sem, recv_sem):
        self.sems, self.count, self.open = (send_sem, recv_sem), 0, []

    def send(self, src, dst, to):
        t = self.count
        self.count += 1
        if to is None:
            copy = pltpu.make_async_copy(src, dst, self.sems[0].at[t])
        else:
            copy = pltpu.make_async_remote_copy(
                src_ref=src,
                dst_ref=dst,
                send_sem=self.sems[0].at[t],
                recv_sem=self.sems[1].at[t],
                device_id=to,
                device_id_type=MESH,
            )
        copy.start()
        entry = [copy, to is None, False]
        self.open.append(entry)
        return entry

    def landed(self, entry):
        copy, own, seen = entry
        if not seen:
            copy.wait() if own else copy.wait_recv()
            entry[2] = True

    done = landed

    def finish(self):
        for copy, own, seen in self.open:
            if own and not seen:
                copy.wait()
            elif not own and seen:
                copy.wait_send()
            elif not own:
                copy.wait()


NT = (((1,), (1,)), ((), ()))
TN = (((0,), (0,)), ((), ()))


def kernel(
    lat, go, wq, ch, wi0, wi1, wo, wk, wv, gain, gain2, lengths, owner,
    attn_out, dxn_out, gq_out, gkv_out,
    lat_v, xn_v, wp_v, ch_v, row_v, wi_v, wo_v, wkv_v, wx_v, xs_v, gs_v, gl_v, hid_v,
    give_v, keep_v, rc_v, fz_v, fr_v, qs_v, qr_v, q_v, cap_v, kv_v, sel_v, kvr_v,
    attn_v, gq_v, gkv_v, gkvr_v, gkvs_v, kvp_v, gqa_v, grc_v, r1_v, r2_v, s1_v, s2_v, t1_v, t2_v,
    fin_v, ka_v, kb_v, k2a_v, k2b_v, sems_a, sems_b,
):
    place = coords()
    y, zh, zl, x, c = place
    pair = core_peer(*place)[0][0]
    across = device(y, zh, 1 - zl, x, c)
    behind = device(y, 1 - zh, 1 - zl, x, c)
    here, mine = zl * 4 + x, zl * 2 + c
    xp = x_peers(*place)
    s = Sender(sems_a, sems_b)
    one = [1.0 - jnp.minimum(owner[i], 1).astype(F32) for i in (0, 1)]
    mine_first = 1 - jnp.minimum(owner[zl], 1)
    length = lengths[0] * mine_first + lengths[1] * (1 - mine_first)

    perm = [
        s.send(wq.at[:, pl.ds(h * 1024 + v * 256, 256)], wp_v.at[:, pl.ds(v * 512 + h * 256, 256)], None)
        for h in (0, 1)
        for v in range(4)
    ]
    lat_in = s.send(lat, lat_v, None)
    ch_in = [s.send(ch.at[pl.ds(i * 128, 128)], ch_v.at[i], None) for i in range(4)]
    wi_in = [
        s.send(wi0, wi_v.at[:, pl.ds(0, 384)], None),
        s.send(wi1, wi_v.at[:, pl.ds(384, 384)], None),
    ]
    wo_in = s.send(wo, wo_v, None)
    wkv_in = [
        s.send(wk, wkv_v.at[:, pl.ds(0, 128)], None),
        s.send(wv, wkv_v.at[:, pl.ds(128, 128)], None),
    ]
    barrier = pltpu.get_barrier_semaphore()
    peers = [to for group in GROUPS for to, _ in group(*place)]
    for to in peers:
        pl.semaphore_signal(barrier, inc=1, device_id=to, device_id_type=MESH)
    pl.semaphore_wait(barrier, len(peers))

    for copy in perm:
        s.done(copy)
    w_over = [
        s.send(wp_v.at[pl.ds(i * 128, 128)], wx_v.at[span(mine * 2 + i, 128)], to)
        for i, to in enumerate((across, behind))
    ]
    w_pair = s.send(wp_v, wx_v.at[span(mine, 256)], pair)
    w_own = s.send(wp_v, wx_v.at[span(mine, 256)], None)

    s.done(lat_in)

    @pl.loop(0, 8)
    def _(i):
        rows = pl.ds(pl.multiple_of(i * 16, 16), 16)
        v = lat_v[rows, :].astype(F32)
        r = v - jnp.mean(v, axis=-1, keepdims=True)
        xn_v[rows, :] = (r * lax.rsqrt(jnp.mean(r * r, axis=-1, keepdims=True) + 1e-06)).astype(BF)

    x_in, g_in = [], []
    for to, v in xp + [(None, x)]:
        for half in (0, 1):
            x_in.append(
                s.send(
                    xn_v.at[:, span(half * 4 + v, 512)],
                    xs_v.at[span(x, 128), pl.ds(half * 512, 512)],
                    to,
                )
            )
    for to, v in xp + [(None, x)]:
        for half in (0, 1):
            g_in.append(
                s.send(
                    go.at[:, span(half * 4 + v, 256)],
                    gs_v.at[span(x, 128), pl.ds(half * 256, 256)],
                    to,
                )
            )

    for copy in ch_in:
        s.done(copy)
    row_v[...] = ch_v[c * 2 + here // 4, span(here % 4, 32), :]

    gain_row = gain[...].astype(F32).reshape(1, 4096)

    @pl.loop(0, 32)
    def _(i):
        rows = pl.ds(pl.multiple_of((i % 8) * 16, 16), 16)
        v = ch_v[i // 8, rows, :].astype(F32)
        v = v * lax.rsqrt(jnp.mean(v * v, axis=-1, keepdims=True) + 1e-06) * gain_row
        ch_v[i // 8, rows, :] = v.astype(BF)

    for copy in wi_in:
        s.done(copy)

    @pl.loop(0, 6)
    def _(i):
        rows = pl.ds(pl.multiple_of((i // 3) * 256, 256), 256)
        cols = pl.ds(pl.multiple_of((i % 3) * 256, 256), 256)
        normed = ch_v[pl.ds((i // 3) * 2, 2)].reshape(256, 4096)
        gl_v[rows, cols] = jnp.dot(normed, wi_v[:, cols], preferred_element_type=F32)

    @pl.loop(0, 8)
    def _(i):
        rows = pl.ds(pl.multiple_of(i * 64, 64), 64)
        g, u = gl_v[rows, :384], gl_v[rows, 384:]
        hid_v[rows, :] = (jax.nn.gelu(g, approximate=True) * u).astype(BF)

    s.done(wo_in)

    def term(which, out):
        rows = span(which, 256)

        @pl.loop(0, 8)
        def _(i):
            cols = pl.ds(pl.multiple_of(i * 512, 512), 512)
            out[:, cols] = jnp.dot(
                hid_v[rows, :], wo_v[:, cols], preferred_element_type=F32
            ).astype(BF)

    term(1 - c, give_v)
    ff_pair = s.send(give_v, rc_v, pair)
    term(c, keep_v)
    s.landed(ff_pair)

    def add_core(z):
        @pl.loop(0, 8)
        def _(i):
            rows = pl.ds(pl.multiple_of(z * 128 + i * 16, 16), 16)
            total = keep_v[rows, :].astype(F32) + rc_v[rows, :].astype(F32)
            keep_v[rows, :] = total.astype(BF)

    add_core(1 - zl)
    order = [1, 3, 2, 0]
    fz_in = [
        s.send(keep_v.at[span((1 - zl) * 4 + (x + k) % 4, 32)], fz_v.at[(x + k) % 4], across)
        for k in order
    ]
    add_core(zl)

    for copy in w_over:
        s.landed(copy)
    theirs = (1 - zl) * 2 + c
    w_far = s.send(wx_v.at[span(theirs, 256)], wx_v.at[span(theirs, 256)], pair)
    for copy in x_in + [w_pair, w_own, w_far]:
        s.landed(copy)

    def query_block(v, out, at):
        @pl.loop(0, 4)
        def _(i):
            rows = pl.ds(pl.multiple_of((i // 2) * 256, 256), 256)
            cols = pl.ds(pl.multiple_of((i % 2) * 256, 256), 256)
            from_cols = pl.ds(pl.multiple_of(v * 512 + (i % 2) * 256, 256), 256)
            out[at, rows, cols] = jnp.dot(
                xs_v[rows, :], wx_v[:, from_cols], preferred_element_type=F32
            ).astype(BF)

    q_in = []
    for k in (0, 2):
        query_block(xp[k][1], qs_v, k)
        q_in.append(s.send(qs_v.at[k], qr_v.at[x], xp[k][0]))

    ff_in = []

    def add_across(n):
        k = order[n]
        s.landed(fz_in[n])
        v = (x + k) % 4
        rows = span(zl * 4 + v, 32)
        total = keep_v[rows, :].astype(F32) + fz_v[v].astype(F32)
        if k:
            keep_v[rows, :] = total.astype(BF)
            ff_in.append(s.send(keep_v.at[rows], fr_v.at[k - 1], xp[k - 1][0]))
        return total

    add_across(0)
    query_block(xp[1][1], qs_v, 1)
    add_across(1)
    query_block(x, qr_v, x)
    add_across(2)
    ff = add_across(3)
    q_in.append(s.send(qs_v.at[1], qr_v.at[x], xp[1][0]))

    for copy in ff_in:
        s.landed(copy)
    for k in range(3):
        ff = ff + fr_v[k].astype(F32)
    r = row_v[...].astype(F32) + ff
    r = r * lax.rsqrt(jnp.mean(r * r, axis=-1, keepdims=True) + 1e-06) * gain2[...].astype(F32).reshape(1, 4096)
    cap_v[c, here] = r.astype(BF)
    own = cap_v.at[c, here]
    there = (1 - zl) * 4 + x

    def piece(j, half):
        return cap_v.at[c, j, pl.ds(half * 16, 16)]

    def pass_on(ref, to):
        return s.send(ref, ref, to)

    z_own = [pass_on(piece(here, half), across) for half in (0, 1)]
    x_own = [(k, pass_on(own, xp[k - 1][0])) for k in (1, 3, 2)]
    cap_pair = [pass_on(own, pair)]
    s.landed(z_own[0])
    x_far = [(k, pass_on(piece(there, 0), xp[k - 1][0])) for k in (1, 3, 2)]
    cap_pair.append(pass_on(piece(there, 0), pair))
    z_far = []
    for k, copy in x_own:
        s.landed(copy)
        j = zl * 4 + (x + 4 - k) % 4
        z_far.append((k, pass_on(piece(j, 1), across)))
        cap_pair.append(pass_on(cap_v.at[c, j], pair))
    s.landed(z_own[1])
    cap_pair.append(pass_on(piece(there, 1), pair))
    for half, group in ((0, x_far), (1, z_far)):
        for k, copy in group:
            s.landed(copy)
            cap_pair.append(pass_on(piece((1 - zl) * 4 + (x + 4 - k) % 4, half), pair))
    for copy in q_in:
        s.landed(copy)

    @pl.loop(0, 8)
    def _(i):
        rows = pl.ds(pl.multiple_of(i * 64, 64), 64)
        q = qr_v[0, rows, :].astype(F32) + qr_v[1, rows, :].astype(F32)
        q = q + qr_v[2, rows, :].astype(F32) + qr_v[3, rows, :].astype(F32)
        q_v[rows, :] = q.astype(BF)

    for copy in wkv_in:
        s.done(copy)

    def key_value(which):
        rows = cap_v[which].reshape(256, 4096)
        kv_v[which] = jnp.dot(rows, wkv_v[...], preferred_element_type=F32).astype(BF)

    key_value(c)
    for copy in cap_pair:
        s.landed(copy)
    key_value(1 - c)
    for i in (0, 1):
        p = one[i]
        both = kv_v[0].astype(F32) * p + kv_v[1].astype(F32) * (1.0 - p)
        sel_v[i] = both.astype(BF)
    kv_in = [s.send(sel_v.at[q // 2], kvr_v.at[mine], to) for to, q in quad_peers(*place)]
    kvr_v[mine] = sel_v[zl]
    for copy in g_in + kv_in:
        s.landed(copy)

    inv_root = 1.0 / math.sqrt(HD)

    @pl.loop(0, 4)
    def _(h):
        cols = pl.ds(pl.multiple_of(h * HD, HD), HD)
        q, g = q_v[:, cols], gs_v[:, cols]
        k, v = kvr_v[h, :, :HD], kvr_v[h, :, HD:]
        scores = lax.dot_general(q, k, NT, preferred_element_type=F32) * inv_root
        live = lax.broadcasted_iota(jnp.int32, scores.shape, 1) < length
        scores = jnp.where(live, scores, -1e30)
        e = jnp.exp(scores - jnp.max(scores, axis=-1, keepdims=True))
        probs = e / jnp.sum(e, axis=-1, keepdims=True)
        probs_b = probs.astype(BF)
        attn_v[:, cols] = jnp.dot(probs_b, v, preferred_element_type=F32).astype(BF)
        gp = lax.dot_general(g, v, NT, preferred_element_type=F32)
        gs = (probs * (gp - jnp.sum(probs * gp, axis=-1, keepdims=True))).astype(BF)
        gq_v[:, cols] = (jnp.dot(gs, k, preferred_element_type=F32) * inv_root).astype(BF)
        gk = lax.dot_general(gs, q, TN, preferred_element_type=F32) * inv_root
        gv = lax.dot_general(probs_b, g, TN, preferred_element_type=F32)
        gkv_v[h, :, :HD] = gk.astype(BF)
        gkv_v[h, :, HD:] = gv.astype(BF)

    right, left = xp[0][0], xp[2][0]

    def part(who, half):
        return gqa_v.at[pl.ds(half * 256, 256), span(who, 512)]

    def own_part(half):
        return gq_v.at[pl.ds(half * 256, 256)]

    to_right = [s.send(own_part(h), part(x, h), right) for h in (0, 1)]
    to_left = [s.send(own_part(h), part(x, h), left) for h in (1, 0)]
    gq_in = [s.send(gq_v, gqa_v.at[:, span(x, 512)], None), to_right[1], to_left[1]]
    gkv_in = [
        s.send(gkv_v.at[q], gkvr_v.at[mine], to) for to, q in quad_peers(*place)
    ]
    gkvr_v[mine] = gkv_v[mine]
    for copy in gkv_in:
        s.landed(copy)
    s.landed(to_right[0])
    gq_in.append(s.send(part((x + 3) % 4, 0), part((x + 3) % 4, 0), right))
    s.landed(to_left[0])
    gq_in.append(s.send(part((x + 1) % 4, 1), part((x + 1) % 4, 1), left))
    im0 = gkvr_v[0].astype(F32) + gkvr_v[1].astype(F32)
    im1 = gkvr_v[2].astype(F32) + gkvr_v[3].astype(F32)
    p0, p1 = one
    gkvs_v[:LCAP, :] = (im0 * p0 + im1 * p1).astype(BF)
    gkvs_v[LCAP:, :] = (im0 * (1.0 - p0) + im1 * (1.0 - p1)).astype(BF)

    def kv_block(j):
        cols = span(j, 512)
        rows = cap_v[:, :, :, cols].reshape(512, 512)
        kvp_v[j] = lax.dot_general(rows, gkvs_v[...], TN, preferred_element_type=F32).astype(BF)

    yp, zp = y_peers(*place), z_peers(*place)
    zpair = device(y, 1 - zh, zl, x, c)
    here_dp = y * 2 + zh
    first, second = pl.ds(0, 256), pl.ds(256, 256)
    ka_in, kb_in = [], []
    for k in (1, 3, 2, 0):
        v = (y + k) % 4
        kv_block(v * 2 + 1 - zh)
        ka_in.append(s.send(kvp_v.at[v * 2 + 1 - zh, first], ka_v.at[v], zpair))
        kv_block(v * 2 + zh)
        if k:
            both = kvp_v.at[pl.ds(v * 2, 2), second]
            kb_in.append(s.send(both, kb_v.at[k - 1], yp[k - 1][0]))
    for to, v in xp + [(None, x)]:
        for half in (0, 1):
            s.send(
                attn_v.at[span(v, 128), pl.ds(half * 256, 256)],
                attn_out.at[:, span(half * 4 + x, 256)],
                to,
            )

    for copy in ka_in + kb_in:
        s.landed(copy)
    k2a_in = []
    for k in (1, 3, 2, 0):
        v = (y + k) % 4
        total = kvp_v[v * 2 + zh, first, :].astype(F32) + ka_v[v].astype(F32)
        kvp_v[v * 2 + zh, first, :] = total.astype(BF)
        if k:
            k2a_in.append(s.send(kvp_v.at[v * 2 + zh, first], k2a_v.at[k - 1], yp[k - 1][0]))
    for w in (1 - zh, zh):
        total = kvp_v[y * 2 + w, second, :].astype(F32)
        for k in range(3):
            total = total + kb_v[k, w].astype(F32)
        kvp_v[y * 2 + w, second, :] = total.astype(BF)
    k2b_in = s.send(kvp_v.at[y * 2 + 1 - zh, second], k2b_v, zpair)

    for copy in gq_in:
        s.landed(copy)

    def q_grad(which, at):
        @pl.loop(0, 8)
        def _(i):
            f = i // 4
            cols = pl.ds(pl.multiple_of((i % 4) * 512, 512), 512)
            to_cols = pl.ds(pl.multiple_of(at + (i % 4) * 512, 512), 512)
            from_rows = pl.ds(pl.multiple_of(f * 512 + which * 256, 256), 256)
            part = lax.dot_general(
                xs_v[:, from_rows], gqa_v[:, cols], TN, preferred_element_type=F32
            ).astype(BF)
            ch_v[f * 2, :, to_cols] = part[:128]
            ch_v[f * 2 + 1, :, to_cols] = part[128:]

    q_grad(1 - c, 0)
    qg_pair = s.send(ch_v.at[:, :, pl.ds(0, 2048)], grc_v, pair)
    q_grad(c, 2048)

    @pl.loop(0, 4)
    def _(i):
        rows = pl.ds(pl.multiple_of(i * 256, 256), 256)
        part = lax.dot_general(
            gqa_v[...], wx_v[rows, :], NT, preferred_element_type=F32
        ).astype(BF)
        for v in range(4):
            lat_v[:, pl.ds(pl.multiple_of(v * 1024 + i * 256, 256), 256)] = part[
                v * 128 : (v + 1) * 128
            ]

    for to, v in xp + [(None, x)]:
        for half in (0, 1):
            s.send(
                lat_v.at[:, span(v * 2 + half, 512)],
                dxn_out.at[:, span(half * 4 + x, 512)],
                to,
            )
    s.landed(qg_pair)

    @pl.loop(0, 32)
    def _(i):
        rows = pl.ds(pl.multiple_of((i % 8) * 16, 16), 16)
        keep = ch_v[i // 8, rows, 2048:].astype(F32) + grc_v[i // 8, rows, :].astype(F32)
        ch_v[i // 8, rows, 2048:] = keep.astype(BF)

    r1_in = [
        s.send(ch_v.at[:, span(v, 32), pl.ds(2048, 1024)], r1_v.at[k], to)
        for k, (to, v) in enumerate(yp)
    ]
    r2_in = [
        s.send(ch_v.at[(t % 2) * 2 + t // 2, :, pl.ds(3072, 1024)], r2_v.at[k], to)
        for k, (to, t) in enumerate(zp)
    ]

    for copy in k2a_in + [k2b_in]:
        s.landed(copy)
    total = kvp_v[here_dp, first, :].astype(F32)
    for k in range(3):
        total = total + k2a_v[k].astype(F32)
    kvp_v[here_dp, first, :] = total.astype(BF)
    total = kvp_v[here_dp, second, :].astype(F32) + k2b_v[...].astype(F32)
    kvp_v[here_dp, second, :] = total.astype(BF)

    def kv_at(v, w):
        return gkv_out.at[v * 2 + w]

    def q_at(v, w):
        return gq_out.at[w * 4 + v]

    def spread(own, out, rows):
        s.send(own, out(y, zh), None)
        over = s.send(own.at[pl.ds(0, rows)], out(y, zh).at[pl.ds(0, rows)], zpair)
        along = [(k, s.send(own, out(y, zh), yp[k - 1][0])) for k in (1, 3, 2)]
        s.send(own.at[pl.ds(rows, rows)], out(y, zh).at[pl.ds(rows, rows)], zpair)
        return over, along

    def pass_first(over, out, rows):
        s.landed(over)
        for k in (1, 3, 2):
            pass_on(out(y, 1 - zh).at[pl.ds(0, rows)], yp[k - 1][0])

    def pass_second(along, out, rows):
        for k, copy in along:
            s.landed(copy)
            pass_on(out((y + 4 - k) % 4, zh).at[pl.ds(rows, rows)], zpair)

    kv_over, kv_along = spread(kvp_v.at[here_dp], kv_at, 256)
    for copy in r1_in + r2_in:
        s.landed(copy)
    for i in range(4):
        total = ch_v[i, span(y, 32), 2048:3072].astype(F32)
        for k in range(3):
            total = total + r1_v[k, i].astype(F32)
        s1_v[i] = total.astype(BF)
    at = zl * 2 + zh
    for i in range(4):
        rows = pl.ds(i * 32, 32)
        total = ch_v[at, rows, 3072:].astype(F32)
        for k in range(3):
            total = total + r2_v[k, rows, :].astype(F32)
        s2_v[i] = total.astype(BF)
    t_in = [
        s.send(s1_v.at[(t % 2) * 2 + t // 2], t1_v.at[k], to) for k, (to, t) in enumerate(zp)
    ]
    t_in += [s.send(s2_v.at[v], t2_v.at[k], to) for k, (to, v) in enumerate(yp)]
    pass_first(kv_over, kv_at, 256)
    for copy in t_in:
        s.landed(copy)
    left, right = s1_v[at].astype(F32), s2_v[y].astype(F32)
    for k in range(3):
        left = left + t1_v[k].astype(F32)
        right = right + t2_v[k].astype(F32)
    fin_v[:, :1024] = left.astype(BF)
    fin_v[:, 1024:] = right.astype(BF)
    q_over, q_along = spread(fin_v, q_at, 16)
    pass_second(kv_along, kv_at, 256)
    pass_first(q_over, q_at, 16)
    pass_second(q_along, q_at, 16)
    s.finish()


GROUPS = (x_peers, quad_peers, y_peers, z_peers)
COPIES = 180


def main(*ins):
    anys, vmem = pl.BlockSpec(memory_space=pl.ANY), pl.BlockSpec(memory_space=pltpu.VMEM)
    shapes = [(128, 2048), (128, 4096), (8, 32, 2048), (8, 512, 256)]
    scratch = [
        (128, 4096), (128, 4096), (256, 2048), (4, 128, 4096), (32, 4096), (4096, 768), (384, 4096),
        (4096, 256), (1024, 2048), (512, 1024), (512, 512), None, (512, 384),
        (256, 4096), (256, 4096), (256, 4096), (4, 32, 4096), (3, 32, 4096), (3, 512, 512), (4, 512, 512),
        (512, 512), (2, 8, 32, 4096), (2, LCAP, 256), (2, LCAP, 256), (4, LCAP, 256),
        (512, 512), (512, 512), (4, LCAP, 256), (4, LCAP, 256), (512, 256), (8, 512, 256),
        (512, 2048), (4, 128, 2048), (3, 4, 32, 1024), (3, 128, 1024), (4, 32, 1024), (4, 32, 1024),
        (3, 32, 1024), (3, 32, 1024), (32, 2048), (4, 256, 256), (3, 2, 256, 256),
        (3, 256, 256), (256, 256),
    ]
    return pl.pallas_call(
        kernel,
        out_shape=[jax.ShapeDtypeStruct(shape, BF) for shape in shapes],
        in_specs=[anys] * 9 + [vmem] * 2 + [pl.BlockSpec(memory_space=pltpu.SMEM)] * 2,
        out_specs=[anys] * 4,
        scratch_shapes=[
            pltpu.VMEM((512, 768), F32) if shape is None else pltpu.VMEM(shape, BF)
            for shape in scratch
        ]
        + [pltpu.SemaphoreType.DMA((COPIES,))] * 2,
        compiler_params=pltpu.CompilerParams(
            collective_id=0, has_side_effects=True, vmem_limit_bytes=63 * 2**20
        ),
        name="main",
    )(*ins)


def last_kernel(
    attn, dxn, lat, gq, gkv, attn_o, lat_o, gq_o, gk_o, gv_o,
    attn_v, dxn_v, lat_v, gq_v, gkv_v, attn_f, lat_f, gq_f, gk_f, gv_f, sems,
):
    copies = []

    def move(src, dst):
        copy = pltpu.make_async_copy(src, dst, sems.at[len(copies)])
        copy.start()
        copies.append(copy)
        return copy

    def part(i, size):
        return pl.ds(i * size, size)

    outs = []
    kv_in = [move(gkv.at[part(i, 2)], gkv_v.at[part(i, 2)]) for i in range(4)]
    lat_in = []
    for i in range(4):
        rows = part(i, 32)
        lat_in.append(
            (move(lat.at[rows], lat_v.at[rows]), move(dxn.at[rows], dxn_v.at[rows]))
        )
    gq_in = [move(gq.at[part(i, 4)], gq_v.at[part(i, 4)]) for i in (0, 1)]
    attn_in = move(attn, attn_v)
    for i in range(4):
        kv_in[i].wait()

        @pl.loop(0, 8)
        def _(n, i=i):
            at, rows = i * 2 + n // 4, pl.ds(pl.multiple_of((n % 4) * 128, 128), 128)
            to = pl.ds(pl.multiple_of(i * 1024 + n * 128, 128), 128)
            gk_f[to, :] = gkv_v[at, rows, :HD].astype(F32)
            gv_f[to, :] = gkv_v[at, rows, HD:].astype(F32)

        rows = part(i, 1024)
        outs += [move(gk_f.at[rows], gk_o.at[rows]), move(gv_f.at[rows], gv_o.at[rows])]
    for i in range(4):
        for copy in lat_in[i]:
            copy.wait()

        @pl.loop(0, 2)
        def _(n, i=i):
            rows = pl.ds(pl.multiple_of(i * 32 + n * 16, 16), 16)
            v = lat_v[rows, :].astype(F32)
            r = v - jnp.mean(v, axis=-1, keepdims=True)
            rstd = lax.rsqrt(jnp.mean(r * r, axis=-1, keepdims=True) + 1e-06)
            xhat = r * rstd
            g = dxn_v[rows, :].astype(F32)
            lat_f[rows, :] = rstd * (
                g
                - jnp.mean(g, axis=-1, keepdims=True)
                - xhat * jnp.mean(g * xhat, axis=-1, keepdims=True)
            )

        rows = part(i, 32)
        outs.append(move(lat_f.at[rows], lat_o.at[rows]))
    for i in (0, 1):
        gq_in[i].wait()

        @pl.loop(0, 4)
        def _(n, i=i):
            rows = pl.ds(pl.multiple_of((i * 4 + n) * 32, 32), 32)
            for w in range(4):
                for h in (0, 1):
                    there, here = h * 1024 + w * 256, w * 512 + h * 256
                    gq_f[rows, there : there + 256] = gq_v[i * 4 + n, :, here : here + 256].astype(
                        F32
                    )

        rows = part(i, 128)
        outs.append(move(gq_f.at[rows], gq_o.at[rows]))
    attn_in.wait()

    @pl.loop(0, 4)
    def _(n):
        rows = pl.ds(pl.multiple_of(n * 32, 32), 32)
        attn_f[rows, :] = attn_v[rows, :].astype(F32)

    outs.append(move(attn_f, attn_o))
    for copy in outs:
        copy.wait()


def last(*ins):
    anys = pl.BlockSpec(memory_space=pl.ANY)
    shapes = [(128, 2048), (128, 4096), (256, 2048), (4096, HD), (4096, HD)]
    return pl.pallas_call(
        last_kernel,
        out_shape=[jax.ShapeDtypeStruct(shape, F32) for shape in shapes],
        in_specs=[anys] * 5,
        out_specs=[anys] * 5,
        scratch_shapes=[pltpu.VMEM(a.shape, BF) for a in ins]
        + [pltpu.VMEM(shape, F32) for shape in shapes]
        + [pltpu.SemaphoreType.DMA((40,))],
        compiler_params=pltpu.CompilerParams(vmem_limit_bytes=63 * 2**20),
        name="last",
    )(*ins)


def local(
    cap_hidden,
    t5_norm_gain,
    t5_wi0,
    t5_wi1,
    t5_wo,
    t5_final_gain,
    cap_lengths,
    latents,
    w_query,
    w_key,
    w_value,
    caption_of_image,
    grad_out,
):
    attn, dxn, gq, gkv = main(
        latents,
        grad_out,
        w_query,
        cap_hidden,
        t5_wi0,
        t5_wi1,
        t5_wo,
        w_key,
        w_value,
        t5_norm_gain,
        t5_final_gain,
        cap_lengths,
        caption_of_image,
    )
    return last(attn, dxn, latents, gq, gkv)


def solution(mesh):
    placed = (
        P("dp", None),
        P(),
        P(None, "fsdp"),
        P(None, "fsdp"),
        P("fsdp", None),
        P(),
        P("dp"),
        P(("dp", "fsdp"), None),
        P("fsdp", None),
        P(None, "fsdp"),
        P(None, "fsdp"),
        P("dp"),
        P(("dp", "fsdp"), None),
    )
    return jax.shard_map(
        local,
        mesh=mesh,
        in_specs=placed,
        out_specs=(
            P(("dp", "fsdp"), None),
            P(("dp", "fsdp"), None),
            P("fsdp", None),
            P(None, "fsdp"),
            P(None, "fsdp"),
        ),
        check_vma=False,
    )
```

```python
import functools
import math

import jax
import jax.numpy as jnp
from jax import lax
from jax.experimental import pallas as pl
from jax.experimental.pallas import tpu as pltpu
from jax.sharding import PartitionSpec as P

HD = 128
LCAP = 256
BF = jnp.bfloat16
F32 = jnp.float32
MESH = pl.DeviceIdType.MESH


def coords():
    d, f = lax.axis_index("dp"), lax.axis_index("fsdp")
    return d // 2, d % 2, f // 8, (f // 2) % 4, f % 2


def device(y, zh, zl, x, c):
    return (y * 2 + zh, zl * 8 + x * 2 + c)


def x_peers(y, zh, zl, x, c):
    return [(device(y, zh, zl, (x + k) % 4, c), (x + k) % 4) for k in (1, 2, 3)]


def y_peers(y, zh, zl, x, c):
    return [(device((y + k) % 4, zh, zl, x, c), (y + k) % 4) for k in (1, 2, 3)]


def z_peers(y, zh, zl, x, c):
    z = zh * 2 + zl
    there = [(z + k) % 4 for k in (1, 2, 3)]
    return [(device(y, t // 2, t % 2, x, c), t) for t in there]


def quad_peers(y, zh, zl, x, c):
    there = [((zl + a) % 2, (c + b) % 2) for a in (0, 1) for b in (0, 1) if a or b]
    return [(device(y, zh, w, x, b), w * 2 + b) for w, b in there]


def core_peer(y, zh, zl, x, c):
    return [(device(y, zh, zl, x, 1 - c), 1 - c)]


def span(index, size):
    return pl.ds(pl.multiple_of(index * size, size), size)


class Sender:
    def __init__(self, send_sem, recv_sem):
        self.sems, self.count, self.open = (send_sem, recv_sem), 0, []

    def send(self, src, dst, to):
        t = self.count
        self.count += 1
        if to is None:
            copy = pltpu.make_async_copy(src, dst, self.sems[0].at[t])
        else:
            copy = pltpu.make_async_remote_copy(
                src_ref=src,
                dst_ref=dst,
                send_sem=self.sems[0].at[t],
                recv_sem=self.sems[1].at[t],
                device_id=to,
                device_id_type=MESH,
            )
        copy.start()
        entry = [copy, to is None, False]
        self.open.append(entry)
        return entry

    def landed(self, entry):
        copy, own, seen = entry
        if not seen:
            copy.wait() if own else copy.wait_recv()
            entry[2] = True

    done = landed

    def finish(self):
        for copy, own, seen in self.open:
            if own and not seen:
                copy.wait()
            elif not own and seen:
                copy.wait_send()
            elif not own:
                copy.wait()


NT = (((1,), (1,)), ((), ()))
TN = (((0,), (0,)), ((), ()))


def kernel(
    lat, go, wq, ch, wi0, wi1, wo, wk, wv, gain, gain2, lengths, owner,
    attn_out, dxn_out, gq_out, gkv_out,
    lat_v, xn_v, wp_v, ch_v, row_v, wi_v, wo_v, wkv_v, wx_v, xs_v, gs_v, gl_v, hid_v,
    give_v, keep_v, rc_v, fz_v, fr_v, qs_v, qh_v, qr_v, q_v, cap_v, kv_v, sel_v, kvr_v,
    attn_v, gq_v, gkv_v, gkvr_v, gkvs_v, kvp_v, gqa_v, grc_v, r1_v, r2_v, s1_v, s2_v, t1_v, t2_v,
    fin_v, ka_v, kb_v, k2a_v, k2b_v, sems_a, sems_b,
):
    place = coords()
    y, zh, zl, x, c = place
    pair = core_peer(*place)[0][0]
    across = device(y, zh, 1 - zl, x, c)
    behind = device(y, 1 - zh, 1 - zl, x, c)
    here, mine = zl * 4 + x, zl * 2 + c
    xp = x_peers(*place)
    s = Sender(sems_a, sems_b)
    one = [1.0 - jnp.minimum(owner[i], 1).astype(F32) for i in (0, 1)]
    mine_first = 1 - jnp.minimum(owner[zl], 1)
    length = lengths[0] * mine_first + lengths[1] * (1 - mine_first)

    barrier = pltpu.get_barrier_semaphore()
    peers = [to for group in GROUPS for to, _ in group(*place)]
    for to in peers:
        pl.semaphore_signal(barrier, inc=1, device_id=to, device_id_type=MESH)
    lat_in = s.send(lat, lat_v, None)
    perm = [
        s.send(wq.at[:, pl.ds(h * 1024 + v * 256, 256)], wp_v.at[:, pl.ds(v * 512 + h * 256, 256)], None)
        for h in (0, 1)
        for v in range(4)
    ]
    ch_in = [s.send(ch.at[pl.ds(i * 128, 128)], ch_v.at[i], None) for i in range(4)]
    wi_in = [
        s.send(wi0, wi_v.at[:, pl.ds(0, 384)], None),
        s.send(wi1, wi_v.at[:, pl.ds(384, 384)], None),
    ]
    wo_in = s.send(wo, wo_v, None)
    wkv_in = [
        s.send(wk, wkv_v.at[:, pl.ds(0, 128)], None),
        s.send(wv, wkv_v.at[:, pl.ds(128, 128)], None),
    ]
    s.done(lat_in)

    @pl.loop(0, 8)
    def _(i):
        rows = pl.ds(pl.multiple_of(i * 16, 16), 16)
        v = lat_v[rows, :].astype(F32)
        r = v - jnp.mean(v, axis=-1, keepdims=True)
        xn_v[rows, :] = (r * lax.rsqrt(jnp.mean(r * r, axis=-1, keepdims=True) + 1e-06)).astype(BF)

    pl.semaphore_wait(barrier, len(peers))
    x_in, g_in = [], []
    for to, v in xp + [(None, x)]:
        for half in (0, 1):
            x_in.append(
                s.send(
                    xn_v.at[:, span(half * 4 + v, 512)],
                    xs_v.at[span(x, 128), pl.ds(half * 512, 512)],
                    to,
                )
            )
    for copy in perm:
        s.done(copy)
    w_over = [
        s.send(wp_v.at[pl.ds(i * 128, 128)], wx_v.at[span(mine * 2 + i, 128)], to)
        for i, to in enumerate((across, behind))
    ]
    w_pair = s.send(wp_v, wx_v.at[span(mine, 256)], pair)
    w_own = s.send(wp_v, wx_v.at[span(mine, 256)], None)

    for copy in ch_in:
        s.done(copy)
    row_v[...] = ch_v[c * 2 + here // 4, span(here % 4, 32), :]

    gain_row = gain[...].astype(F32).reshape(1, 4096)

    @pl.loop(0, 32)
    def _(i):
        rows = pl.ds(pl.multiple_of((i % 8) * 16, 16), 16)
        v = ch_v[i // 8, rows, :].astype(F32)
        v = v * lax.rsqrt(jnp.mean(v * v, axis=-1, keepdims=True) + 1e-06) * gain_row
        ch_v[i // 8, rows, :] = v.astype(BF)

    for copy in wi_in:
        s.done(copy)

    @pl.loop(0, 6)
    def _(i):
        rows = pl.ds(pl.multiple_of((i // 3) * 256, 256), 256)
        cols = pl.ds(pl.multiple_of((i % 3) * 256, 256), 256)
        normed = ch_v[pl.ds((i // 3) * 2, 2)].reshape(256, 4096)
        gl_v[rows, cols] = jnp.dot(normed, wi_v[:, cols], preferred_element_type=F32)

    for copy in w_over:
        s.landed(copy)
    theirs = (1 - zl) * 2 + c
    w_far = s.send(wx_v.at[span(theirs, 256)], wx_v.at[span(theirs, 256)], pair)
    for copy in x_in + [w_pair, w_own, w_far]:
        s.landed(copy)

    def query_block(v, out, at):
        @pl.loop(0, 4)
        def _(i):
            rows = pl.ds(pl.multiple_of((i // 2) * 256, 256), 256)
            cols = pl.ds(pl.multiple_of((i % 2) * 256, 256), 256)
            from_cols = pl.ds(pl.multiple_of(v * 512 + (i % 2) * 256, 256), 256)
            out[at, rows, cols] = jnp.dot(
                xs_v[rows, :], wx_v[:, from_cols], preferred_element_type=F32
            ).astype(BF)

    right, left = xp[0][0], xp[2][0]
    upper, lower = pl.ds(0, 256), pl.ds(256, 256)
    query_block(xp[1][1], qs_v, 1)
    qh_in = [
        s.send(qs_v.at[1, upper], qh_v.at[0], right),
        s.send(qs_v.at[1, lower], qh_v.at[1], left),
    ]
    query_block(xp[0][1], qs_v, 0)
    q_in = [s.send(qs_v.at[0, lower], qr_v.at[1, lower], right)]
    query_block(xp[2][1], qs_v, 2)
    q_in.append(s.send(qs_v.at[2, upper], qr_v.at[2, upper], left))

    def pass_query(n, slot, rows, to):
        s.landed(qh_in[n])
        total = qs_v[slot, rows, :].astype(F32) + qh_v[n].astype(F32)
        qs_v[slot, rows, :] = total.astype(BF)
        q_in.append(s.send(qs_v.at[slot, rows], qr_v.at[1 + n, rows], to))

    @pl.loop(0, 8)
    def _(i):
        rows = pl.ds(pl.multiple_of(i * 64, 64), 64)
        g, u = gl_v[rows, :384], gl_v[rows, 384:]
        hid_v[rows, :] = (jax.nn.gelu(g, approximate=True) * u).astype(BF)

    s.done(wo_in)

    def term(which, z, out):
        rows, to_rows = span(which * 2 + z, 128), span(z, 128)

        @pl.loop(0, 4)
        def _(i):
            cols = pl.ds(pl.multiple_of(i * 1024, 1024), 1024)
            out[to_rows, cols] = jnp.dot(
                hid_v[rows, :], wo_v[:, cols], preferred_element_type=F32
            ).astype(BF)

    pair_in = []
    for z in (1 - zl, zl):
        term(1 - c, z, give_v)
        pair_in.append(s.send(give_v.at[span(z, 128)], rc_v.at[span(z, 128)], pair))

    def add_core(z):
        @pl.loop(0, 8)
        def _(i):
            rows = pl.ds(pl.multiple_of(z * 128 + i * 16, 16), 16)
            total = keep_v[rows, :].astype(F32) + rc_v[rows, :].astype(F32)
            keep_v[rows, :] = total.astype(BF)

    term(c, 1 - zl, keep_v)
    s.landed(pair_in[0])
    add_core(1 - zl)
    order = [1, 3, 2, 0]
    fz_in = [
        s.send(keep_v.at[span((1 - zl) * 4 + (x + k) % 4, 32)], fz_v.at[(x + k) % 4], across)
        for k in order
    ]
    term(c, zl, keep_v)
    s.landed(pair_in[1])
    add_core(zl)

    pass_query(0, 0, upper, right)
    pass_query(1, 2, lower, left)
    ff_in = []

    def add_across(n):
        k = order[n]
        s.landed(fz_in[n])
        v = (x + k) % 4
        rows = span(zl * 4 + v, 32)
        total = keep_v[rows, :].astype(F32) + fz_v[v].astype(F32)
        if k:
            keep_v[rows, :] = total.astype(BF)
            ff_in.append(s.send(keep_v.at[rows], fr_v.at[k - 1], xp[k - 1][0]))
        return total

    add_across(0)
    query_block(x, qr_v, 0)
    add_across(1)
    add_across(2)
    ff = add_across(3)

    for copy in ff_in:
        s.landed(copy)
    for k in range(3):
        ff = ff + fr_v[k].astype(F32)
    r = row_v[...].astype(F32) + ff
    r = r * lax.rsqrt(jnp.mean(r * r, axis=-1, keepdims=True) + 1e-06) * gain2[...].astype(F32).reshape(1, 4096)
    cap_v[c, here] = r.astype(BF)
    own = cap_v.at[c, here]
    there = (1 - zl) * 4 + x

    def piece(j, half):
        return cap_v.at[c, j, pl.ds(half * 16, 16)]

    def pass_on(ref, to):
        return s.send(ref, ref, to)

    z_own = [pass_on(piece(here, half), across) for half in (0, 1)]
    x_own = [(k, pass_on(own, xp[k - 1][0])) for k in (1, 3, 2)]
    cap_pair = [pass_on(own, pair)]
    s.landed(z_own[0])
    x_far = [(k, pass_on(piece(there, 0), xp[k - 1][0])) for k in (1, 3, 2)]
    cap_pair.append(pass_on(piece(there, 0), pair))
    for to, v in xp + [(None, x)]:
        for half in (0, 1):
            g_in.append(
                s.send(
                    go.at[:, span(half * 4 + v, 256)],
                    gs_v.at[span(x, 128), pl.ds(half * 256, 256)],
                    to,
                )
            )

    z_far = []
    for k, copy in x_own:
        s.landed(copy)
        j = zl * 4 + (x + 4 - k) % 4
        z_far.append((k, pass_on(piece(j, 1), across)))
        cap_pair.append(pass_on(cap_v.at[c, j], pair))
    s.landed(z_own[1])
    cap_pair.append(pass_on(piece(there, 1), pair))
    for half, group in ((0, x_far), (1, z_far)):
        for k, copy in group:
            s.landed(copy)
            cap_pair.append(pass_on(piece((1 - zl) * 4 + (x + 4 - k) % 4, half), pair))
    for copy in q_in:
        s.landed(copy)

    @pl.loop(0, 8)
    def _(i):
        rows = pl.ds(pl.multiple_of(i * 64, 64), 64)
        q = qr_v[0, rows, :].astype(F32) + qr_v[1, rows, :].astype(F32)
        q = q + qr_v[2, rows, :].astype(F32)
        q_v[rows, :] = q.astype(BF)

    for copy in wkv_in:
        s.done(copy)

    def key_value(which):
        rows = cap_v[which].reshape(256, 4096)
        kv_v[which] = jnp.dot(rows, wkv_v[...], preferred_element_type=F32).astype(BF)

    key_value(c)
    for copy in cap_pair:
        s.landed(copy)
    key_value(1 - c)
    for i in (0, 1):
        p = one[i]
        both = kv_v[0].astype(F32) * p + kv_v[1].astype(F32) * (1.0 - p)
        sel_v[i] = both.astype(BF)
    kv_over = s.send(sel_v.at[1 - zl], kvr_v.at[mine], across)
    kv_pair = s.send(sel_v.at[zl], kvr_v.at[mine], pair)
    kvr_v[mine] = sel_v[zl]
    for copy in g_in + [kv_pair]:
        s.landed(copy)

    inv_root = 1.0 / math.sqrt(HD)

    def attend(h):
        cols = pl.ds(pl.multiple_of(h * HD, HD), HD)
        q, g = q_v[:, cols], gs_v[:, cols]
        k, v = kvr_v[h, :, :HD], kvr_v[h, :, HD:]
        scores = lax.dot_general(q, k, NT, preferred_element_type=F32) * inv_root
        live = lax.broadcasted_iota(jnp.int32, scores.shape, 1) < length
        scores = jnp.where(live, scores, -1e30)
        e = jnp.exp(scores - jnp.max(scores, axis=-1, keepdims=True))
        probs = e / jnp.sum(e, axis=-1, keepdims=True)
        probs_b = probs.astype(BF)
        attn_v[:, cols] = jnp.dot(probs_b, v, preferred_element_type=F32).astype(BF)
        gp = lax.dot_general(g, v, NT, preferred_element_type=F32)
        gs = (probs * (gp - jnp.sum(probs * gp, axis=-1, keepdims=True))).astype(BF)
        gq_v[:, cols] = (jnp.dot(gs, k, preferred_element_type=F32) * inv_root).astype(BF)
        gk = lax.dot_general(gs, q, TN, preferred_element_type=F32) * inv_root
        gv = lax.dot_general(probs_b, g, TN, preferred_element_type=F32)
        gkv_v[h, :, :HD] = gk.astype(BF)
        gkv_v[h, :, HD:] = gv.astype(BF)

    @pl.loop(0, 2)
    def _(i):
        attend(zl * 2 + i)

    s.landed(kv_over)
    kv_far = s.send(kvr_v.at[theirs], kvr_v.at[theirs], pair)
    attend(theirs)
    s.landed(kv_far)
    attend((1 - zl) * 2 + 1 - c)

    right, left = xp[0][0], xp[2][0]

    def part(who, half):
        return gqa_v.at[pl.ds(half * 256, 256), span(who, 512)]

    def own_part(half):
        return gq_v.at[pl.ds(half * 256, 256)]

    to_right = [s.send(own_part(h), part(x, h), right) for h in (0, 1)]
    to_left = [s.send(own_part(h), part(x, h), left) for h in (1, 0)]
    gq_in = [s.send(gq_v, gqa_v.at[:, span(x, 512)], None), to_right[1], to_left[1]]
    gkv_in = [
        s.send(gkv_v.at[q], gkvr_v.at[mine], to) for to, q in quad_peers(*place)
    ]
    gkvr_v[mine] = gkv_v[mine]
    for copy in gkv_in:
        s.landed(copy)
    s.landed(to_right[0])
    gq_in.append(s.send(part((x + 3) % 4, 0), part((x + 3) % 4, 0), right))
    s.landed(to_left[0])
    gq_in.append(s.send(part((x + 1) % 4, 1), part((x + 1) % 4, 1), left))
    im0 = gkvr_v[0].astype(F32) + gkvr_v[1].astype(F32)
    im1 = gkvr_v[2].astype(F32) + gkvr_v[3].astype(F32)
    p0, p1 = one
    gkvs_v[:LCAP, :] = (im0 * p0 + im1 * p1).astype(BF)
    gkvs_v[LCAP:, :] = (im0 * (1.0 - p0) + im1 * (1.0 - p1)).astype(BF)

    def kv_block(j):
        cols = span(j, 512)
        rows = cap_v[:, :, :, cols].reshape(512, 512)
        kvp_v[j] = lax.dot_general(rows, gkvs_v[...], TN, preferred_element_type=F32).astype(BF)

    yp, zp = y_peers(*place), z_peers(*place)
    zpair = device(y, 1 - zh, zl, x, c)
    here_dp = y * 2 + zh
    first, second = pl.ds(0, 256), pl.ds(256, 256)
    ka_in, kb_in = [], []
    for k in (1, 3, 2, 0):
        v = (y + k) % 4
        kv_block(v * 2 + 1 - zh)
        ka_in.append(s.send(kvp_v.at[v * 2 + 1 - zh, first], ka_v.at[v], zpair))
        kv_block(v * 2 + zh)
        if k:
            both = kvp_v.at[pl.ds(v * 2, 2), second]
            kb_in.append(s.send(both, kb_v.at[k - 1], yp[k - 1][0]))
    for to, v in xp + [(None, x)]:
        for half in (0, 1):
            s.send(
                attn_v.at[span(v, 128), pl.ds(half * 256, 256)],
                attn_out.at[:, span(half * 4 + x, 256)],
                to,
            )

    for copy in ka_in + kb_in:
        s.landed(copy)
    k2a_in = []
    for k in (1, 3, 2, 0):
        v = (y + k) % 4
        total = kvp_v[v * 2 + zh, first, :].astype(F32) + ka_v[v].astype(F32)
        kvp_v[v * 2 + zh, first, :] = total.astype(BF)
        if k:
            k2a_in.append(s.send(kvp_v.at[v * 2 + zh, first], k2a_v.at[k - 1], yp[k - 1][0]))
    for w in (1 - zh, zh):
        total = kvp_v[y * 2 + w, second, :].astype(F32)
        for k in range(3):
            total = total + kb_v[k, w].astype(F32)
        kvp_v[y * 2 + w, second, :] = total.astype(BF)
    k2b_in = s.send(kvp_v.at[y * 2 + 1 - zh, second], k2b_v, zpair)

    for copy in gq_in:
        s.landed(copy)

    def q_grad(which, at):
        @pl.loop(0, 8)
        def _(i):
            f = i // 4
            cols = pl.ds(pl.multiple_of((i % 4) * 512, 512), 512)
            to_cols = pl.ds(pl.multiple_of(at + (i % 4) * 512, 512), 512)
            from_rows = pl.ds(pl.multiple_of(f * 512 + which * 256, 256), 256)
            part = lax.dot_general(
                xs_v[:, from_rows], gqa_v[:, cols], TN, preferred_element_type=F32
            ).astype(BF)
            ch_v[f * 2, :, to_cols] = part[:128]
            ch_v[f * 2 + 1, :, to_cols] = part[128:]

    q_grad(1 - c, 0)
    qg_pair = s.send(ch_v.at[:, :, pl.ds(0, 2048)], grc_v, pair)
    q_grad(c, 2048)

    @pl.loop(0, 4)
    def _(i):
        rows = pl.ds(pl.multiple_of(i * 256, 256), 256)
        part = lax.dot_general(
            gqa_v[...], wx_v[rows, :], NT, preferred_element_type=F32
        ).astype(BF)
        for v in range(4):
            lat_v[:, pl.ds(pl.multiple_of(v * 1024 + i * 256, 256), 256)] = part[
                v * 128 : (v + 1) * 128
            ]

    for to, v in xp + [(None, x)]:
        for half in (0, 1):
            s.send(
                lat_v.at[:, span(v * 2 + half, 512)],
                dxn_out.at[:, span(half * 4 + x, 512)],
                to,
            )
    s.landed(qg_pair)

    @pl.loop(0, 32)
    def _(i):
        rows = pl.ds(pl.multiple_of((i % 8) * 16, 16), 16)
        keep = ch_v[i // 8, rows, 2048:].astype(F32) + grc_v[i // 8, rows, :].astype(F32)
        ch_v[i // 8, rows, 2048:] = keep.astype(BF)

    r1_in = [
        s.send(ch_v.at[:, span(v, 32), pl.ds(2048, 1024)], r1_v.at[k], to)
        for k, (to, v) in enumerate(yp)
    ]
    r2_in = [
        s.send(ch_v.at[(t % 2) * 2 + t // 2, :, pl.ds(3072, 1024)], r2_v.at[k], to)
        for k, (to, t) in enumerate(zp)
    ]

    for copy in k2a_in + [k2b_in]:
        s.landed(copy)
    total = kvp_v[here_dp, first, :].astype(F32)
    for k in range(3):
        total = total + k2a_v[k].astype(F32)
    kvp_v[here_dp, first, :] = total.astype(BF)
    total = kvp_v[here_dp, second, :].astype(F32) + k2b_v[...].astype(F32)
    kvp_v[here_dp, second, :] = total.astype(BF)

    def kv_at(v, w):
        return gkv_out.at[v * 2 + w]

    def q_at(v, w):
        return gq_out.at[w * 4 + v]

    def spread(own, out, rows):
        s.send(own, out(y, zh), None)
        over = s.send(own.at[pl.ds(0, rows)], out(y, zh).at[pl.ds(0, rows)], zpair)
        along = [(k, s.send(own, out(y, zh), yp[k - 1][0])) for k in (1, 3, 2)]
        s.send(own.at[pl.ds(rows, rows)], out(y, zh).at[pl.ds(rows, rows)], zpair)
        return over, along

    def pass_first(over, out, rows):
        s.landed(over)
        for k in (1, 3, 2):
            pass_on(out(y, 1 - zh).at[pl.ds(0, rows)], yp[k - 1][0])

    def pass_second(along, out, rows):
        for k, copy in along:
            s.landed(copy)
            pass_on(out((y + 4 - k) % 4, zh).at[pl.ds(rows, rows)], zpair)

    dp_over, kv_along = spread(kvp_v.at[here_dp], kv_at, 256)
    for copy in r1_in + r2_in:
        s.landed(copy)
    for i in range(4):
        total = ch_v[i, span(y, 32), 2048:3072].astype(F32)
        for k in range(3):
            total = total + r1_v[k, i].astype(F32)
        s1_v[i] = total.astype(BF)
    at = zl * 2 + zh
    for i in range(4):
        rows = pl.ds(i * 32, 32)
        total = ch_v[at, rows, 3072:].astype(F32)
        for k in range(3):
            total = total + r2_v[k, rows, :].astype(F32)
        s2_v[i] = total.astype(BF)
    t_in = [
        s.send(s1_v.at[(t % 2) * 2 + t // 2], t1_v.at[k], to) for k, (to, t) in enumerate(zp)
    ]
    t_in += [s.send(s2_v.at[v], t2_v.at[k], to) for k, (to, v) in enumerate(yp)]
    pass_first(dp_over, kv_at, 256)
    for copy in t_in:
        s.landed(copy)
    left, right = s1_v[at].astype(F32), s2_v[y].astype(F32)
    for k in range(3):
        left = left + t1_v[k].astype(F32)
        right = right + t2_v[k].astype(F32)
    fin_v[:, :1024] = left.astype(BF)
    fin_v[:, 1024:] = right.astype(BF)
    q_over, q_along = spread(fin_v, q_at, 16)
    pass_second(kv_along, kv_at, 256)
    pass_first(q_over, q_at, 16)
    pass_second(q_along, q_at, 16)
    s.finish()


GROUPS = (x_peers, quad_peers, y_peers, z_peers)
COPIES = 180


def main(*ins):
    anys, vmem = pl.BlockSpec(memory_space=pl.ANY), pl.BlockSpec(memory_space=pltpu.VMEM)
    shapes = [(128, 2048), (128, 4096), (8, 32, 2048), (8, 512, 256)]
    scratch = [
        (128, 4096), (128, 4096), (256, 2048), (4, 128, 4096), (32, 4096), (4096, 768), (384, 4096),
        (4096, 256), (1024, 2048), (512, 1024), (512, 512), None, (512, 384),
        (256, 4096), (256, 4096), (256, 4096), (4, 32, 4096), (3, 32, 4096), (3, 512, 512), (2, 256, 512), (3, 512, 512),
        (512, 512), (2, 8, 32, 4096), (2, LCAP, 256), (2, LCAP, 256), (4, LCAP, 256),
        (512, 512), (512, 512), (4, LCAP, 256), (4, LCAP, 256), (512, 256), (8, 512, 256),
        (512, 2048), (4, 128, 2048), (3, 4, 32, 1024), (3, 128, 1024), (4, 32, 1024), (4, 32, 1024),
        (3, 32, 1024), (3, 32, 1024), (32, 2048), (4, 256, 256), (3, 2, 256, 256),
        (3, 256, 256), (256, 256),
    ]
    return pl.pallas_call(
        kernel,
        out_shape=[jax.ShapeDtypeStruct(shape, BF) for shape in shapes],
        in_specs=[anys] * 9 + [vmem] * 2 + [pl.BlockSpec(memory_space=pltpu.SMEM)] * 2,
        out_specs=[anys] * 4,
        scratch_shapes=[
            pltpu.VMEM((512, 768), F32) if shape is None else pltpu.VMEM(shape, BF)
            for shape in scratch
        ]
        + [pltpu.SemaphoreType.DMA((COPIES,))] * 2,
        compiler_params=pltpu.CompilerParams(
            collective_id=0, has_side_effects=True, vmem_limit_bytes=63 * 2**20
        ),
        name="main",
    )(*ins)


def last_kernel(
    attn, dxn, lat, gq, gkv, attn_o, lat_o, gq_o, gk_o, gv_o,
    attn_v, dxn_v, lat_v, gq_v, gkv_v, attn_f, lat_f, gq_f, gk_f, gv_f, sems,
):
    copies = []

    def move(src, dst):
        copy = pltpu.make_async_copy(src, dst, sems.at[len(copies)])
        copy.start()
        copies.append(copy)
        return copy

    def part(i, size):
        return pl.ds(i * size, size)

    outs = []
    kv_in = [move(gkv.at[part(i, 2)], gkv_v.at[part(i, 2)]) for i in range(4)]
    lat_in = []
    for i in range(4):
        rows = part(i, 32)
        lat_in.append(
            (move(lat.at[rows], lat_v.at[rows]), move(dxn.at[rows], dxn_v.at[rows]))
        )
    gq_in = [move(gq.at[part(i, 4)], gq_v.at[part(i, 4)]) for i in (0, 1)]
    attn_in = move(attn, attn_v)
    for i in range(4):
        kv_in[i].wait()

        @pl.loop(0, 8)
        def _(n, i=i):
            at, rows = i * 2 + n // 4, pl.ds(pl.multiple_of((n % 4) * 128, 128), 128)
            to = pl.ds(pl.multiple_of(i * 1024 + n * 128, 128), 128)
            gk_f[to, :] = gkv_v[at, rows, :HD].astype(F32)
            gv_f[to, :] = gkv_v[at, rows, HD:].astype(F32)

        rows = part(i, 1024)
        outs += [move(gk_f.at[rows], gk_o.at[rows]), move(gv_f.at[rows], gv_o.at[rows])]
    for i in range(4):
        for copy in lat_in[i]:
            copy.wait()

        @pl.loop(0, 2)
        def _(n, i=i):
            rows = pl.ds(pl.multiple_of(i * 32 + n * 16, 16), 16)
            v = lat_v[rows, :].astype(F32)
            r = v - jnp.mean(v, axis=-1, keepdims=True)
            rstd = lax.rsqrt(jnp.mean(r * r, axis=-1, keepdims=True) + 1e-06)
            xhat = r * rstd
            g = dxn_v[rows, :].astype(F32)
            lat_f[rows, :] = rstd * (
                g
                - jnp.mean(g, axis=-1, keepdims=True)
                - xhat * jnp.mean(g * xhat, axis=-1, keepdims=True)
            )

        rows = part(i, 32)
        outs.append(move(lat_f.at[rows], lat_o.at[rows]))
    for i in (0, 1):
        gq_in[i].wait()

        @pl.loop(0, 4)
        def _(n, i=i):
            rows = pl.ds(pl.multiple_of((i * 4 + n) * 32, 32), 32)
            for w in range(4):
                for h in (0, 1):
                    there, here = h * 1024 + w * 256, w * 512 + h * 256
                    gq_f[rows, there : there + 256] = gq_v[i * 4 + n, :, here : here + 256].astype(
                        F32
                    )

        rows = part(i, 128)
        outs.append(move(gq_f.at[rows], gq_o.at[rows]))
    attn_in.wait()

    @pl.loop(0, 4)
    def _(n):
        rows = pl.ds(pl.multiple_of(n * 32, 32), 32)
        attn_f[rows, :] = attn_v[rows, :].astype(F32)

    outs.append(move(attn_f, attn_o))
    for copy in outs:
        copy.wait()


def last(*ins):
    anys = pl.BlockSpec(memory_space=pl.ANY)
    shapes = [(128, 2048), (128, 4096), (256, 2048), (4096, HD), (4096, HD)]
    return pl.pallas_call(
        last_kernel,
        out_shape=[jax.ShapeDtypeStruct(shape, F32) for shape in shapes],
        in_specs=[anys] * 5,
        out_specs=[anys] * 5,
        scratch_shapes=[pltpu.VMEM(a.shape, BF) for a in ins]
        + [pltpu.VMEM(shape, F32) for shape in shapes]
        + [pltpu.SemaphoreType.DMA((40,))],
        compiler_params=pltpu.CompilerParams(vmem_limit_bytes=63 * 2**20),
        name="last",
    )(*ins)


def local(
    cap_hidden,
    t5_norm_gain,
    t5_wi0,
    t5_wi1,
    t5_wo,
    t5_final_gain,
    cap_lengths,
    latents,
    w_query,
    w_key,
    w_value,
    caption_of_image,
    grad_out,
):
    attn, dxn, gq, gkv = main(
        latents,
        grad_out,
        w_query,
        cap_hidden,
        t5_wi0,
        t5_wi1,
        t5_wo,
        w_key,
        w_value,
        t5_norm_gain,
        t5_final_gain,
        cap_lengths,
        caption_of_image,
    )
    return last(attn, dxn, latents, gq, gkv)


def solution(mesh):
    placed = (
        P("dp", None),
        P(),
        P(None, "fsdp"),
        P(None, "fsdp"),
        P("fsdp", None),
        P(),
        P("dp"),
        P(("dp", "fsdp"), None),
        P("fsdp", None),
        P(None, "fsdp"),
        P(None, "fsdp"),
        P("dp"),
        P(("dp", "fsdp"), None),
    )
    return jax.shard_map(
        local,
        mesh=mesh,
        in_specs=placed,
        out_specs=(
            P(("dp", "fsdp"), None),
            P(("dp", "fsdp"), None),
            P("fsdp", None),
            P(None, "fsdp"),
            P(None, "fsdp"),
        ),
        check_vma=False,
    )
```

```python
import functools
import math

import jax
import jax.numpy as jnp
from jax import lax
from jax.experimental import pallas as pl
from jax.experimental.pallas import tpu as pltpu
from jax.sharding import PartitionSpec as P

HD = 128
LCAP = 256
BF = jnp.bfloat16
F32 = jnp.float32
MESH = pl.DeviceIdType.MESH


def coords():
    d, f = lax.axis_index("dp"), lax.axis_index("fsdp")
    return d // 2, d % 2, f // 8, (f // 2) % 4, f % 2


def device(y, zh, zl, x, c):
    return (y * 2 + zh, zl * 8 + x * 2 + c)


def x_peers(y, zh, zl, x, c):
    return [(device(y, zh, zl, (x + k) % 4, c), (x + k) % 4) for k in (1, 2, 3)]


def y_peers(y, zh, zl, x, c):
    return [(device((y + k) % 4, zh, zl, x, c), (y + k) % 4) for k in (1, 2, 3)]


def z_peers(y, zh, zl, x, c):
    z = zh * 2 + zl
    there = [(z + k) % 4 for k in (1, 2, 3)]
    return [(device(y, t // 2, t % 2, x, c), t) for t in there]


def quad_peers(y, zh, zl, x, c):
    there = [((zl + a) % 2, (c + b) % 2) for a in (0, 1) for b in (0, 1) if a or b]
    return [(device(y, zh, w, x, b), w * 2 + b) for w, b in there]


def core_peer(y, zh, zl, x, c):
    return [(device(y, zh, zl, x, 1 - c), 1 - c)]


def span(index, size):
    return pl.ds(pl.multiple_of(index * size, size), size)


class Sender:
    def __init__(self, send_sem, recv_sem):
        self.sems, self.count, self.open = (send_sem, recv_sem), 0, []

    def send(self, src, dst, to):
        t = self.count
        self.count += 1
        if to is None:
            copy = pltpu.make_async_copy(src, dst, self.sems[0].at[t])
        else:
            copy = pltpu.make_async_remote_copy(
                src_ref=src,
                dst_ref=dst,
                send_sem=self.sems[0].at[t],
                recv_sem=self.sems[1].at[t],
                device_id=to,
                device_id_type=MESH,
            )
        copy.start()
        entry = [copy, to is None, False]
        self.open.append(entry)
        return entry

    def landed(self, entry):
        copy, own, seen = entry
        if not seen:
            copy.wait() if own else copy.wait_recv()
            entry[2] = True

    done = landed

    def finish(self):
        for copy, own, seen in self.open:
            if own and not seen:
                copy.wait()
            elif not own and seen:
                copy.wait_send()
            elif not own:
                copy.wait()


NT = (((1,), (1,)), ((), ()))
TN = (((0,), (0,)), ((), ()))


def kernel(
    lat, go, wq, ch, wi0, wi1, wo, wk, wv, gain, gain2, lengths, owner,
    attn_out, dxn_out, gq_out, gkv_out,
    lat_v, xn_v, wp_v, ch_v, row_v, wi_v, wo_v, wkv_v, wx_v, xs_v, gs_v, gl_v, hid_v,
    give_v, keep_v, rc_v, fz_v, fr_v, qs_v, qh_v, qr_v, q_v, cap_v, kv_v, sel_v, kvr_v,
    attn_v, gq_v, gkv_v, gkvr_v, gkvs_v, kvp_v, gqa_v, grc_v, r1_v, r2_v, s1_v, s2_v, t1_v, t2_v,
    fin_v, ka_v, kb_v, k2a_v, k2b_v, sems_a, sems_b,
):
    place = coords()
    y, zh, zl, x, c = place
    pair = core_peer(*place)[0][0]
    across = device(y, zh, 1 - zl, x, c)
    behind = device(y, 1 - zh, 1 - zl, x, c)
    here, mine = zl * 4 + x, zl * 2 + c
    xp = x_peers(*place)
    s = Sender(sems_a, sems_b)
    one = [1.0 - jnp.minimum(owner[i], 1).astype(F32) for i in (0, 1)]
    mine_first = 1 - jnp.minimum(owner[zl], 1)
    length = lengths[0] * mine_first + lengths[1] * (1 - mine_first)

    barrier = pltpu.get_barrier_semaphore()
    peers = [to for group in GROUPS for to, _ in group(*place)]
    for to in peers:
        pl.semaphore_signal(barrier, inc=1, device_id=to, device_id_type=MESH)
    lat_in = s.send(lat, lat_v, None)
    perm = [
        s.send(wq.at[:, pl.ds(h * 1024 + v * 256, 256)], wp_v.at[:, pl.ds(v * 512 + h * 256, 256)], None)
        for h in (0, 1)
        for v in range(4)
    ]
    ch_in = [s.send(ch.at[pl.ds(i * 128, 128)], ch_v.at[i], None) for i in range(4)]
    wi_in = [
        s.send(wi0, wi_v.at[:, pl.ds(0, 384)], None),
        s.send(wi1, wi_v.at[:, pl.ds(384, 384)], None),
    ]
    wo_in = s.send(wo, wo_v, None)
    wkv_in = [
        s.send(wk, wkv_v.at[:, pl.ds(0, 128)], None),
        s.send(wv, wkv_v.at[:, pl.ds(128, 128)], None),
    ]
    s.done(lat_in)

    @pl.loop(0, 8)
    def _(i):
        rows = pl.ds(pl.multiple_of(i * 16, 16), 16)
        v = lat_v[rows, :].astype(F32)
        r = v - jnp.mean(v, axis=-1, keepdims=True)
        xn_v[rows, :] = (r * lax.rsqrt(jnp.mean(r * r, axis=-1, keepdims=True) + 1e-06)).astype(BF)

    pl.semaphore_wait(barrier, len(peers))
    x_in, g_in = [], []
    for to, v in xp + [(None, x)]:
        for half in (0, 1):
            x_in.append(
                s.send(
                    xn_v.at[:, span(half * 4 + v, 512)],
                    xs_v.at[span(x, 128), pl.ds(half * 512, 512)],
                    to,
                )
            )
    for copy in perm:
        s.done(copy)
    w_over = [
        s.send(wp_v.at[pl.ds(i * 128, 128)], wx_v.at[span(mine * 2 + i, 128)], to)
        for i, to in enumerate((across, behind))
    ]
    w_pair = s.send(wp_v, wx_v.at[span(mine, 256)], pair)
    w_own = s.send(wp_v, wx_v.at[span(mine, 256)], None)

    for copy in ch_in:
        s.done(copy)
    row_v[...] = ch_v[c * 2 + here // 4, span(here % 4, 32), :]

    gain_row = gain[...].astype(F32).reshape(1, 4096)

    @pl.loop(0, 32)
    def _(i):
        rows = pl.ds(pl.multiple_of((i % 8) * 16, 16), 16)
        v = ch_v[i // 8, rows, :].astype(F32)
        v = v * lax.rsqrt(jnp.mean(v * v, axis=-1, keepdims=True) + 1e-06) * gain_row
        ch_v[i // 8, rows, :] = v.astype(BF)

    for copy in wi_in:
        s.done(copy)

    @pl.loop(0, 6)
    def _(i):
        rows = pl.ds(pl.multiple_of((i // 3) * 256, 256), 256)
        cols = pl.ds(pl.multiple_of((i % 3) * 256, 256), 256)
        normed = ch_v[pl.ds((i // 3) * 2, 2)].reshape(256, 4096)
        gl_v[rows, cols] = jnp.dot(normed, wi_v[:, cols], preferred_element_type=F32)

    for copy in w_over:
        s.landed(copy)
    theirs = (1 - zl) * 2 + c
    w_far = s.send(wx_v.at[span(theirs, 256)], wx_v.at[span(theirs, 256)], pair)
    for copy in x_in + [w_pair, w_own, w_far]:
        s.landed(copy)

    def query_block(v, out, at):
        @pl.loop(0, 4)
        def _(i):
            rows = pl.ds(pl.multiple_of((i // 2) * 256, 256), 256)
            cols = pl.ds(pl.multiple_of((i % 2) * 256, 256), 256)
            from_cols = pl.ds(pl.multiple_of(v * 512 + (i % 2) * 256, 256), 256)
            out[at, rows, cols] = jnp.dot(
                xs_v[rows, :], wx_v[:, from_cols], preferred_element_type=F32
            ).astype(BF)

    right, left = xp[0][0], xp[2][0]
    upper, lower = pl.ds(0, 256), pl.ds(256, 256)
    query_block(xp[1][1], qs_v, 1)
    qh_in = [
        s.send(qs_v.at[1, upper], qh_v.at[0], right),
        s.send(qs_v.at[1, lower], qh_v.at[1], left),
    ]
    query_block(xp[0][1], qs_v, 0)
    q_in = [s.send(qs_v.at[0, lower], qr_v.at[1, lower], right)]
    query_block(xp[2][1], qs_v, 2)
    q_in.append(s.send(qs_v.at[2, upper], qr_v.at[2, upper], left))

    def pass_query(n, slot, rows, to):
        s.landed(qh_in[n])
        total = qs_v[slot, rows, :].astype(F32) + qh_v[n].astype(F32)
        qs_v[slot, rows, :] = total.astype(BF)
        q_in.append(s.send(qs_v.at[slot, rows], qr_v.at[1 + n, rows], to))

    @pl.loop(0, 8)
    def _(i):
        rows = pl.ds(pl.multiple_of(i * 64, 64), 64)
        g, u = gl_v[rows, :384], gl_v[rows, 384:]
        hid_v[rows, :] = (jax.nn.gelu(g, approximate=True) * u).astype(BF)

    s.done(wo_in)

    def term(which, z, out):
        rows, to_rows = span(which * 2 + z, 128), span(z, 128)

        @pl.loop(0, 4)
        def _(i):
            cols = pl.ds(pl.multiple_of(i * 1024, 1024), 1024)
            out[to_rows, cols] = jnp.dot(
                hid_v[rows, :], wo_v[:, cols], preferred_element_type=F32
            ).astype(BF)

    pair_in = []
    for z in (1 - zl, zl):
        term(1 - c, z, give_v)
        pair_in.append(s.send(give_v.at[span(z, 128)], rc_v.at[span(z, 128)], pair))

    def add_core(z):
        @pl.loop(0, 8)
        def _(i):
            rows = pl.ds(pl.multiple_of(z * 128 + i * 16, 16), 16)
            total = keep_v[rows, :].astype(F32) + rc_v[rows, :].astype(F32)
            keep_v[rows, :] = total.astype(BF)

    term(c, 1 - zl, keep_v)
    s.landed(pair_in[0])
    add_core(1 - zl)
    order = [1, 3, 2, 0]
    fz_in = [
        s.send(keep_v.at[span((1 - zl) * 4 + (x + k) % 4, 32)], fz_v.at[(x + k) % 4], across)
        for k in order
    ]
    term(c, zl, keep_v)
    s.landed(pair_in[1])
    add_core(zl)

    pass_query(0, 0, upper, right)
    pass_query(1, 2, lower, left)
    ff_in = []

    def add_across(n):
        k = order[n]
        s.landed(fz_in[n])
        v = (x + k) % 4
        rows = span(zl * 4 + v, 32)
        total = keep_v[rows, :].astype(F32) + fz_v[v].astype(F32)
        if k:
            keep_v[rows, :] = total.astype(BF)
            ff_in.append(s.send(keep_v.at[rows], fr_v.at[k - 1], xp[k - 1][0]))
        return total

    add_across(0)
    query_block(x, qr_v, 0)
    add_across(1)
    add_across(2)
    ff = add_across(3)

    for copy in ff_in:
        s.landed(copy)
    for k in range(3):
        ff = ff + fr_v[k].astype(F32)
    r = row_v[...].astype(F32) + ff
    r = r * lax.rsqrt(jnp.mean(r * r, axis=-1, keepdims=True) + 1e-06) * gain2[...].astype(F32).reshape(1, 4096)
    cap_v[c, here] = r.astype(BF)
    own = cap_v.at[c, here]
    there = (1 - zl) * 4 + x

    def piece(j, half):
        return cap_v.at[c, j, pl.ds(half * 16, 16)]

    def pass_on(ref, to):
        return s.send(ref, ref, to)

    z_own = [pass_on(piece(here, half), across) for half in (0, 1)]
    x_own = [(k, pass_on(own, xp[k - 1][0])) for k in (1, 3, 2)]
    cap_pair = [pass_on(own, pair)]
    s.landed(z_own[0])
    x_far = [(k, pass_on(piece(there, 0), xp[k - 1][0])) for k in (1, 3, 2)]
    cap_pair.append(pass_on(piece(there, 0), pair))
    for to, v in xp + [(None, x)]:
        for half in (0, 1):
            g_in.append(
                s.send(
                    go.at[:, span(half * 4 + v, 256)],
                    gs_v.at[span(x, 128), pl.ds(half * 256, 256)],
                    to,
                )
            )

    z_far = []
    for k, copy in x_own:
        s.landed(copy)
        j = zl * 4 + (x + 4 - k) % 4
        z_far.append((k, pass_on(piece(j, 1), across)))
        cap_pair.append(pass_on(cap_v.at[c, j], pair))
    s.landed(z_own[1])
    cap_pair.append(pass_on(piece(there, 1), pair))
    for half, group in ((0, x_far), (1, z_far)):
        for k, copy in group:
            s.landed(copy)
            cap_pair.append(pass_on(piece((1 - zl) * 4 + (x + 4 - k) % 4, half), pair))
    for copy in q_in:
        s.landed(copy)

    @pl.loop(0, 8)
    def _(i):
        rows = pl.ds(pl.multiple_of(i * 64, 64), 64)
        q = qr_v[0, rows, :].astype(F32) + qr_v[1, rows, :].astype(F32)
        q = q + qr_v[2, rows, :].astype(F32)
        q_v[rows, :] = q.astype(BF)

    for copy in wkv_in:
        s.done(copy)

    def key_value(which):
        rows = cap_v[which].reshape(256, 4096)
        kv_v[which] = jnp.dot(rows, wkv_v[...], preferred_element_type=F32).astype(BF)

    key_value(c)
    for copy in cap_pair:
        s.landed(copy)
    key_value(1 - c)
    for i in (0, 1):
        p = one[i]
        both = kv_v[0].astype(F32) * p + kv_v[1].astype(F32) * (1.0 - p)
        sel_v[i] = both.astype(BF)
    kv_over = s.send(sel_v.at[1 - zl], kvr_v.at[mine], across)
    kv_pair = s.send(sel_v.at[zl], kvr_v.at[mine], pair)
    kvr_v[mine] = sel_v[zl]
    for copy in g_in + [kv_pair]:
        s.landed(copy)

    inv_root = 1.0 / math.sqrt(HD)

    def attend(h):
        cols = pl.ds(pl.multiple_of(h * HD, HD), HD)
        q, g = q_v[:, cols], gs_v[:, cols]
        k, v = kvr_v[h, :, :HD], kvr_v[h, :, HD:]
        scores = lax.dot_general(q, k, NT, preferred_element_type=F32) * inv_root
        live = lax.broadcasted_iota(jnp.int32, scores.shape, 1) < length
        scores = jnp.where(live, scores, -1e30)
        e = jnp.exp(scores - jnp.max(scores, axis=-1, keepdims=True))
        probs = e / jnp.sum(e, axis=-1, keepdims=True)
        probs_b = probs.astype(BF)
        attn_v[:, cols] = jnp.dot(probs_b, v, preferred_element_type=F32).astype(BF)
        gp = lax.dot_general(g, v, NT, preferred_element_type=F32)
        gs = (probs * (gp - jnp.sum(probs * gp, axis=-1, keepdims=True))).astype(BF)
        gq_v[:, cols] = (jnp.dot(gs, k, preferred_element_type=F32) * inv_root).astype(BF)
        gk = lax.dot_general(gs, q, TN, preferred_element_type=F32) * inv_root
        gv = lax.dot_general(probs_b, g, TN, preferred_element_type=F32)
        gkv_v[h, :, :HD] = gk.astype(BF)
        gkv_v[h, :, HD:] = gv.astype(BF)

    @pl.loop(0, 2)
    def _(i):
        attend(zl * 2 + i)

    s.landed(kv_over)
    kv_far = s.send(kvr_v.at[theirs], kvr_v.at[theirs], pair)
    attend(theirs)
    s.landed(kv_far)
    attend((1 - zl) * 2 + 1 - c)

    right, left = xp[0][0], xp[2][0]

    def part(who, half):
        return gqa_v.at[pl.ds(half * 256, 256), span(who, 512)]

    def own_part(half):
        return gq_v.at[pl.ds(half * 256, 256)]

    to_right = [s.send(own_part(h), part(x, h), right) for h in (0, 1)]
    to_left = [s.send(own_part(h), part(x, h), left) for h in (1, 0)]
    gq_in = [s.send(gq_v, gqa_v.at[:, span(x, 512)], None), to_right[1], to_left[1]]
    gkv_in = [
        s.send(gkv_v.at[q], gkvr_v.at[mine], to) for to, q in quad_peers(*place)
    ]
    gkvr_v[mine] = gkv_v[mine]
    for copy in gkv_in:
        s.landed(copy)
    s.landed(to_right[0])
    gq_in.append(s.send(part((x + 3) % 4, 0), part((x + 3) % 4, 0), right))
    s.landed(to_left[0])
    gq_in.append(s.send(part((x + 1) % 4, 1), part((x + 1) % 4, 1), left))
    im0 = gkvr_v[0].astype(F32) + gkvr_v[1].astype(F32)
    im1 = gkvr_v[2].astype(F32) + gkvr_v[3].astype(F32)
    p0, p1 = one
    gkvs_v[:LCAP, :] = (im0 * p0 + im1 * p1).astype(BF)
    gkvs_v[LCAP:, :] = (im0 * (1.0 - p0) + im1 * (1.0 - p1)).astype(BF)

    def kv_block(j):
        cols = span(j, 512)
        rows = cap_v[:, :, :, cols].reshape(512, 512)
        kvp_v[j] = lax.dot_general(rows, gkvs_v[...], TN, preferred_element_type=F32).astype(BF)

    yp, zp = y_peers(*place), z_peers(*place)
    zpair = device(y, 1 - zh, zl, x, c)
    here_dp = y * 2 + zh
    first, second = pl.ds(0, 256), pl.ds(256, 256)
    ka_in, kb_in = [], []
    for k in (1, 3, 2, 0):
        v = (y + k) % 4
        kv_block(v * 2 + 1 - zh)
        ka_in.append(s.send(kvp_v.at[v * 2 + 1 - zh, first], ka_v.at[v], zpair))
        kv_block(v * 2 + zh)
        if k:
            both = kvp_v.at[pl.ds(v * 2, 2), second]
            kb_in.append(s.send(both, kb_v.at[k - 1], yp[k - 1][0]))
    for to, v in xp + [(None, x)]:
        for half in (0, 1):
            s.send(
                attn_v.at[span(v, 128), pl.ds(half * 256, 256)],
                attn_out.at[:, span(half * 4 + x, 256)],
                to,
            )

    for copy in ka_in + kb_in:
        s.landed(copy)
    k2a_in = []
    for k in (1, 3, 2, 0):
        v = (y + k) % 4
        total = kvp_v[v * 2 + zh, first, :].astype(F32) + ka_v[v].astype(F32)
        kvp_v[v * 2 + zh, first, :] = total.astype(BF)
        if k:
            k2a_in.append(s.send(kvp_v.at[v * 2 + zh, first], k2a_v.at[k - 1], yp[k - 1][0]))
    for w in (1 - zh, zh):
        total = kvp_v[y * 2 + w, second, :].astype(F32)
        for k in range(3):
            total = total + kb_v[k, w].astype(F32)
        kvp_v[y * 2 + w, second, :] = total.astype(BF)
    k2b_in = s.send(kvp_v.at[y * 2 + 1 - zh, second], k2b_v, zpair)

    for copy in gq_in:
        s.landed(copy)

    def q_grad(which, at):
        @pl.loop(0, 8)
        def _(i):
            f = i // 4
            cols = pl.ds(pl.multiple_of((i % 4) * 512, 512), 512)
            to_cols = pl.ds(pl.multiple_of(at + (i % 4) * 512, 512), 512)
            from_rows = pl.ds(pl.multiple_of(f * 512 + which * 256, 256), 256)
            part = lax.dot_general(
                xs_v[:, from_rows], gqa_v[:, cols], TN, preferred_element_type=F32
            ).astype(BF)
            ch_v[f * 2, :, to_cols] = part[:128]
            ch_v[f * 2 + 1, :, to_cols] = part[128:]

    q_grad(1 - c, 0)
    qg_pair = s.send(ch_v.at[:, :, pl.ds(0, 2048)], grc_v, pair)
    q_grad(c, 2048)

    s.landed(qg_pair)

    @pl.loop(0, 32)
    def _(i):
        rows = pl.ds(pl.multiple_of((i % 8) * 16, 16), 16)
        keep = ch_v[i // 8, rows, 2048:].astype(F32) + grc_v[i // 8, rows, :].astype(F32)
        ch_v[i // 8, rows, 2048:] = keep.astype(BF)

    r1_in = [
        s.send(ch_v.at[:, span(v, 32), pl.ds(2048, 1024)], r1_v.at[k], to)
        for k, (to, v) in enumerate(yp)
    ]
    r2_in = [
        s.send(ch_v.at[(t % 2) * 2 + t // 2, :, pl.ds(3072, 1024)], r2_v.at[k], to)
        for k, (to, t) in enumerate(zp)
    ]

    for copy in k2a_in + [k2b_in]:
        s.landed(copy)
    total = kvp_v[here_dp, first, :].astype(F32)
    for k in range(3):
        total = total + k2a_v[k].astype(F32)
    kvp_v[here_dp, first, :] = total.astype(BF)
    total = kvp_v[here_dp, second, :].astype(F32) + k2b_v[...].astype(F32)
    kvp_v[here_dp, second, :] = total.astype(BF)

    def kv_at(v, w):
        return gkv_out.at[v * 2 + w]

    def q_at(v, w):
        return gq_out.at[w * 4 + v]

    def spread(own, out, rows):
        s.send(own, out(y, zh), None)
        over = s.send(own.at[pl.ds(0, rows)], out(y, zh).at[pl.ds(0, rows)], zpair)
        along = [(k, s.send(own, out(y, zh), yp[k - 1][0])) for k in (1, 3, 2)]
        s.send(own.at[pl.ds(rows, rows)], out(y, zh).at[pl.ds(rows, rows)], zpair)
        return over, along

    def pass_first(over, out, rows):
        s.landed(over)
        for k in (1, 3, 2):
            pass_on(out(y, 1 - zh).at[pl.ds(0, rows)], yp[k - 1][0])

    def pass_second(along, out, rows):
        for k, copy in along:
            s.landed(copy)
            pass_on(out((y + 4 - k) % 4, zh).at[pl.ds(rows, rows)], zpair)

    dp_over, kv_along = spread(kvp_v.at[here_dp], kv_at, 256)
    @pl.loop(0, 4)
    def _(i):
        rows = pl.ds(pl.multiple_of(i * 256, 256), 256)
        part = lax.dot_general(
            gqa_v[...], wx_v[rows, :], NT, preferred_element_type=F32
        ).astype(BF)
        for v in range(4):
            lat_v[:, pl.ds(pl.multiple_of(v * 1024 + i * 256, 256), 256)] = part[
                v * 128 : (v + 1) * 128
            ]

    for to, v in xp + [(None, x)]:
        for half in (0, 1):
            s.send(
                lat_v.at[:, span(v * 2 + half, 512)],
                dxn_out.at[:, span(half * 4 + x, 512)],
                to,
            )
    for copy in r1_in + r2_in:
        s.landed(copy)
    for i in range(4):
        total = ch_v[i, span(y, 32), 2048:3072].astype(F32)
        for k in range(3):
            total = total + r1_v[k, i].astype(F32)
        s1_v[i] = total.astype(BF)
    at = zl * 2 + zh
    for i in range(4):
        rows = pl.ds(i * 32, 32)
        total = ch_v[at, rows, 3072:].astype(F32)
        for k in range(3):
            total = total + r2_v[k, rows, :].astype(F32)
        s2_v[i] = total.astype(BF)
    t_in = [
        s.send(s1_v.at[(t % 2) * 2 + t // 2], t1_v.at[k], to) for k, (to, t) in enumerate(zp)
    ]
    t_in += [s.send(s2_v.at[v], t2_v.at[k], to) for k, (to, v) in enumerate(yp)]
    pass_first(dp_over, kv_at, 256)
    for copy in t_in:
        s.landed(copy)
    left, right = s1_v[at].astype(F32), s2_v[y].astype(F32)
    for k in range(3):
        left = left + t1_v[k].astype(F32)
        right = right + t2_v[k].astype(F32)
    fin_v[:, :1024] = left.astype(BF)
    fin_v[:, 1024:] = right.astype(BF)
    q_over, q_along = spread(fin_v, q_at, 16)
    pass_second(kv_along, kv_at, 256)
    pass_first(q_over, q_at, 16)
    pass_second(q_along, q_at, 16)
    s.finish()


GROUPS = (x_peers, quad_peers, y_peers, z_peers)
COPIES = 180


def main(*ins):
    anys, vmem = pl.BlockSpec(memory_space=pl.ANY), pl.BlockSpec(memory_space=pltpu.VMEM)
    shapes = [(128, 2048), (128, 4096), (8, 32, 2048), (8, 512, 256)]
    scratch = [
        (128, 4096), (128, 4096), (256, 2048), (4, 128, 4096), (32, 4096), (4096, 768), (384, 4096),
        (4096, 256), (1024, 2048), (512, 1024), (512, 512), None, (512, 384),
        (256, 4096), (256, 4096), (256, 4096), (4, 32, 4096), (3, 32, 4096), (3, 512, 512), (2, 256, 512), (3, 512, 512),
        (512, 512), (2, 8, 32, 4096), (2, LCAP, 256), (2, LCAP, 256), (4, LCAP, 256),
        (512, 512), (512, 512), (4, LCAP, 256), (4, LCAP, 256), (512, 256), (8, 512, 256),
        (512, 2048), (4, 128, 2048), (3, 4, 32, 1024), (3, 128, 1024), (4, 32, 1024), (4, 32, 1024),
        (3, 32, 1024), (3, 32, 1024), (32, 2048), (4, 256, 256), (3, 2, 256, 256),
        (3, 256, 256), (256, 256),
    ]
    return pl.pallas_call(
        kernel,
        out_shape=[jax.ShapeDtypeStruct(shape, BF) for shape in shapes],
        in_specs=[anys] * 9 + [vmem] * 2 + [pl.BlockSpec(memory_space=pltpu.SMEM)] * 2,
        out_specs=[anys] * 4,
        scratch_shapes=[
            pltpu.VMEM((512, 768), F32) if shape is None else pltpu.VMEM(shape, BF)
            for shape in scratch
        ]
        + [pltpu.SemaphoreType.DMA((COPIES,))] * 2,
        compiler_params=pltpu.CompilerParams(
            collective_id=0, has_side_effects=True, vmem_limit_bytes=63 * 2**20
        ),
        name="main",
    )(*ins)


def last_kernel(
    attn, dxn, lat, gq, gkv, attn_o, lat_o, gq_o, gk_o, gv_o,
    attn_v, dxn_v, lat_v, gq_v, gkv_v, attn_f, lat_f, gq_f, gk_f, gv_f, sems,
):
    copies = []

    def move(src, dst):
        copy = pltpu.make_async_copy(src, dst, sems.at[len(copies)])
        copy.start()
        copies.append(copy)
        return copy

    def part(i, size):
        return pl.ds(i * size, size)

    outs = []
    kv_in = [move(gkv.at[part(i, 2)], gkv_v.at[part(i, 2)]) for i in range(4)]
    lat_in = []
    for i in range(4):
        rows = part(i, 32)
        lat_in.append(
            (move(lat.at[rows], lat_v.at[rows]), move(dxn.at[rows], dxn_v.at[rows]))
        )
    gq_in = [move(gq.at[part(i, 4)], gq_v.at[part(i, 4)]) for i in (0, 1)]
    attn_in = move(attn, attn_v)
    for i in range(4):
        kv_in[i].wait()

        @pl.loop(0, 8)
        def _(n, i=i):
            at, rows = i * 2 + n // 4, pl.ds(pl.multiple_of((n % 4) * 128, 128), 128)
            to = pl.ds(pl.multiple_of(i * 1024 + n * 128, 128), 128)
            gk_f[to, :] = gkv_v[at, rows, :HD].astype(F32)
            gv_f[to, :] = gkv_v[at, rows, HD:].astype(F32)

        rows = part(i, 1024)
        outs += [move(gk_f.at[rows], gk_o.at[rows]), move(gv_f.at[rows], gv_o.at[rows])]
    for i in range(4):
        for copy in lat_in[i]:
            copy.wait()

        @pl.loop(0, 2)
        def _(n, i=i):
            rows = pl.ds(pl.multiple_of(i * 32 + n * 16, 16), 16)
            v = lat_v[rows, :].astype(F32)
            r = v - jnp.mean(v, axis=-1, keepdims=True)
            rstd = lax.rsqrt(jnp.mean(r * r, axis=-1, keepdims=True) + 1e-06)
            xhat = r * rstd
            g = dxn_v[rows, :].astype(F32)
            lat_f[rows, :] = rstd * (
                g
                - jnp.mean(g, axis=-1, keepdims=True)
                - xhat * jnp.mean(g * xhat, axis=-1, keepdims=True)
            )

        rows = part(i, 32)
        outs.append(move(lat_f.at[rows], lat_o.at[rows]))
    for i in (0, 1):
        gq_in[i].wait()

        @pl.loop(0, 4)
        def _(n, i=i):
            rows = pl.ds(pl.multiple_of((i * 4 + n) * 32, 32), 32)
            for w in range(4):
                for h in (0, 1):
                    there, here = h * 1024 + w * 256, w * 512 + h * 256
                    gq_f[rows, there : there + 256] = gq_v[i * 4 + n, :, here : here + 256].astype(
                        F32
                    )

        rows = part(i, 128)
        outs.append(move(gq_f.at[rows], gq_o.at[rows]))
    attn_in.wait()

    @pl.loop(0, 4)
    def _(n):
        rows = pl.ds(pl.multiple_of(n * 32, 32), 32)
        attn_f[rows, :] = attn_v[rows, :].astype(F32)

    outs.append(move(attn_f, attn_o))
    for copy in outs:
        copy.wait()


def last(*ins):
    anys = pl.BlockSpec(memory_space=pl.ANY)
    shapes = [(128, 2048), (128, 4096), (256, 2048), (4096, HD), (4096, HD)]
    return pl.pallas_call(
        last_kernel,
        out_shape=[jax.ShapeDtypeStruct(shape, F32) for shape in shapes],
        in_specs=[anys] * 5,
        out_specs=[anys] * 5,
        scratch_shapes=[pltpu.VMEM(a.shape, BF) for a in ins]
        + [pltpu.VMEM(shape, F32) for shape in shapes]
        + [pltpu.SemaphoreType.DMA((40,))],
        compiler_params=pltpu.CompilerParams(vmem_limit_bytes=63 * 2**20),
        name="last",
    )(*ins)


def local(
    cap_hidden,
    t5_norm_gain,
    t5_wi0,
    t5_wi1,
    t5_wo,
    t5_final_gain,
    cap_lengths,
    latents,
    w_query,
    w_key,
    w_value,
    caption_of_image,
    grad_out,
):
    attn, dxn, gq, gkv = main(
        latents,
        grad_out,
        w_query,
        cap_hidden,
        t5_wi0,
        t5_wi1,
        t5_wo,
        w_key,
        w_value,
        t5_norm_gain,
        t5_final_gain,
        cap_lengths,
        caption_of_image,
    )
    return last(attn, dxn, latents, gq, gkv)


def solution(mesh):
    placed = (
        P("dp", None),
        P(),
        P(None, "fsdp"),
        P(None, "fsdp"),
        P("fsdp", None),
        P(),
        P("dp"),
        P(("dp", "fsdp"), None),
        P("fsdp", None),
        P(None, "fsdp"),
        P(None, "fsdp"),
        P("dp"),
        P(("dp", "fsdp"), None),
    )
    return jax.shard_map(
        local,
        mesh=mesh,
        in_specs=placed,
        out_specs=(
            P(("dp", "fsdp"), None),
            P(("dp", "fsdp"), None),
            P("fsdp", None),
            P(None, "fsdp"),
            P(None, "fsdp"),
        ),
        check_vma=False,
    )
```
